128 devices in a mesh: dp: 32 (over x, y, core), rep: 4 (over z).
Axes of the slice: x: 4, y: 4, z: 4, core: 2. Of those that a mesh axis runs over, the one named last changes fastest.
Arguments:
- clip_tiles: bfloat16 [16384, 256, 128], P(('dp', 'rep')), may hold values from -16 to 16
- clip_size: int32 [128, 64], P(('dp', 'rep')), may hold values from 0 to 8, as said below
- clip_dest: int32 [128, 64], P(('dp', 'rep')), may hold values from 0 to 31, as said below
- timesteps: int32 [128, 64], P(('dp', 'rep')), may hold values from 0 to 999
- noise_seeds: int32 [128, 64], P(('dp', 'rep')), may hold values from 0 to 1048575
- w_time: bfloat16 [256, 256], replicated, may hold values from -0.375 to 0.375
- gain: float32 [128], replicated, may hold values from 0.1 to 1.9
- w_in: bfloat16 [128, 256], replicated, may hold values from -0.5 to 0.5
- w_out: bfloat16 [256, 128], replicated, may hold values from -0.375 to 0.375
- w_down: bfloat16 [512, 256], replicated, may hold values from -0.25 to 0.25
- w_up: bfloat16 [256, 512], replicated, may hold values from -0.375 to 0.375
Outputs:
- grad_time: float32 [256, 256], replicated
- grad_gain: float32 [128], replicated
- grad_in: float32 [128, 256], replicated
- grad_out: float32 [256, 128], replicated
- grad_down: float32 [512, 256], replicated
- grad_up: float32 [256, 512], replicated
- device_loss: float32 [128], P(('dp', 'rep'))
The draws below stay inside these ranges and needn't reach their ends.
Inputs may be any that keep to these rules, and one draw needn't show every extreme that they name: `clip_size`: each loader's entries come in runs of four (entries 4j to 4j+3) that together hold exactly 8 tiles or none, the holding runs first; sizes are 0, 1, 2, 4 or 8. In every replica group the loaders hold 256 such runs in all, one loader holds 16 and one none. `clip_dest`: all entries of one run of four share one destination. Within a replica group every compute device receives exactly 64 tiles, and one loader sends at most 8 tiles to one compute device, some loader exactly 8.
All inputs are finite; a program needn't handle non-finite values.
Results may differ from the reference program's by a relative error of at most 0.00034.
Values may be sent and summed in bfloat16 or wider, within the bound.
A program may use at most 128 MiB of HBM per device.

```python
import math
import jax
import jax.numpy as jnp
from jax import lax

C = 128
C2 = 256
HID = 256
EMB = 256
GN_GROUPS = 32
TR = 8
TC = 32
TSTEPS = 1000
TILES_DEV = 128
PIX = 256
SPANS = 16
CLIPS_DEV = 64
LOADERS = 128
TILES = 16384
N_DP = 32
N_REP = 4


def layout(key):
    base_key = jax.random.fold_in(key, 11)
    key_pair, key_order, key_shape = jax.random.split(base_key, 3)
    half_count = N_DP // 2
    leading = jax.random.randint(key_pair, (N_REP, half_count), 1, SPANS)
    leading = leading.at[:, 0].set(SPANS)
    paired = jnp.concatenate([leading, SPANS - leading], axis=1)
    order_keys = jax.random.split(key_order, N_REP)
    orders = jax.vmap(lambda single: jax.random.permutation(single, N_DP))(order_keys)
    live_spans = jnp.take_along_axis(paired, orders, axis=1).T
    earlier = jnp.cumsum(live_spans, axis=0, dtype=jnp.int32) - live_spans
    first_live = jnp.argmax((live_spans > 0).astype(jnp.int32), axis=0).astype(jnp.int32)
    group_index = jnp.arange(N_REP, dtype=jnp.int32)
    shift_by = jnp.where(group_index % 2 == 0, 1, N_DP // 2).astype(jnp.int32)
    offset = (first_live + shift_by) % N_DP
    span_index = jnp.arange(SPANS, dtype=jnp.int32)
    global_rank = earlier[:, :, None] + span_index[None, None, :]
    target = (global_rank + offset[None, :, None]) % N_DP
    active = (span_index[None, None, :] < live_spans[:, :, None]).astype(jnp.int32)
    patterns = jnp.array([[8, 0, 0, 0], [4, 4, 0, 0], [4, 2, 2, 0], [2, 2, 2, 2], [4, 2, 1, 1], [2, 4, 2, 0], [1, 1, 2, 4], [2, 2, 4, 0]], jnp.int32)
    picked = jax.random.randint(key_shape, (N_DP, N_REP, SPANS), 0, 8)
    sizes_all = patterns[picked] * active[..., None]
    targets = jnp.broadcast_to(target[..., None], sizes_all.shape)
    return (sizes_all.reshape(LOADERS, CLIPS_DEV), targets.reshape(LOADERS, CLIPS_DEV))


def draw_clip_size(key, part):
    return layout(key)[0]


def draw_clip_dest(key, part):
    return layout(key)[1]


def draw_clip_tiles(key, part):
    key_base, key_tile, key_chan = jax.random.split(jax.random.fold_in(key, 23), 3)
    tile_scale = jnp.exp(jax.random.uniform(key_tile, (TILES, 1, 1), jnp.float32, -1.15, 1.15))
    chan_scale = jnp.exp(jax.random.uniform(key_chan, (1, 1, C), jnp.float32, -1.15, 1.15))
    base_values = jax.random.normal(key_base, (TILES, PIX, C), jnp.float32)
    return jnp.clip(base_values * tile_scale * chan_scale, -16.0, 16.0).astype(jnp.bfloat16)


def place_ends(entries, own_key, low, high):
    spot = [jax.random.randint(jax.random.fold_in(own_key, axis), (), 0, length) for axis, length in enumerate(entries.shape)]
    longest = entries.shape.index(max(entries.shape))
    next_to = spot[:longest] + [(spot[longest] + 1) % entries.shape[longest]] + spot[longest + 1:]
    return entries.at[tuple(spot)].set(low).at[tuple(next_to)].set(high)


def centred(rng, dims, scale, most, kind=jnp.bfloat16):
    return jnp.clip(scale * jax.random.normal(rng, dims, jnp.float32), -most, most).astype(kind)


def setup_inputs(seed: int = 0) -> dict:
    key_of = jax.random.split(jax.random.key(seed), 12)
    return {
        "clip_tiles": draw_clip_tiles(jax.random.fold_in(key_of[11], 71), 0),
        "clip_size": draw_clip_size(jax.random.fold_in(key_of[11], 71), 0),
        "clip_dest": draw_clip_dest(jax.random.fold_in(key_of[11], 71), 0),
        "timesteps": place_ends(jax.random.randint(key_of[3], (LOADERS, CLIPS_DEV), 0, TSTEPS), jax.random.fold_in(key_of[3], 1), 0, TSTEPS - 1).astype(jnp.int32),
        "noise_seeds": place_ends(jax.random.randint(key_of[4], (LOADERS, CLIPS_DEV), 0, 1048576), jax.random.fold_in(key_of[4], 1), 0, 1048575).astype(jnp.int32),
        "w_time": centred(key_of[5], (EMB, 2 * C), EMB ** -0.5, 0.375),
        "gain": jnp.clip(1.0 + 0.18 * jax.random.normal(key_of[6], (C,), jnp.float32), 0.1, 1.9),
        "w_in": centred(key_of[7], (C, HID), C ** -0.5, 0.5),
        "w_out": centred(key_of[8], (HID, C), HID ** -0.5, 0.375),
        "w_down": centred(key_of[9], (4 * C, C2), (4 * C) ** -0.5, 0.25),
        "w_up": centred(key_of[10], (C2, 4 * C), C2 ** -0.5, 0.375),
    }


def hashed_noise(seed_grid, position):
    mixed = position * 1103515245 + seed_grid * 747796405 + 1013904223
    mixed = mixed ^ mixed >> 16 & 65535
    mixed = mixed * 73244475
    mixed = mixed ^ mixed >> 16 & 65535
    mixed = mixed * 73244475
    mixed = mixed ^ mixed >> 16 & 65535
    uniform_bits = mixed >> 8 & 16777215
    unit_value = (uniform_bits.astype(jnp.float32) + 0.5) * (1.0 / 16777216.0)
    return 1.7320508 * (2.0 * unit_value - 1.0)

def silu_slope(value):
    sigma = jax.nn.sigmoid(value)
    return sigma * (1.0 + value * (1.0 - sigma))

def to_patches(field):
    tile_count, pixel_count, channels = field.shape
    grid = field.reshape(tile_count, TR // 2, 2, TC // 2, 2, channels)
    return grid.transpose(0, 1, 3, 2, 4, 5).reshape(tile_count, pixel_count // 4, 4 * channels)

def from_patches(patch_field):
    tile_count, quarter, wide_count = patch_field.shape
    channels = wide_count // 4
    grid = patch_field.reshape(tile_count, TR // 2, TC // 2, 2, 2, channels)
    return grid.transpose(0, 1, 3, 2, 4, 5).reshape(tile_count, quarter * 4, channels)

def tile_meta(sizes_row, dest_row, time_row, seed_row, tile_count):
    clip_count = sizes_row.shape[0]
    ends = jnp.cumsum(sizes_row, dtype=jnp.int32)
    starts = ends - sizes_row
    tile_index = jnp.arange(tile_count, dtype=jnp.int32)
    owner = lax.optimization_barrier(jnp.sum((ends[None, :] <= tile_index[:, None]).astype(jnp.int32), axis=1, dtype=jnp.int32))
    onehot = (owner[:, None] == jnp.arange(clip_count, dtype=jnp.int32)[None, :]).astype(jnp.int32)

    def lookup(values):
        return lax.optimization_barrier(jnp.sum(onehot * values[None, :], axis=1, dtype=jnp.int32))
    usable = (owner < clip_count).astype(jnp.int32)
    within = (tile_index - lookup(starts)) * usable
    tile_info = jnp.stack([usable, within, lookup(sizes_row), lookup(time_row), lookup(seed_row)], axis=1)
    return (tile_info, lookup(dest_row))

def process(tile_data, tile_info, w_time, gain, w_in, w_out, w_down, w_up, loaders):
    highest = lax.Precision.HIGHEST
    row_count, pixel_count, channels = tile_data.shape
    usable = tile_info[:, 0] > 0
    within = tile_info[:, 1]
    clip_len = jnp.where(usable, tile_info[:, 2], 1)
    step_float = tile_info[:, 3].astype(jnp.float32)
    seed_grid = tile_info[:, 4][:, None, None]
    position = (within[:, None, None] * pixel_count + jnp.arange(pixel_count, dtype=jnp.int32)[None, :, None]) * channels + jnp.arange(channels, dtype=jnp.int32)[None, None, :]
    noise_field = hashed_noise(seed_grid, position)
    alpha_bar = jnp.cos(((step_float + 1.0) / TSTEPS + 0.008) / 1.008 * (math.pi / 2.0)) ** 2
    noisy = jnp.sqrt(alpha_bar)[:, None, None] * tile_data.astype(jnp.float32) + jnp.sqrt(1.0 - alpha_bar)[:, None, None] * noise_field
    group_width = channels // GN_GROUPS
    grouped = noisy.reshape(row_count, pixel_count, GN_GROUPS, group_width)
    first_sum = lax.optimization_barrier(jnp.sum(grouped, axis=(1, 3)))
    square_sum = lax.optimization_barrier(jnp.sum(grouped * grouped, axis=(1, 3)))
    opening = (usable & (within == 0)).astype(jnp.int32)
    segment = jnp.cumsum(opening, dtype=jnp.int32) - 1
    member = ((segment[:, None] == jnp.arange(row_count, dtype=jnp.int32)[None, :]) & usable[:, None]).astype(jnp.float32)
    clip_first = jnp.dot(member.T, first_sum, precision=highest)
    clip_square = jnp.dot(member.T, square_sum, precision=highest)
    tile_first = jnp.dot(member, clip_first, precision=highest)
    tile_square = jnp.dot(member, clip_square, precision=highest)
    denominator = (clip_len * (pixel_count * group_width)).astype(jnp.float32)[:, None]
    group_mean = tile_first / denominator
    variance = tile_square / denominator - group_mean * group_mean
    inv_spread = lax.rsqrt(variance + 1e-05)
    loss_weight = jnp.where(usable, 2.0 / (clip_len.astype(jnp.float32) * pixel_count * loaders), 0.0)
    mean_weight = jnp.where(usable, 1.0 / (clip_len.astype(jnp.float32) * (pixel_count * channels)), 0.0)
    usable_count = usable.astype(jnp.int32)
    half_width = EMB // 2
    frequency = jnp.exp(-math.log(10000.0) * jnp.arange(half_width, dtype=jnp.float32) / half_width)
    angle = step_float[:, None] * frequency[None, :]
    embedding = jnp.concatenate([jnp.cos(angle), jnp.sin(angle)], axis=1).astype(jnp.bfloat16)
    modulation = jnp.dot(embedding, w_time, preferred_element_type=jnp.float32)
    block_tiles = math.gcd(row_count, 16)

    def block_work(start, totals):

        def take_block(values):
            return lax.dynamic_slice_in_dim(values, start, block_tiles, 0)
        noisy_block = take_block(noisy)
        noise_block = take_block(noise_field)
        mean_block = take_block(group_mean)
        spread_block = take_block(inv_spread)
        weight_block = take_block(loss_weight)
        mean_weight_block = take_block(mean_weight)
        embed_block = take_block(embedding)
        modul_block = take_block(modulation)
        group_view = noisy_block.reshape(block_tiles, pixel_count, GN_GROUPS, group_width)
        normed = ((group_view - mean_block[:, None, :, None]) * spread_block[:, None, :, None]).reshape(block_tiles, pixel_count, channels)
        film_scale = modul_block[:, None, :channels]
        film_shift = modul_block[:, None, channels:]
        normal_in = (normed * gain * (1.0 + film_scale) + film_shift).astype(jnp.bfloat16)
        pre_hidden = jnp.einsum('rpc,ch->rph', normal_in, w_in, preferred_element_type=jnp.float32)
        hidden = jax.nn.silu(pre_hidden).astype(jnp.bfloat16)
        residual_out = noisy_block + jnp.einsum('rph,hc->rpc', hidden, w_out, preferred_element_type=jnp.float32)
        patches = to_patches(residual_out.astype(jnp.bfloat16))
        pre_down = jnp.einsum('rqk,kd->rqd', patches, w_down, preferred_element_type=jnp.float32)
        down_act = jax.nn.silu(pre_down).astype(jnp.bfloat16)
        lifted = jnp.einsum('rqd,dk->rqk', down_act, w_up, preferred_element_type=jnp.float32)
        prediction = residual_out + from_patches(lifted)
        error = prediction - noise_block
        tile_loss = lax.optimization_barrier(jnp.sum(error * error, axis=(1, 2))) * mean_weight_block
        grad_pred = error * weight_block[:, None, None]
        grad_lifted = to_patches(grad_pred).astype(jnp.bfloat16)
        add_up = jnp.einsum('rqd,rqk->dk', down_act, grad_lifted, preferred_element_type=jnp.float32)
        grad_pre_down = (jnp.einsum('rqk,dk->rqd', grad_lifted, w_up, preferred_element_type=jnp.float32) * silu_slope(pre_down)).astype(jnp.bfloat16)
        add_down = jnp.einsum('rqk,rqd->kd', patches, grad_pre_down, preferred_element_type=jnp.float32)
        back_patch = jnp.einsum('rqd,kd->rqk', grad_pre_down, w_down, preferred_element_type=jnp.float32)
        grad_residual = (grad_pred + from_patches(back_patch)).astype(jnp.bfloat16)
        add_out = jnp.einsum('rph,rpc->hc', hidden, grad_residual, preferred_element_type=jnp.float32)
        grad_pre_hidden = (jnp.einsum('rpc,hc->rph', grad_residual, w_out, preferred_element_type=jnp.float32) * silu_slope(pre_hidden)).astype(jnp.bfloat16)
        add_in = jnp.einsum('rpc,rph->ch', normal_in, grad_pre_hidden, preferred_element_type=jnp.float32)
        grad_normal = jnp.einsum('rph,ch->rpc', grad_pre_hidden, w_in, preferred_element_type=jnp.float32)
        add_gain = lax.optimization_barrier(jnp.sum(grad_normal * normed * (1.0 + film_scale), axis=(0, 1)))
        grad_scale = lax.optimization_barrier(jnp.sum(grad_normal * normed * gain, axis=1))
        grad_shift = lax.optimization_barrier(jnp.sum(grad_normal, axis=1))
        grad_modul = jnp.concatenate([grad_scale, grad_shift], axis=1)
        add_time = jnp.einsum('re,rf->ef', embed_block.astype(jnp.float32), grad_modul, precision=highest)
        losses = lax.dynamic_update_slice_in_dim(totals[6], tile_loss, start, 0)
        return (totals[0] + add_time, totals[1] + add_gain, totals[2] + add_in, totals[3] + add_out, totals[4] + add_down, totals[5] + add_up, losses)

    def one_block(block_index, totals):
        start = block_index * block_tiles
        live = jnp.sum(lax.dynamic_slice_in_dim(usable_count, start, block_tiles, 0)) > 0
        return lax.cond(live, lambda held: block_work(start, held), lambda held: held, totals)
    zeros = (jnp.zeros(w_time.shape, jnp.float32), jnp.zeros(gain.shape, jnp.float32), jnp.zeros(w_in.shape, jnp.float32), jnp.zeros(w_out.shape, jnp.float32), jnp.zeros(w_down.shape, jnp.float32), jnp.zeros(w_up.shape, jnp.float32), jnp.zeros((row_count,), jnp.float32))
    return lax.fori_loop(0, row_count // block_tiles, one_block, zeros)

def reference(clip_tiles, clip_size, clip_dest, timesteps, noise_seeds, w_time, gain, w_in, w_out, w_down, w_up):
    loader_tiles = clip_tiles.reshape(LOADERS, TILES_DEV, PIX, C)
    loader_ids = jnp.arange(LOADERS, dtype=jnp.int32)

    def one_loader(carry, block):
        totals, device_loss = carry
        tile_data, sizes_row, dest_row, time_row, seed_row, loader_id = block
        tile_info, dest_tile = tile_meta(sizes_row, dest_row, time_row, seed_row, TILES_DEV)
        added = process(tile_data, tile_info, w_time, gain, w_in, w_out, w_down, w_up, LOADERS)
        slot = dest_tile * N_REP + loader_id % N_REP
        onehot = (slot[:, None] == jnp.arange(LOADERS, dtype=jnp.int32)[None, :]).astype(jnp.float32)
        device_loss = device_loss + lax.optimization_barrier(jnp.sum(onehot * added[6][:, None], axis=0))
        return ((tuple((left + right for left, right in zip(totals, added[:6]))), device_loss), None)
    zeros = (jnp.zeros(w_time.shape, jnp.float32), jnp.zeros(gain.shape, jnp.float32), jnp.zeros(w_in.shape, jnp.float32), jnp.zeros(w_out.shape, jnp.float32), jnp.zeros(w_down.shape, jnp.float32), jnp.zeros(w_up.shape, jnp.float32))
    carry, unused = lax.scan(one_loader, (zeros, jnp.zeros((LOADERS,), jnp.float32)), (loader_tiles, clip_size, clip_dest, timesteps, noise_seeds, loader_ids))
    totals, device_loss = carry
    return (totals[0], totals[1], totals[2], totals[3], totals[4], totals[5], device_loss)
```

```python
import math

import jax
import jax.numpy as jnp
import numpy as np
from jax import lax
from jax.experimental import pallas as pl
from jax.experimental.pallas import tpu as pltpu
from jax.sharding import PartitionSpec as P

EMB = 256
TR = 8
TC = 32
TSTEPS = 1000
C = 128
PIX = 256
HID = 256
SPAN = 8
MUL_POS = 1103515245
MUL_SEED = 747796405
ADD_POS = 1013904223
MUL_MIX = 73244475
ROOT3 = 1.7320508
NOISE_A = float(np.float32(2.0 * ROOT3 / 16777216.0))
NOISE_B = float(np.float32(ROOT3 * (1.0 / 16777216.0 - 1.0)))
F32 = jnp.float32
BF16 = jnp.bfloat16


def wrap32(value):
    value &= 0xFFFFFFFF
    return value - (1 << 32) if value >= (1 << 31) else value


def dot(a, b):
    return lax.dot_general(a, b, (((1,), (0,)), ((), ())), preferred_element_type=F32)


def dot_bt(a, b):
    return lax.dot_general(a, b, (((1,), (1,)), ((), ())), preferred_element_type=F32)


def dot_at(a, b):
    return lax.dot_general(a, b, (((0,), (0,)), ((), ())), preferred_element_type=F32)


def shift_right(value, amount):
    return lax.shift_right_logical(value, jnp.int32(amount))


def group_sum(x, lane):
    pair = x + jnp.where(lane % 2 == 0, pltpu.roll(x, 127, 1), pltpu.roll(x, 1, 1))
    return pair + jnp.where(lane % 4 < 2, pltpu.roll(pair, 126, 1), pltpu.roll(pair, 2, 1))


def span_kernel(
    count_ref, mix_ref, sa_ref, sb_ref, weight_ref, seg_ref,
    tiles_hbm, col_ref, emb_ref, slot_ref, wt_ref, gain_ref,
    win_ref, wout_ref, wdown_ref, wup_ref,
    gt_ref, misc_ref, gin_ref, gout_ref, gdown_ref, gup_ref,
    buf, sem, itab, perm, modul, noise, noisy, x_s, hid, slope, resid, patch,
    dact, dslope, glift, gpd_s, gres, gph_s, s1_s, s2_s, loss_s, stat,
    win_h, wout_h, wdown_h, wup_h,
):
    count = count_ref[0]

    def fetch(span, slot):
        return pltpu.make_async_copy(
            tiles_hbm.at[pl.ds(span * SPAN, SPAN)], buf.at[slot], sem.at[slot]
        )

    @pl.when(count > 0)
    def _():
        fetch(0, 0).start()

    row = lax.broadcasted_iota(jnp.int32, (PIX, C), 0)
    lane = lax.broadcasted_iota(jnp.int32, (PIX, C), 1)
    quad, rest = row // 64, row % 64
    pixel = (2 * (rest // 16) + quad // 2) * TC + 2 * (rest % 16) + quad % 2
    itab[...] = (pixel * C + lane) * jnp.int32(MUL_POS)
    prow = lax.broadcasted_iota(jnp.int32, (PIX, PIX), 0)
    pcol = lax.broadcasted_iota(jnp.int32, (PIX, PIX), 1)
    pquad, prest = prow // 64, prow % 64
    ppix = (2 * (prest // 16) + pquad // 2) * TC + 2 * (prest % 16) + pquad % 2
    perm[...] = jnp.where(ppix == pcol, 1.0, 0.0).astype(BF16)
    modul[...] = dot(emb_ref[...], wt_ref[...])
    win_h[...] = win_ref[...] * jnp.asarray(0.5, BF16)
    wdown_h[...] = wdown_ref[...] * jnp.asarray(0.5, BF16)
    wout_h[...] = wout_ref[...] * jnp.asarray(0.5, BF16)
    wup_h[...] = wup_ref[...] * jnp.asarray(0.5, BF16)
    for ref in (gin_ref, gout_ref, gdown_ref, gup_ref, s1_s, s2_s, loss_s):
        ref[...] = jnp.zeros_like(ref)
    lane8 = lax.broadcasted_iota(jnp.int32, (SPAN, C), 1)

    @pl.loop(0, count)
    def _(span):
        slot = lax.rem(span, 2)
        base = span * SPAN

        @pl.when(span + 1 < count)
        def _():
            fetch(span + 1, 1 - slot).start()

        fetch(span, slot).wait()

        for k in range(SPAN):
            mixed = itab[...] + mix_ref[base + k]
            mixed = mixed ^ shift_right(mixed, 16)
            mixed = mixed * jnp.int32(MUL_MIX)
            mixed = mixed ^ shift_right(mixed, 16)
            mixed = mixed * jnp.int32(MUL_MIX)
            mixed = mixed ^ shift_right(mixed, 16)
            field = shift_right(mixed, 8).astype(F32) * NOISE_A + NOISE_B
            noise[k] = field
            pixels = dot(perm[...], buf[slot, k])
            value = sa_ref[base + k] * pixels + sb_ref[base + k] * field
            noisy[k] = value
            stat[0, pl.ds(k, 1), :] = jnp.sum(value, axis=0, keepdims=True)
            stat[1, pl.ds(k, 1), :] = jnp.sum(value * value, axis=0, keepdims=True)

        rows8 = pl.ds(pl.multiple_of(base, SPAN), SPAN)
        seg = col_ref[0, rows8, :]
        inv_count = col_ref[1, rows8, :]
        first = jnp.zeros((SPAN, C), F32)
        square = jnp.zeros((SPAN, C), F32)
        for k in range(SPAN):
            member = seg == seg_ref[base + k]
            first += jnp.where(member, stat[0, pl.ds(k, 1), :], 0.0)
            square += jnp.where(member, stat[1, pl.ds(k, 1), :], 0.0)
        mean = group_sum(first, lane8) * inv_count
        var = group_sum(square, lane8) * inv_count - mean * mean
        spread = lax.rsqrt(var + 1e-05)
        factor = spread * gain_ref[...] * (1.0 + modul[rows8, :C])
        shift = modul[rows8, C:]
        stat[0] = mean
        stat[1] = factor
        stat[2] = shift
        stat[3] = spread

        for k in range(SPAN):
            one = pl.ds(k, 1)
            centre = noisy[k] - stat[0, one, :]
            normal = (centre * stat[1, one, :] + stat[2, one, :]).astype(BF16)
            x_s[k] = normal
            half = dot(normal, win_h[...])
            th = jnp.tanh(half)
            q = 1.0 + th
            h = half * q
            slope[k] = q + h * (1.0 - th)
            hb = h.astype(BF16)
            hid[k] = hb
            out = dot(hb, wout_ref[...]) + noisy[k]
            resid[k] = out
            outb = out.astype(BF16)
            for j in range(4):
                patch[pl.ds(k * 64, 64), pl.ds(j * C, C)] = outb[j * 64:(j + 1) * 64]

        for m in range(4):
            rows = pl.ds(m * 128, 128)
            half = dot(patch[rows, :], wdown_h[...])
            th = jnp.tanh(half)
            q = 1.0 + th
            h = half * q
            dslope[rows, :] = q + h * (1.0 - th)
            hb = h.astype(BF16)
            dact[rows, :] = hb
            lifted = dot(hb, wup_ref[...])
            for t in range(2):
                k = m * 2 + t
                weight = weight_ref[base + k]
                total = jnp.zeros((64, C), F32)
                for j in range(4):
                    part = pl.ds(j * 64, 64)
                    err = (
                        resid[k, part, :]
                        + lifted[t * 64:(t + 1) * 64, j * C:(j + 1) * C]
                        - noise[k, part, :]
                    )
                    total += err * err
                    gp = err * weight
                    resid[k, part, :] = gp
                    glift[pl.ds(k * 64, 64), pl.ds(j * C, C)] = gp.astype(BF16)
                loss_s[pl.ds(base + k, 1), :] = jnp.sum(total, axis=0, keepdims=True)
            gpd = (dot_bt(glift[rows, :], wup_h[...]) * dslope[rows, :]).astype(BF16)
            gpd_s[rows, :] = gpd
            back = dot_bt(gpd, wdown_ref[...])
            for t in range(2):
                k = m * 2 + t
                for j in range(4):
                    part = pl.ds(j * 64, 64)
                    gres[k, part, :] = (
                        resid[k, part, :] + back[t * 64:(t + 1) * 64, j * C:(j + 1) * C]
                    ).astype(BF16)

        for k in range(SPAN):
            one = pl.ds(k, 1)
            gph = (dot_bt(gres[k], wout_h[...]) * slope[k]).astype(BF16)
            gph_s[k] = gph
            gn = dot_bt(gph, win_ref[...])
            centre = noisy[k] - stat[0, one, :]
            s1_s[pl.ds(base + k, 1), :] = jnp.sum(gn, axis=0, keepdims=True)
            s2_s[pl.ds(base + k, 1), :] = (
                jnp.sum(gn * centre, axis=0, keepdims=True) * stat[3, one, :]
            )

        flat = SPAN * PIX
        gup_ref[...] += dot_at(dact[...], glift[...])
        gdown_ref[...] += dot_at(gpd_s[...], patch[...])
        gout_ref[...] += dot_at(gres[...].reshape(flat, C), hid[...].reshape(flat, HID))
        gin_ref[...] += dot_at(x_s[...].reshape(flat, C), gph_s[...].reshape(flat, HID))

    scale1 = 1.0 + modul[:, :C]
    s2 = s2_s[...]
    misc_ref[...] = jnp.zeros_like(misc_ref)
    misc_ref[pl.ds(0, 1), :] = jnp.sum(s2 * scale1, axis=0, keepdims=True)
    tile_loss = jnp.sum(loss_s[...], axis=1, keepdims=True) * col_ref[2]
    hits = slot_ref[...] == lax.broadcasted_iota(jnp.int32, (C, C), 1)
    misc_ref[pl.ds(1, 1), :] = jnp.sum(jnp.where(hits, tile_loss, 0.0), axis=0, keepdims=True)
    emb = emb_ref[...].astype(F32)
    for ref, part in ((s2 * gain_ref[...], 0), (s1_s[...], 1)):
        gt_ref[:, pl.ds(part * C, C)] = lax.dot_general(
            emb, ref, (((0,), (0,)), ((), ())),
            precision=lax.Precision.HIGHEST, preferred_element_type=F32,
        )


def tile_tables(sizes, dests, times, seeds, group, tile_count):
    clip_count = sizes.shape[0]
    ends = jnp.cumsum(sizes, dtype=jnp.int32)
    tile = jnp.arange(tile_count, dtype=jnp.int32)
    owner = jnp.sum((ends[None, :] <= tile[:, None]).astype(jnp.int32), axis=1)
    onehot = (owner[:, None] == jnp.arange(clip_count, dtype=jnp.int32)[None, :]).astype(jnp.int32)
    columns = jnp.stack([ends - sizes, sizes, dests, times, seeds], axis=0)
    found = jnp.sum(onehot[None] * columns[:, None, :], axis=2)
    usable = owner < clip_count
    within = jnp.where(usable, tile - found[0], 0)
    length = jnp.where(usable, found[1], 1)
    step = found[3].astype(F32)
    alpha_bar = jnp.cos(((step + 1.0) / TSTEPS + 0.008) / 1.008 * (math.pi / 2.0)) ** 2
    mix = within * jnp.int32(wrap32(PIX * C * MUL_POS)) + found[4] * jnp.int32(MUL_SEED) + jnp.int32(ADD_POS)
    inv_len = 1.0 / length.astype(F32)
    weight = jnp.where(usable, inv_len * (2.0 / (PIX * C)), 0.0)
    half = EMB // 2
    freq = jnp.exp(-math.log(10000.0) * jnp.arange(half, dtype=F32) / half)
    angle = step[:, None] * freq[None, :]
    emb = jnp.concatenate([jnp.cos(angle), jnp.sin(angle)], axis=1).astype(BF16)
    slot = jnp.where(usable, found[2] * 4 + group, -1)
    cols = jnp.stack([owner.astype(F32), inv_len / (PIX * 4), weight * 0.5], axis=0)
    cols = jnp.broadcast_to(cols[:, :, None], (3, tile_count, C))
    slots = jnp.broadcast_to(slot[:, None], (tile_count, C))
    count = jnp.sum(sizes) // SPAN
    return (
        count.reshape(1), mix, jnp.sqrt(alpha_bar), jnp.sqrt(1.0 - alpha_bar), weight,
        owner.astype(F32), cols, emb, slots,
    )


def local_grads(clip_tiles, sizes, dests, times, seeds, group, w_time, gain, w_in, w_out, w_down, w_up):
    tile_count = clip_tiles.shape[0]
    count, mix, sa, sb, weight, seg, cols, emb, slots = tile_tables(
        sizes, dests, times, seeds, group, tile_count
    )
    smem = pl.BlockSpec(memory_space=pltpu.SMEM)
    vmem = pl.BlockSpec(memory_space=pltpu.VMEM)
    shapes = [(EMB, 2 * C), (8, C), (C, HID), (C, HID), (256, 512), (256, 512)]
    return pl.pallas_call(
        span_kernel,
        out_shape=[jax.ShapeDtypeStruct(s, F32) for s in shapes],
        in_specs=[smem] * 6 + [pl.BlockSpec(memory_space=pl.ANY)] + [vmem] * 9,
        out_specs=[vmem] * 6,
        scratch_shapes=[
            pltpu.VMEM((2, SPAN, PIX, C), BF16),
            pltpu.SemaphoreType.DMA((2,)),
            pltpu.VMEM((PIX, C), jnp.int32),
            pltpu.VMEM((PIX, PIX), BF16),
            pltpu.VMEM((tile_count, 2 * C), F32),
            pltpu.VMEM((SPAN, PIX, C), F32),
            pltpu.VMEM((SPAN, PIX, C), F32),
            pltpu.VMEM((SPAN, PIX, C), BF16),
            pltpu.VMEM((SPAN, PIX, HID), BF16),
            pltpu.VMEM((SPAN, PIX, HID), F32),
            pltpu.VMEM((SPAN, PIX, C), F32),
            pltpu.VMEM((512, 512), BF16),
            pltpu.VMEM((512, 256), BF16),
            pltpu.VMEM((512, 256), F32),
            pltpu.VMEM((512, 512), BF16),
            pltpu.VMEM((512, 256), BF16),
            pltpu.VMEM((SPAN, PIX, C), BF16),
            pltpu.VMEM((SPAN, PIX, HID), BF16),
            pltpu.VMEM((tile_count, C), F32),
            pltpu.VMEM((tile_count, C), F32),
            pltpu.VMEM((tile_count, C), F32),
            pltpu.VMEM((4, SPAN, C), F32),
            pltpu.VMEM((C, HID), BF16),
            pltpu.VMEM((HID, C), BF16),
            pltpu.VMEM((512, 256), BF16),
            pltpu.VMEM((256, 512), BF16),
        ],
        compiler_params=pltpu.CompilerParams(vmem_limit_bytes=56 * 1024 * 1024),
    )(count, mix, sa, sb, weight, seg, clip_tiles, cols, emb, slots, w_time,
      gain.reshape(1, C), w_in, w_out, w_down, w_up)


def body(clip_tiles, clip_size, clip_dest, timesteps, noise_seeds, w_time, gain, w_in, w_out, w_down, w_up):
    group = lax.axis_index("rep")
    me = lax.axis_index("dp") * lax.axis_size("rep") + group
    parts = local_grads(
        clip_tiles, clip_size[0], clip_dest[0], timesteps[0], noise_seeds[0], group,
        w_time, gain, w_in, w_out, w_down, w_up,
    )
    gt, misc, gin, gout, gdown, gup = lax.psum(tuple(parts), ("dp", "rep"))
    own_loss = lax.dynamic_slice_in_dim(misc[1], me, 1)
    return (gt, misc[0], gin, gout.T, gdown.T, gup, own_loss)


def solution(mesh):
    rows = P(("dp", "rep"), None)
    in_specs = (P(("dp", "rep"), None, None), rows, rows, rows, rows) + (P(),) * 6
    out_specs = (P(),) * 6 + (P(("dp", "rep")),)
    return jax.shard_map(body, mesh=mesh, in_specs=in_specs, out_specs=out_specs, check_vma=False)
```

```python
import functools
import math

import jax
import jax.numpy as jnp
import numpy as np
from jax import lax
from jax.experimental import pallas as pl
from jax.experimental.pallas import tpu as pltpu
from jax.sharding import PartitionSpec as P

EMB = 256
TR = 8
TC = 32
TSTEPS = 1000
C = 128
PIX = 256
HID = 256
SPAN = 8
MUL_POS = 1103515245
MUL_SEED = 747796405
ADD_POS = 1013904223
MUL_MIX = 73244475
ROOT3 = 1.7320508
NOISE_A = float(np.float32(2.0 * ROOT3 / 16777216.0))
NOISE_B = float(np.float32(ROOT3 * (1.0 / 16777216.0 - 1.0)))
F32 = jnp.float32
BF16 = jnp.bfloat16
ROW_TIME, ROW_IN, ROW_OUT, ROW_DOWN, ROW_UP, ROWS = 0, 512, 768, 1024, 2048, 3072
PARTS = 3
HALF = ROWS // 2
PART = HALF // PARTS


def wrap32(value):
    value &= 0xFFFFFFFF
    return value - (1 << 32) if value >= (1 << 31) else value


def dot(a, b):
    return lax.dot_general(a, b, (((1,), (0,)), ((), ())), preferred_element_type=F32)


def dot_bt(a, b):
    return lax.dot_general(a, b, (((1,), (1,)), ((), ())), preferred_element_type=F32)


def dot_at(a, b):
    return lax.dot_general(a, b, (((0,), (0,)), ((), ())), preferred_element_type=F32)


def shift_right(value, amount):
    return lax.shift_right_logical(value, jnp.int32(amount))


def group_sum(x, lane):
    pair = x + jnp.where(lane % 2 == 0, pltpu.roll(x, 127, 1), pltpu.roll(x, 1, 1))
    return pair + jnp.where(lane % 4 < 2, pltpu.roll(pair, 126, 1), pltpu.roll(pair, 2, 1))


def add_blocks(pack_ref, start, value):
    height = value.shape[0]
    for j in range(value.shape[1] // C):
        pack_ref[pl.ds(start + j * height, height), :] += value[:, j * C:(j + 1) * C]


def span_kernel(
    count_ref, mix_ref, sa_ref, sb_ref, weight_ref, seg_ref,
    tiles_hbm, col_ref, emb_ref, slot_ref, wt_ref, gain_ref,
    win_ref, wout_ref, wdown_ref, wup_ref,
    pack_ref, misc_ref,
    buf, sem, itab, perm, modul, noise, noisy, x_s, hid, slope, resid, patch,
    dact, dslope, glift, gpd_s, gres, gph_s, s1_s, s2_s, loss_s, stat,
    win_h, wout_h, wdown_h, wup_h,
):
    count = count_ref[0]

    def fetch(span, slot):
        return pltpu.make_async_copy(
            tiles_hbm.at[pl.ds(span * SPAN, SPAN)], buf.at[slot], sem.at[slot]
        )

    @pl.when(count > 0)
    def _():
        fetch(0, 0).start()

    row = lax.broadcasted_iota(jnp.int32, (PIX, C), 0)
    lane = lax.broadcasted_iota(jnp.int32, (PIX, C), 1)
    quad, rest = row // 64, row % 64
    pixel = (2 * (rest // 16) + quad // 2) * TC + 2 * (rest % 16) + quad % 2
    itab[...] = (pixel * C + lane) * jnp.int32(MUL_POS)
    prow = lax.broadcasted_iota(jnp.int32, (PIX, PIX), 0)
    pcol = lax.broadcasted_iota(jnp.int32, (PIX, PIX), 1)
    pquad, prest = prow // 64, prow % 64
    ppix = (2 * (prest // 16) + pquad // 2) * TC + 2 * (prest % 16) + pquad % 2
    perm[...] = jnp.where(ppix == pcol, 1.0, 0.0).astype(BF16)
    modul[...] = dot(emb_ref[...], wt_ref[...])
    win_h[...] = win_ref[...] * jnp.asarray(0.5, BF16)
    wdown_h[...] = wdown_ref[...] * jnp.asarray(0.5, BF16)
    wout_h[...] = wout_ref[...] * jnp.asarray(0.5, BF16)
    wup_h[...] = wup_ref[...] * jnp.asarray(0.5, BF16)
    for ref in (pack_ref, s1_s, s2_s, loss_s):
        ref[...] = jnp.zeros_like(ref)
    lane8 = lax.broadcasted_iota(jnp.int32, (SPAN, C), 1)

    @pl.loop(0, count)
    def _(span):
        slot = lax.rem(span, 2)
        base = span * SPAN

        @pl.when(span + 1 < count)
        def _():
            fetch(span + 1, 1 - slot).start()

        fetch(span, slot).wait()

        for k in range(SPAN):
            mixed = itab[...] + mix_ref[base + k]
            mixed = mixed ^ shift_right(mixed, 16)
            mixed = mixed * jnp.int32(MUL_MIX)
            mixed = mixed ^ shift_right(mixed, 16)
            mixed = mixed * jnp.int32(MUL_MIX)
            mixed = mixed ^ shift_right(mixed, 16)
            field = shift_right(mixed, 8).astype(F32) * NOISE_A + NOISE_B
            noise[k] = field
            pixels = dot(perm[...], buf[slot, k])
            value = sa_ref[base + k] * pixels + sb_ref[base + k] * field
            noisy[k] = value
            stat[0, pl.ds(k, 1), :] = jnp.sum(value, axis=0, keepdims=True)
            stat[1, pl.ds(k, 1), :] = jnp.sum(value * value, axis=0, keepdims=True)

        rows8 = pl.ds(pl.multiple_of(base, SPAN), SPAN)
        seg = col_ref[0, rows8, :]
        inv_count = col_ref[1, rows8, :]
        first = jnp.zeros((SPAN, C), F32)
        square = jnp.zeros((SPAN, C), F32)
        for k in range(SPAN):
            member = seg == seg_ref[base + k]
            first += jnp.where(member, stat[0, pl.ds(k, 1), :], 0.0)
            square += jnp.where(member, stat[1, pl.ds(k, 1), :], 0.0)
        mean = group_sum(first, lane8) * inv_count
        var = group_sum(square, lane8) * inv_count - mean * mean
        spread = lax.rsqrt(var + 1e-05)
        factor = spread * gain_ref[...] * (1.0 + modul[rows8, :C])
        shift = modul[rows8, C:]
        stat[0] = mean
        stat[1] = factor
        stat[2] = shift
        stat[3] = spread

        for k in range(SPAN):
            one = pl.ds(k, 1)
            centre = noisy[k] - stat[0, one, :]
            normal = (centre * stat[1, one, :] + stat[2, one, :]).astype(BF16)
            x_s[k] = normal
            half = dot(normal, win_h[...])
            th = jnp.tanh(half)
            q = 1.0 + th
            h = half * q
            slope[k] = q + h * (1.0 - th)
            hb = h.astype(BF16)
            hid[k] = hb
            out = dot(hb, wout_ref[...]) + noisy[k]
            resid[k] = out
            outb = out.astype(BF16)
            for j in range(4):
                patch[pl.ds(k * 64, 64), pl.ds(j * C, C)] = outb[j * 64:(j + 1) * 64]

        for m in range(4):
            rows = pl.ds(m * 128, 128)
            half = dot(patch[rows, :], wdown_h[...])
            th = jnp.tanh(half)
            q = 1.0 + th
            h = half * q
            dslope[rows, :] = q + h * (1.0 - th)
            hb = h.astype(BF16)
            dact[rows, :] = hb
            lifted = dot(hb, wup_ref[...])
            for t in range(2):
                k = m * 2 + t
                weight = weight_ref[base + k]
                total = jnp.zeros((64, C), F32)
                for j in range(4):
                    part = pl.ds(j * 64, 64)
                    err = (
                        resid[k, part, :]
                        + lifted[t * 64:(t + 1) * 64, j * C:(j + 1) * C]
                        - noise[k, part, :]
                    )
                    total += err * err
                    gp = err * weight
                    resid[k, part, :] = gp
                    glift[pl.ds(k * 64, 64), pl.ds(j * C, C)] = gp.astype(BF16)
                loss_s[pl.ds(base + k, 1), :] = jnp.sum(total, axis=0, keepdims=True)
            gpd = (dot_bt(glift[rows, :], wup_h[...]) * dslope[rows, :]).astype(BF16)
            gpd_s[rows, :] = gpd
            back = dot_bt(gpd, wdown_ref[...])
            for t in range(2):
                k = m * 2 + t
                for j in range(4):
                    part = pl.ds(j * 64, 64)
                    gres[k, part, :] = (
                        resid[k, part, :] + back[t * 64:(t + 1) * 64, j * C:(j + 1) * C]
                    ).astype(BF16)

        for k in range(SPAN):
            one = pl.ds(k, 1)
            gph = (dot_bt(gres[k], wout_h[...]) * slope[k]).astype(BF16)
            gph_s[k] = gph
            gn = dot_bt(gph, win_ref[...])
            centre = noisy[k] - stat[0, one, :]
            s1_s[pl.ds(base + k, 1), :] = jnp.sum(gn, axis=0, keepdims=True)
            s2_s[pl.ds(base + k, 1), :] = (
                jnp.sum(gn * centre, axis=0, keepdims=True) * stat[3, one, :]
            )

        flat = SPAN * PIX
        add_blocks(pack_ref, ROW_UP, dot_at(dact[...], glift[...]))
        add_blocks(pack_ref, ROW_DOWN, dot_at(gpd_s[...], patch[...]))
        add_blocks(
            pack_ref, ROW_OUT, dot_at(gres[...].reshape(flat, C), hid[...].reshape(flat, HID))
        )
        add_blocks(
            pack_ref, ROW_IN, dot_at(x_s[...].reshape(flat, C), gph_s[...].reshape(flat, HID))
        )

    scale1 = 1.0 + modul[:, :C]
    s2 = s2_s[...]
    misc_ref[...] = jnp.zeros_like(misc_ref)
    misc_ref[pl.ds(0, 1), :] = jnp.sum(s2 * scale1, axis=0, keepdims=True)
    tile_loss = jnp.sum(loss_s[...], axis=1, keepdims=True) * col_ref[2]
    hits = slot_ref[...] == lax.broadcasted_iota(jnp.int32, (C, C), 1)
    misc_ref[pl.ds(1, 1), :] = jnp.sum(jnp.where(hits, tile_loss, 0.0), axis=0, keepdims=True)
    emb = emb_ref[...].astype(F32)
    for ref, part in ((s2 * gain_ref[...], 0), (s1_s[...], 1)):
        pack_ref[pl.ds(ROW_TIME + part * EMB, EMB), :] = lax.dot_general(
            emb, ref, (((0,), (0,)), ((), ())),
            precision=lax.Precision.HIGHEST, preferred_element_type=F32,
        )


def tile_tables(sizes, dests, times, seeds, group, tile_count):
    clip_count = sizes.shape[0]
    ends = jnp.cumsum(sizes, dtype=jnp.int32)
    tile = jnp.arange(tile_count, dtype=jnp.int32)
    owner = jnp.sum((ends[None, :] <= tile[:, None]).astype(jnp.int32), axis=1)
    onehot = (owner[:, None] == jnp.arange(clip_count, dtype=jnp.int32)[None, :]).astype(jnp.int32)
    columns = jnp.stack([ends - sizes, sizes, dests, times, seeds], axis=0)
    found = jnp.sum(onehot[None] * columns[:, None, :], axis=2)
    usable = owner < clip_count
    within = jnp.where(usable, tile - found[0], 0)
    length = jnp.where(usable, found[1], 1)
    step = found[3].astype(F32)
    alpha_bar = jnp.cos(((step + 1.0) / TSTEPS + 0.008) / 1.008 * (math.pi / 2.0)) ** 2
    mix = within * jnp.int32(wrap32(PIX * C * MUL_POS)) + found[4] * jnp.int32(MUL_SEED) + jnp.int32(ADD_POS)
    inv_len = 1.0 / length.astype(F32)
    weight = jnp.where(usable, inv_len * (2.0 / (PIX * C)), 0.0)
    half = EMB // 2
    freq = jnp.exp(-math.log(10000.0) * jnp.arange(half, dtype=F32) / half)
    angle = step[:, None] * freq[None, :]
    emb = jnp.concatenate([jnp.cos(angle), jnp.sin(angle)], axis=1).astype(BF16)
    slot = jnp.where(usable, found[2] * 4 + group, -1)
    cols = jnp.stack([owner.astype(F32), inv_len / (PIX * 4), weight * 0.5], axis=0)
    cols = jnp.broadcast_to(cols[:, :, None], (3, tile_count, C))
    slots = jnp.broadcast_to(slot[:, None], (tile_count, C))
    count = jnp.sum(sizes) // SPAN
    return (
        count.reshape(1), mix, jnp.sqrt(alpha_bar), jnp.sqrt(1.0 - alpha_bar), weight,
        owner.astype(F32), cols, emb, slots,
    )


def local_grads(clip_tiles, sizes, dests, times, seeds, group, w_time, gain, w_in, w_out, w_down, w_up):
    tile_count = clip_tiles.shape[0]
    count, mix, sa, sb, weight, seg, cols, emb, slots = tile_tables(
        sizes, dests, times, seeds, group, tile_count
    )
    smem = pl.BlockSpec(memory_space=pltpu.SMEM)
    vmem = pl.BlockSpec(memory_space=pltpu.VMEM)
    shapes = [(ROWS, C), (8, C)]
    return pl.pallas_call(
        span_kernel,
        out_shape=[jax.ShapeDtypeStruct(s, F32) for s in shapes],
        in_specs=[smem] * 6 + [pl.BlockSpec(memory_space=pl.ANY)] + [vmem] * 9,
        out_specs=[vmem] * 2,
        scratch_shapes=[
            pltpu.VMEM((2, SPAN, PIX, C), BF16),
            pltpu.SemaphoreType.DMA((2,)),
            pltpu.VMEM((PIX, C), jnp.int32),
            pltpu.VMEM((PIX, PIX), BF16),
            pltpu.VMEM((tile_count, 2 * C), F32),
            pltpu.VMEM((SPAN, PIX, C), F32),
            pltpu.VMEM((SPAN, PIX, C), F32),
            pltpu.VMEM((SPAN, PIX, C), BF16),
            pltpu.VMEM((SPAN, PIX, HID), BF16),
            pltpu.VMEM((SPAN, PIX, HID), F32),
            pltpu.VMEM((SPAN, PIX, C), F32),
            pltpu.VMEM((512, 512), BF16),
            pltpu.VMEM((512, 256), BF16),
            pltpu.VMEM((512, 256), F32),
            pltpu.VMEM((512, 512), BF16),
            pltpu.VMEM((512, 256), BF16),
            pltpu.VMEM((SPAN, PIX, C), BF16),
            pltpu.VMEM((SPAN, PIX, HID), BF16),
            pltpu.VMEM((tile_count, C), F32),
            pltpu.VMEM((tile_count, C), F32),
            pltpu.VMEM((tile_count, C), F32),
            pltpu.VMEM((4, SPAN, C), F32),
            pltpu.VMEM((C, HID), BF16),
            pltpu.VMEM((HID, C), BF16),
            pltpu.VMEM((512, 256), BF16),
            pltpu.VMEM((256, 512), BF16),
        ],
        compiler_params=pltpu.CompilerParams(vmem_limit_bytes=56 * 1024 * 1024),
    )(count, mix, sa, sb, weight, seg, clip_tiles, cols, emb, slots, w_time,
      gain.reshape(1, C), w_in, w_out, w_down, w_up)


def reduce_kernel(
    sizes, x_hbm, misc_ref, res, misc_out,
    acc, other, r1, r2, r3, m_core, m_axes, local_sem, send_sem, recv_sem,
):
    dp, z = lax.axis_index("dp"), lax.axis_index("rep")
    ny = sizes[1]
    core = lax.rem(dp, 2)
    chip = lax.div(dp, 2)
    coord = (lax.div(chip, ny), lax.rem(chip, ny), z)

    def device(x, y, zz, c):
        return ((x * ny + y) * 2 + c, zz)

    def peer(axis, r):
        other_coord = lax.rem(coord[axis] + r, sizes[axis])
        place = list(coord)
        place[axis] = other_coord
        return other_coord, device(*place, core)

    sibling = device(*coord, 1 - core)
    peers = [(axis, r) for axis in range(3) for r in range(1, sizes[axis])]
    barrier = pltpu.get_barrier_semaphore()
    for target in [sibling] + [peer(axis, r)[1] for axis, r in peers]:
        pl.semaphore_signal(barrier, inc=1, device_id=target, device_id_type=pl.DeviceIdType.MESH)

    mine = core * HALF
    theirs = (1 - core) * HALF
    local = []
    for p in range(PARTS):
        copy = pltpu.make_async_copy(
            x_hbm.at[pl.ds(pl.multiple_of(mine + p * PART, 8), PART)],
            acc.at[pl.ds(p * PART, PART)], local_sem.at[p],
        )
        copy.start()
        local.append(copy)
    pl.semaphore_wait(barrier, 1 + len(peers))

    started = []

    def send(src, dst, target):
        index = len(started)
        copy = pltpu.make_async_remote_copy(
            src_ref=src, dst_ref=dst, send_sem=send_sem.at[index], recv_sem=recv_sem.at[index],
            device_id=target, device_id_type=pl.DeviceIdType.MESH,
        )
        copy.start()
        started.append(copy)
        return copy

    m_core_copy = send(misc_ref, m_core, sibling)
    first = [
        send(
            x_hbm.at[pl.ds(pl.multiple_of(theirs + p * PART, 8), PART)],
            other.at[pl.ds(p * PART, PART)], sibling,
        )
        for p in range(PARTS)
    ]

    order = [[(p + s) % 3 for s in range(3)] for p in range(PARTS)]
    lengths = []
    for p in range(PARTS):
        length, row = PART, []
        for s in range(3):
            length //= sizes[order[p][s]]
            row.append(length)
        lengths.append(row)
    landing = (r1, r2, r3)
    base = [jnp.int32(p * PART) for p in range(PARTS)]
    starts = [[None] * 3 for _ in range(PARTS)]

    def scatter(p, s):
        axis, length = order[p][s], lengths[p][s]
        copies = []
        for r in range(1, sizes[axis]):
            q, target = peer(axis, r)
            rows = pl.ds(pl.multiple_of(base[p] + q * length, 8), length)
            copies.append(send(acc.at[rows], landing[s].at[p, r - 1], target))
        base[p] = base[p] + coord[axis] * length
        starts[p][s] = base[p]
        return copies

    flying = [None] * PARTS
    for p in range(PARTS):
        local[p].wait()
        first[p].wait_recv()
        rows = pl.ds(p * PART, PART)
        acc[rows, :] = acc[rows, :] + other[rows, :]
        flying[p] = scatter(p, 0)
    m_core_copy.wait_recv()

    def misc_stage(axis, value):
        m_axes[axis, coord[axis]] = value
        return [
            send(m_axes.at[axis, coord[axis]], m_axes.at[axis, coord[axis]], peer(axis, r)[1])
            for r in range(1, sizes[axis])
        ]

    def misc_total(axis, copies):
        for copy in copies:
            copy.wait_recv()
        total = m_axes[axis, 0]
        for i in range(1, sizes[axis]):
            total = total + m_axes[axis, i]
        return total

    misc_copies = misc_stage(0, misc_ref[...] + m_core[...])
    for s in range(3):
        for p in range(PARTS):
            for copy in flying[p]:
                copy.wait_recv()
            rows = pl.ds(pl.multiple_of(base[p], 8), lengths[p][s])
            total = acc[rows, :]
            for r in range(sizes[order[p][s]] - 1):
                total = total + landing[s][p, r]
            if s < 2:
                acc[rows, :] = total
                flying[p] = scatter(p, s + 1)
            else:
                final = pl.ds(pl.multiple_of(mine + base[p], 8), lengths[p][s])
                res[final, :] = total
                flying[p] = gather(p, 2, sizes, order, lengths, starts, mine, peer, send, res)
        misc_value = misc_total(s, misc_copies)
        if s < 2:
            misc_copies = misc_stage(s + 1, misc_value)
    misc_out[...] = misc_value
    for s in (1, 0):
        for p in range(PARTS):
            for copy in flying[p]:
                copy.wait_recv()
            flying[p] = gather(p, s, sizes, order, lengths, starts, mine, peer, send, res)
    last = []
    for p in range(PARTS):
        for copy in flying[p]:
            copy.wait_recv()
        rows = pl.ds(pl.multiple_of(mine + p * PART, 8), PART)
        last.append(send(res.at[rows], res.at[rows], sibling))
    for copy in last:
        copy.wait_recv()
    for copy in started:
        copy.wait_send()


def gather(p, s, sizes, order, lengths, starts, mine, peer, send, res):
    axis = order[p][s]
    rows = pl.ds(pl.multiple_of(mine + starts[p][s], 8), lengths[p][s])
    return [send(res.at[rows], res.at[rows], peer(axis, r)[1]) for r in range(1, sizes[axis])]


def all_reduce(packed, misc, sizes):
    vmem = pl.BlockSpec(memory_space=pltpu.VMEM)
    most = max(sizes) - 1
    per_axis = sum(n - 1 for n in sizes)
    copies = 1 + PARTS + per_axis * (2 * PARTS + 1) + PARTS
    shapes = []
    for s in range(3):
        longest = 0
        for p in range(PARTS):
            length = PART
            for i in range(s + 1):
                length //= sizes[(p + i) % 3]
            longest = max(longest, length)
        shapes.append(longest)
    return pl.pallas_call(
        functools.partial(reduce_kernel, sizes),
        out_shape=[jax.ShapeDtypeStruct((ROWS, C), F32), jax.ShapeDtypeStruct((8, C), F32)],
        in_specs=[pl.BlockSpec(memory_space=pl.ANY), vmem],
        out_specs=[vmem, vmem],
        scratch_shapes=[
            pltpu.VMEM((HALF, C), F32),
            pltpu.VMEM((HALF, C), F32),
            pltpu.VMEM((PARTS, most, shapes[0], C), F32),
            pltpu.VMEM((PARTS, most, shapes[1], C), F32),
            pltpu.VMEM((PARTS, most, shapes[2], C), F32),
            pltpu.VMEM((8, C), F32),
            pltpu.VMEM((3, max(sizes), 8, C), F32),
            pltpu.SemaphoreType.DMA((PARTS,)),
            pltpu.SemaphoreType.DMA((copies,)),
            pltpu.SemaphoreType.DMA((copies,)),
        ],
        compiler_params=pltpu.CompilerParams(
            collective_id=0, has_side_effects=True, vmem_limit_bytes=32 * 1024 * 1024
        ),
    )(packed, misc)


def finish_kernel(packed, misc, gt, gain, gin, gout, gdown, gup, own):
    def block(start, height, j):
        return packed[pl.ds(start + j * height, height), :]

    for j in range(2):
        cols = pl.ds(j * C, C)
        gt[:, cols] = block(ROW_TIME, EMB, j)
        gin[:, cols] = block(ROW_IN, C, j)
        gout[cols, :] = block(ROW_OUT, C, j).T
    for j in range(4):
        cols = pl.ds(j * C, C)
        gdown[cols, :] = block(ROW_DOWN, 256, j).T
        gup[:, cols] = block(ROW_UP, 256, j)
    gain[...] = misc[pl.ds(0, 1), :]
    me = lax.axis_index("dp") * lax.axis_size("rep") + lax.axis_index("rep")
    lane = lax.broadcasted_iota(jnp.int32, (1, C), 1)
    own[0] = jnp.sum(jnp.where(lane == me, misc[pl.ds(1, 1), :], 0.0))


def finish(packed, misc):
    vmem = pl.BlockSpec(memory_space=pltpu.VMEM)
    shapes = [(EMB, 2 * C), (1, C), (C, HID), (HID, C), (512, 256), (256, 512), (1,)]
    return pl.pallas_call(
        finish_kernel,
        out_shape=[jax.ShapeDtypeStruct(s, F32) for s in shapes],
        in_specs=[vmem, vmem],
        out_specs=[vmem] * 6 + [pl.BlockSpec(memory_space=pltpu.SMEM)],
        compiler_params=pltpu.CompilerParams(vmem_limit_bytes=32 * 1024 * 1024),
    )(packed, misc)


def body(sizes, clip_tiles, clip_size, clip_dest, timesteps, noise_seeds, w_time, gain, w_in, w_out, w_down, w_up):
    group = lax.axis_index("rep")
    packed, misc = local_grads(
        clip_tiles, clip_size[0], clip_dest[0], timesteps[0], noise_seeds[0], group,
        w_time, gain, w_in, w_out, w_down, w_up,
    )
    packed, misc = all_reduce(packed, misc, sizes)
    gt, ggain, gin, gout, gdown, gup, own = finish(packed, misc)
    return (gt, ggain.reshape(C), gin, gout, gdown, gup, own)


def solution(mesh):
    rows = P(("dp", "rep"), None)
    in_specs = (P(("dp", "rep"), None, None), rows, rows, rows, rows) + (P(),) * 6
    out_specs = (P(),) * 6 + (P(("dp", "rep")),)
    sizes = (4, mesh.shape["dp"] // 8, mesh.shape["rep"])
    return jax.shard_map(functools.partial(body, sizes), mesh=mesh, in_specs=in_specs, out_specs=out_specs, check_vma=False)
```

```python
import functools
import math

import jax
import jax.numpy as jnp
import numpy as np
from jax import lax
from jax.experimental import pallas as pl
from jax.experimental.pallas import tpu as pltpu
from jax.sharding import PartitionSpec as P

EMB = 256
TR = 8
TC = 32
TSTEPS = 1000
C = 128
PIX = 256
HID = 256
SPAN = 8
RUN = 4
CLIPS = 64
MUL_POS = 1103515245
MUL_SEED = 747796405
ADD_POS = 1013904223
MUL_MIX = 73244475
ROOT3 = 1.7320508
NOISE_A = float(np.float32(2.0 * ROOT3 / 16777216.0))
NOISE_B = float(np.float32(ROOT3 * (1.0 / 16777216.0 - 1.0)))
CHUNK, SKEW = 8, 1
F32 = jnp.float32
BF16 = jnp.bfloat16
ROW_TIME, ROW_IN, ROW_OUT, ROW_DOWN, ROW_UP, ROWS = 0, 512, 768, 1024, 2048, 3072
PARTS = 3
HALF = ROWS // 2
PART = HALF // PARTS


def wrap32(value):
    value &= 0xFFFFFFFF
    return value - (1 << 32) if value >= (1 << 31) else value


def dot(a, b):
    return lax.dot_general(a, b, (((1,), (0,)), ((), ())), preferred_element_type=F32)


def dot_bt(a, b):
    return lax.dot_general(a, b, (((1,), (1,)), ((), ())), preferred_element_type=F32)


def dot_at(a, b):
    return lax.dot_general(a, b, (((0,), (0,)), ((), ())), preferred_element_type=F32)


def shift_right(value, amount):
    return lax.shift_right_logical(value, jnp.int32(amount))


def group_sum(x, lane):
    pair = x + jnp.where(lane % 2 == 0, pltpu.roll(x, 127, 1), pltpu.roll(x, 1, 1))
    return pair + jnp.where(lane % 4 < 2, pltpu.roll(pair, 126, 1), pltpu.roll(pair, 2, 1))


def add_blocks(pack_ref, start, value):
    height = value.shape[0]
    for j in range(value.shape[1] // C):
        pack_ref[pl.ds(start + j * height, height), :] += value[:, j * C:(j + 1) * C]


def span_kernel(
    sizes_ref, seeds_ref, tiles_hbm, sizes_row, dest_row, time_row, freq_ref, wt_ref, gain_ref,
    win_ref, wout_ref, wdown_ref, wup_ref,
    pack_ref, misc_ref,
    buf, sem, itab, perm, emb_s, film_scale, film_shift, sa_s, sb_s, weight_s, inv_s,
    noise, noisy, x_s, hid, slope, resid, patch,
    dact, dslope, glift, gpd_s, gres, gph_s, s1_s, s2_s, loss_s, stat,
    win_h, wout_h, wdown_h, wup_h,
):
    total = sizes_ref[0, 0]
    for entry in range(1, CLIPS):
        total += sizes_ref[0, entry]
    count = total // SPAN

    def fetch(span, slot):
        return pltpu.make_async_copy(
            tiles_hbm.at[pl.ds(span * SPAN, SPAN)], buf.at[slot], sem.at[slot]
        )

    @pl.when(count > 0)
    def _():
        fetch(0, 0).start()

    row = lax.broadcasted_iota(jnp.int32, (PIX, C), 0)
    lane = lax.broadcasted_iota(jnp.int32, (PIX, C), 1)
    quad, rest = row // 64, row % 64
    pixel = (2 * (rest // 16) + quad // 2) * TC + 2 * (rest % 16) + quad % 2
    itab[...] = (pixel * C + lane) * jnp.int32(MUL_POS)
    prow = lax.broadcasted_iota(jnp.int32, (PIX, PIX), 0)
    pcol = lax.broadcasted_iota(jnp.int32, (PIX, PIX), 1)
    pquad, prest = prow // 64, prow % 64
    ppix = (2 * (prest // 16) + pquad // 2) * TC + 2 * (prest % 16) + pquad % 2
    perm[...] = jnp.where(ppix == pcol, 1.0, 0.0).astype(BF16)
    eye = lax.broadcasted_iota(jnp.int32, (CLIPS, CLIPS), 0) == lax.broadcasted_iota(
        jnp.int32, (CLIPS, CLIPS), 1
    )

    def column(values):
        picked = jnp.sum(jnp.where(eye, values, 0.0), axis=1, keepdims=True)
        return jnp.broadcast_to(picked, (CLIPS, C))

    step = time_row[...].astype(F32)
    alpha_bar = jnp.cos(((step + 1.0) / TSTEPS + 0.008) / 1.008 * (math.pi / 2.0)) ** 2
    sa_s[...] = column(jnp.sqrt(alpha_bar))
    sb_s[...] = column(jnp.sqrt(1.0 - alpha_bar))
    inv_len = 1.0 / column(jnp.maximum(sizes_row[...], 1).astype(F32))
    inv_s[...] = inv_len * (1.0 / (PIX * 4))
    weight_s[...] = inv_len * (2.0 / (PIX * C))
    angle = column(step) * freq_ref[...]
    emb_s[:, :C] = jnp.cos(angle).astype(BF16)
    emb_s[:, C:] = jnp.sin(angle).astype(BF16)
    modulation = dot(emb_s[...], wt_ref[...])
    film_scale[...] = modulation[:, :C]
    film_shift[...] = modulation[:, C:]
    win_h[...] = win_ref[...] * jnp.asarray(0.5, BF16)
    wdown_h[...] = wdown_ref[...] * jnp.asarray(0.5, BF16)
    wout_h[...] = wout_ref[...] * jnp.asarray(0.5, BF16)
    wup_h[...] = wup_ref[...] * jnp.asarray(0.5, BF16)
    for ref in (pack_ref, s1_s, s2_s, loss_s):
        ref[...] = jnp.zeros_like(ref)
    lane8 = lax.broadcasted_iota(jnp.int32, (SPAN, C), 1)

    def marks(span):
        one = sizes_ref[0, span * RUN]
        two = one + sizes_ref[0, span * RUN + 1]
        return one, two, two + sizes_ref[0, span * RUN + 2]

    def owner_of(tile, bounds):
        return sum((tile >= bound).astype(jnp.int32) for bound in bounds)

    def make_noisy(span, slot):
        bounds = marks(span)
        owners = [owner_of(jnp.int32(k), bounds) for k in range(SPAN)]
        for k in range(SPAN):
            if k % 2 == 0:
                pair = dot(
                    perm[...], jnp.concatenate([buf[slot, k], buf[slot, k + 1]], axis=1)
                )
            entry = span * RUN + owners[k]
            row = pl.ds(entry, 1)
            start = jnp.int32(0)
            for bound in bounds:
                start = jnp.where(k >= bound, bound, start)
            mix = (
                (k - start) * jnp.int32(wrap32(PIX * C * MUL_POS))
                + seeds_ref[0, entry] * jnp.int32(MUL_SEED) + jnp.int32(ADD_POS)
            )
            stat[4, pl.ds(k, 1), :] = inv_s[row, :]
            stat[5, pl.ds(k, 1), :] = film_scale[row, :]
            stat[6, pl.ds(k, 1), :] = film_shift[row, :]
            mixed = itab[...] + mix
            mixed = mixed ^ shift_right(mixed, 16)
            mixed = mixed * jnp.int32(MUL_MIX)
            mixed = mixed ^ shift_right(mixed, 16)
            mixed = mixed * jnp.int32(MUL_MIX)
            mixed = mixed ^ shift_right(mixed, 16)
            field = shift_right(mixed, 8).astype(F32) * NOISE_A + NOISE_B
            noise[k] = field
            pixels = pair[:, (k % 2) * C:(k % 2 + 1) * C]
            value = sa_s[row, :] * pixels + sb_s[row, :] * field
            noisy[k] = value
            stat[0, pl.ds(k, 1), :] = jnp.sum(value, axis=0, keepdims=True)
            stat[1, pl.ds(k, 1), :] = jnp.sum(value * value, axis=0, keepdims=True)

        tile8 = lax.broadcasted_iota(jnp.int32, (SPAN, C), 0)
        seg = owner_of(tile8, bounds)
        inv_count = stat[4]
        first = jnp.zeros((SPAN, C), F32)
        square = jnp.zeros((SPAN, C), F32)
        for k in range(SPAN):
            member = seg == owners[k]
            first += jnp.where(member, stat[0, pl.ds(k, 1), :], 0.0)
            square += jnp.where(member, stat[1, pl.ds(k, 1), :], 0.0)
        mean = group_sum(first, lane8) * inv_count
        var = group_sum(square, lane8) * inv_count - mean * mean
        spread = lax.rsqrt(var + 1e-05)
        factor = spread * gain_ref[...] * (1.0 + stat[5])
        shift = stat[6]
        stat[0] = mean
        stat[1] = factor
        stat[2] = shift
        stat[3] = spread

    @pl.when(count > 0)
    def _():
        @pl.when(count > 1)
        def _():
            fetch(1, 1).start()

        fetch(0, 0).wait()
        make_noisy(0, 0)

    @pl.loop(0, count)
    def _(span):
        bounds = marks(span)
        entries = [span * RUN + owner_of(jnp.int32(k), bounds) for k in range(SPAN)]
        following = jnp.minimum(span + 1, count - 1)
        slot = lax.rem(span + 1, 2)

        @pl.when(span + 1 < count)
        def _():
            fetch(span + 1, slot).wait()

        @pl.when(span + 2 < count)
        def _():
            fetch(span + 2, 1 - slot).start()

        def chunk_steps(k0):
            tiles = range(k0, k0 + CHUNK)
            rows = pl.ds(k0 * PIX, CHUNK * PIX)
            quads = pl.ds(k0 * 64, CHUNK * 64)
            held = {}

            def normalise():
                for k in tiles:
                    one = pl.ds(k, 1)
                    centre = noisy[k] - stat[0, one, :]
                    x_s[pl.ds(k * PIX, PIX), :] = (
                        centre * stat[1, one, :] + stat[2, one, :]
                    ).astype(BF16)

            def project():
                held["half"] = dot(x_s[rows, :], win_h[...])

            def activate():
                half = held["half"]
                th = jnp.tanh(half)
                q = 1.0 + th
                h = half * q
                slope[rows, :] = q + h * (1.0 - th)
                hid[rows, :] = h.astype(BF16)

            def project_back():
                held["out"] = dot(hid[rows, :], wout_ref[...])

            def residual():
                for k in tiles:
                    at = (k - k0) * PIX
                    out = held["out"][at:at + PIX] + noisy[k]
                    resid[k] = out
                    outb = out.astype(BF16)
                    for j in range(4):
                        patch[pl.ds(k * 64, 64), pl.ds(j * C, C)] = outb[j * 64:(j + 1) * 64]

            def down():
                held["half"] = dot(patch[quads, :], wdown_h[...])

            def down_activate():
                half = held["half"]
                th = jnp.tanh(half)
                q = 1.0 + th
                h = half * q
                dslope[quads, :] = q + h * (1.0 - th)
                dact[quads, :] = h.astype(BF16)

            def up():
                held["lifted"] = dot(dact[quads, :], wup_ref[...])

            def error():
                for k in tiles:
                    at = (k - k0) * 64
                    row = pl.ds(entries[k], 1)
                    weight = weight_s[row, :]
                    total = jnp.zeros((64, C), F32)
                    for j in range(4):
                        part = pl.ds(j * 64, 64)
                        err = (
                            resid[k, part, :]
                            + held["lifted"][at:at + 64, j * C:(j + 1) * C]
                            - noise[k, part, :]
                        )
                        total += err * err
                        gp = err * weight
                        resid[k, part, :] = gp
                        glift[pl.ds(k * 64, 64), pl.ds(j * C, C)] = gp.astype(BF16)
                    loss_s[row, :] += jnp.sum(total, axis=0, keepdims=True)

            def up_back():
                held["gda"] = dot_bt(glift[quads, :], wup_h[...])

            def down_slope():
                gpd_s[quads, :] = (held["gda"] * dslope[quads, :]).astype(BF16)

            def down_back():
                held["back"] = dot_bt(gpd_s[quads, :], wdown_ref[...])

            def grad_residual():
                for k in tiles:
                    at = (k - k0) * 64
                    for j in range(4):
                        part = pl.ds(j * 64, 64)
                        gres[pl.ds(k * PIX + j * 64, 64), :] = (
                            resid[k, part, :] + held["back"][at:at + 64, j * C:(j + 1) * C]
                        ).astype(BF16)

            def out_back():
                held["gh"] = dot_bt(gres[rows, :], wout_h[...])

            def hidden_slope():
                gph_s[rows, :] = (held["gh"] * slope[rows, :]).astype(BF16)

            def in_back():
                held["gn"] = dot_bt(gph_s[rows, :], win_ref[...])

            def tile_sums():
                for k in tiles:
                    at = (k - k0) * PIX
                    one = pl.ds(k, 1)
                    centre = noisy[k] - stat[0, one, :]
                    mine = held["gn"][at:at + PIX]
                    row = pl.ds(entries[k], 1)
                    s1_s[row, :] += jnp.sum(mine, axis=0, keepdims=True)
                    s2_s[row, :] += (
                        jnp.sum(mine * centre, axis=0, keepdims=True) * stat[3, one, :]
                    )

            return [
                normalise, project, activate, project_back, residual, down, down_activate, up,
                error, up_back, down_slope, down_back, grad_residual, out_back, hidden_slope,
                in_back, tile_sums,
            ]

        chunks = [chunk_steps(k0) for k0 in range(0, SPAN, CHUNK)]
        for turn in range(len(chunks[0]) + SKEW * (len(chunks) - 1)):
            for index, steps in enumerate(chunks):
                if 0 <= turn - SKEW * index < len(steps):
                    steps[turn - SKEW * index]()

        make_noisy(following, slot)
        add_blocks(pack_ref, ROW_UP, dot_at(dact[...], glift[...]))
        add_blocks(pack_ref, ROW_DOWN, dot_at(gpd_s[...], patch[...]))
        add_blocks(
            pack_ref, ROW_OUT, dot_at(gres[...], hid[...])
        )
        add_blocks(
            pack_ref, ROW_IN, dot_at(x_s[...], gph_s[...])
        )

    scale1 = 1.0 + film_scale[...]
    s2 = s2_s[...]
    misc_ref[...] = jnp.zeros_like(misc_ref)
    misc_ref[pl.ds(0, 1), :] = jnp.sum(s2 * scale1, axis=0, keepdims=True)
    clip_loss = jnp.sum(loss_s[...], axis=1, keepdims=True) * weight_s[...] * 0.5
    place = column((dest_row[...] * lax.axis_size("rep") + lax.axis_index("rep")).astype(F32))
    hits = place == lax.broadcasted_iota(jnp.int32, (CLIPS, C), 1).astype(F32)
    misc_ref[pl.ds(1, 1), :] = jnp.sum(jnp.where(hits, clip_loss, 0.0), axis=0, keepdims=True)
    emb = emb_s[...].astype(F32)
    for ref, part in ((s2 * gain_ref[...], 0), (s1_s[...], 1)):
        pack_ref[pl.ds(ROW_TIME + part * EMB, EMB), :] = lax.dot_general(
            emb, ref, (((0,), (0,)), ((), ())),
            precision=lax.Precision.HIGHEST, preferred_element_type=F32,
        )


def local_grads(clip_tiles, sizes, dests, times, seeds, w_time, gain, w_in, w_out, w_down, w_up):
    smem = pl.BlockSpec(memory_space=pltpu.SMEM)
    vmem = pl.BlockSpec(memory_space=pltpu.VMEM)
    half = EMB // 2
    freq = np.exp(-math.log(10000.0) * np.arange(half) / half).astype(np.float32)
    return pl.pallas_call(
        span_kernel,
        out_shape=[jax.ShapeDtypeStruct(s, F32) for s in [(ROWS, C), (8, C)]],
        in_specs=[smem] * 2 + [pl.BlockSpec(memory_space=pl.ANY)] + [vmem] * 10,
        out_specs=[vmem] * 2,
        scratch_shapes=[
            pltpu.VMEM((2, SPAN, PIX, C), BF16),
            pltpu.SemaphoreType.DMA((2,)),
            pltpu.VMEM((PIX, C), jnp.int32),
            pltpu.VMEM((PIX, PIX), BF16),
            pltpu.VMEM((CLIPS, EMB), BF16),
            pltpu.VMEM((CLIPS, C), F32),
            pltpu.VMEM((CLIPS, C), F32),
            pltpu.VMEM((CLIPS, C), F32),
            pltpu.VMEM((CLIPS, C), F32),
            pltpu.VMEM((CLIPS, C), F32),
            pltpu.VMEM((CLIPS, C), F32),
            pltpu.VMEM((SPAN, PIX, C), F32),
            pltpu.VMEM((SPAN, PIX, C), F32),
            pltpu.VMEM((SPAN * PIX, C), BF16),
            pltpu.VMEM((SPAN * PIX, HID), BF16),
            pltpu.VMEM((SPAN * PIX, HID), F32),
            pltpu.VMEM((SPAN, PIX, C), F32),
            pltpu.VMEM((512, 512), BF16),
            pltpu.VMEM((512, 256), BF16),
            pltpu.VMEM((512, 256), F32),
            pltpu.VMEM((512, 512), BF16),
            pltpu.VMEM((512, 256), BF16),
            pltpu.VMEM((SPAN * PIX, C), BF16),
            pltpu.VMEM((SPAN * PIX, HID), BF16),
            pltpu.VMEM((CLIPS, C), F32),
            pltpu.VMEM((CLIPS, C), F32),
            pltpu.VMEM((CLIPS, C), F32),
            pltpu.VMEM((7, SPAN, C), F32),
            pltpu.VMEM((C, HID), BF16),
            pltpu.VMEM((HID, C), BF16),
            pltpu.VMEM((512, 256), BF16),
            pltpu.VMEM((256, 512), BF16),
        ],
        compiler_params=pltpu.CompilerParams(vmem_limit_bytes=56 * 1024 * 1024),
    )(sizes, seeds, clip_tiles, sizes, dests, times, freq.reshape(1, half), w_time,
      gain.reshape(1, C), w_in, w_out, w_down, w_up)


def reduce_kernel(
    sizes, x_hbm, misc_ref, res, misc_out,
    acc, other, r1, r2, r3, m_core, m_axes, local_sem, send_sem, recv_sem,
):
    dp, z = lax.axis_index("dp"), lax.axis_index("rep")
    ny = sizes[1]
    core = lax.rem(dp, 2)
    chip = lax.div(dp, 2)
    coord = (lax.div(chip, ny), lax.rem(chip, ny), z)

    def device(x, y, zz, c):
        return ((x * ny + y) * 2 + c, zz)

    def peer(axis, r):
        other_coord = lax.rem(coord[axis] + r, sizes[axis])
        place = list(coord)
        place[axis] = other_coord
        return other_coord, device(*place, core)

    sibling = device(*coord, 1 - core)
    peers = [(axis, r) for axis in range(3) for r in range(1, sizes[axis])]
    barrier = pltpu.get_barrier_semaphore()
    for target in [sibling] + [peer(axis, r)[1] for axis, r in peers]:
        pl.semaphore_signal(barrier, inc=1, device_id=target, device_id_type=pl.DeviceIdType.MESH)

    mine = core * HALF
    theirs = (1 - core) * HALF
    local = []
    for p in range(PARTS):
        copy = pltpu.make_async_copy(
            x_hbm.at[pl.ds(pl.multiple_of(mine + p * PART, 8), PART)],
            acc.at[pl.ds(p * PART, PART)], local_sem.at[p],
        )
        copy.start()
        local.append(copy)
    pl.semaphore_wait(barrier, 1 + len(peers))

    started = []

    def send(src, dst, target):
        index = len(started)
        copy = pltpu.make_async_remote_copy(
            src_ref=src, dst_ref=dst, send_sem=send_sem.at[index], recv_sem=recv_sem.at[index],
            device_id=target, device_id_type=pl.DeviceIdType.MESH,
        )
        copy.start()
        started.append(copy)
        return copy

    m_core_copy = send(misc_ref, m_core, sibling)
    first = [
        send(
            x_hbm.at[pl.ds(pl.multiple_of(theirs + p * PART, 8), PART)],
            other.at[pl.ds(p * PART, PART)], sibling,
        )
        for p in range(PARTS)
    ]

    order = [[(p + s) % 3 for s in range(3)] for p in range(PARTS)]
    lengths = []
    for p in range(PARTS):
        length, row = PART, []
        for s in range(3):
            length //= sizes[order[p][s]]
            row.append(length)
        lengths.append(row)
    landing = (r1, r2, r3)
    base = [jnp.int32(p * PART) for p in range(PARTS)]
    starts = [[None] * 3 for _ in range(PARTS)]

    def scatter(p, s):
        axis, length = order[p][s], lengths[p][s]
        copies = []
        for r in range(1, sizes[axis]):
            q, target = peer(axis, r)
            rows = pl.ds(pl.multiple_of(base[p] + q * length, 8), length)
            copies.append(send(acc.at[rows], landing[s].at[p, r - 1], target))
        base[p] = base[p] + coord[axis] * length
        starts[p][s] = base[p]
        return copies

    flying = [None] * PARTS
    for p in range(PARTS):
        local[p].wait()
        first[p].wait_recv()
        rows = pl.ds(p * PART, PART)
        acc[rows, :] = acc[rows, :] + other[rows, :]
        flying[p] = scatter(p, 0)
    m_core_copy.wait_recv()

    def misc_stage(axis, value):
        m_axes[axis, coord[axis]] = value
        return [
            send(m_axes.at[axis, coord[axis]], m_axes.at[axis, coord[axis]], peer(axis, r)[1])
            for r in range(1, sizes[axis])
        ]

    def misc_total(axis, copies):
        for copy in copies:
            copy.wait_recv()
        total = m_axes[axis, 0]
        for i in range(1, sizes[axis]):
            total = total + m_axes[axis, i]
        return total

    misc_copies = misc_stage(0, misc_ref[...] + m_core[...])
    for s in range(3):
        for p in range(PARTS):
            for copy in flying[p]:
                copy.wait_recv()
            rows = pl.ds(pl.multiple_of(base[p], 8), lengths[p][s])
            total = acc[rows, :]
            for r in range(sizes[order[p][s]] - 1):
                total = total + landing[s][p, r]
            if s < 2:
                acc[rows, :] = total
                flying[p] = scatter(p, s + 1)
            else:
                final = pl.ds(pl.multiple_of(mine + base[p], 8), lengths[p][s])
                res[final, :] = total
                flying[p] = gather(p, 2, sizes, order, lengths, starts, mine, peer, send, res)
        misc_value = misc_total(s, misc_copies)
        if s < 2:
            misc_copies = misc_stage(s + 1, misc_value)
    misc_out[...] = misc_value
    for s in (1, 0):
        for p in range(PARTS):
            for copy in flying[p]:
                copy.wait_recv()
            flying[p] = gather(p, s, sizes, order, lengths, starts, mine, peer, send, res)
    last = []
    for p in range(PARTS):
        for copy in flying[p]:
            copy.wait_recv()
        rows = pl.ds(pl.multiple_of(mine + p * PART, 8), PART)
        last.append(send(res.at[rows], res.at[rows], sibling))
    for copy in last:
        copy.wait_recv()
    for copy in started:
        copy.wait_send()


def gather(p, s, sizes, order, lengths, starts, mine, peer, send, res):
    axis = order[p][s]
    rows = pl.ds(pl.multiple_of(mine + starts[p][s], 8), lengths[p][s])
    return [send(res.at[rows], res.at[rows], peer(axis, r)[1]) for r in range(1, sizes[axis])]


def all_reduce(packed, misc, sizes):
    vmem = pl.BlockSpec(memory_space=pltpu.VMEM)
    most = max(sizes) - 1
    per_axis = sum(n - 1 for n in sizes)
    copies = 1 + PARTS + per_axis * (2 * PARTS + 1) + PARTS
    shapes = []
    for s in range(3):
        longest = 0
        for p in range(PARTS):
            length = PART
            for i in range(s + 1):
                length //= sizes[(p + i) % 3]
            longest = max(longest, length)
        shapes.append(longest)
    return pl.pallas_call(
        functools.partial(reduce_kernel, sizes),
        out_shape=[jax.ShapeDtypeStruct((ROWS, C), F32), jax.ShapeDtypeStruct((8, C), F32)],
        in_specs=[pl.BlockSpec(memory_space=pl.ANY), vmem],
        out_specs=[vmem, vmem],
        scratch_shapes=[
            pltpu.VMEM((HALF, C), F32),
            pltpu.VMEM((HALF, C), F32),
            pltpu.VMEM((PARTS, most, shapes[0], C), F32),
            pltpu.VMEM((PARTS, most, shapes[1], C), F32),
            pltpu.VMEM((PARTS, most, shapes[2], C), F32),
            pltpu.VMEM((8, C), F32),
            pltpu.VMEM((3, max(sizes), 8, C), F32),
            pltpu.SemaphoreType.DMA((PARTS,)),
            pltpu.SemaphoreType.DMA((copies,)),
            pltpu.SemaphoreType.DMA((copies,)),
        ],
        compiler_params=pltpu.CompilerParams(
            collective_id=0, has_side_effects=True, vmem_limit_bytes=32 * 1024 * 1024
        ),
    )(packed, misc)


def finish_kernel(packed, misc, gt, gain, gin, gout, gdown, gup, own):
    def block(start, height, j):
        return packed[pl.ds(start + j * height, height), :]

    for j in range(2):
        cols = pl.ds(j * C, C)
        gt[:, cols] = block(ROW_TIME, EMB, j)
        gin[:, cols] = block(ROW_IN, C, j)
        gout[cols, :] = block(ROW_OUT, C, j).T
    for j in range(4):
        cols = pl.ds(j * C, C)
        gdown[cols, :] = block(ROW_DOWN, 256, j).T
        gup[:, cols] = block(ROW_UP, 256, j)
    gain[...] = misc[pl.ds(0, 1), :]
    me = lax.axis_index("dp") * lax.axis_size("rep") + lax.axis_index("rep")
    lane = lax.broadcasted_iota(jnp.int32, (1, C), 1)
    own[0] = jnp.sum(jnp.where(lane == me, misc[pl.ds(1, 1), :], 0.0))


def finish(packed, misc):
    vmem = pl.BlockSpec(memory_space=pltpu.VMEM)
    shapes = [(EMB, 2 * C), (1, C), (C, HID), (HID, C), (512, 256), (256, 512), (1,)]
    return pl.pallas_call(
        finish_kernel,
        out_shape=[jax.ShapeDtypeStruct(s, F32) for s in shapes],
        in_specs=[vmem, vmem],
        out_specs=[vmem] * 6 + [pl.BlockSpec(memory_space=pltpu.SMEM)],
        compiler_params=pltpu.CompilerParams(vmem_limit_bytes=32 * 1024 * 1024),
    )(packed, misc)


def body(sizes, clip_tiles, clip_size, clip_dest, timesteps, noise_seeds, w_time, gain, w_in, w_out, w_down, w_up):
    packed, misc = local_grads(
        clip_tiles, clip_size, clip_dest, timesteps, noise_seeds,
        w_time, gain, w_in, w_out, w_down, w_up,
    )
    packed, misc = all_reduce(packed, misc, sizes)
    gt, ggain, gin, gout, gdown, gup, own = finish(packed, misc)
    return (gt, ggain.reshape(C), gin, gout, gdown, gup, own)


def solution(mesh):
    rows = P(("dp", "rep"), None)
    in_specs = (P(("dp", "rep"), None, None), rows, rows, rows, rows) + (P(),) * 6
    out_specs = (P(),) * 6 + (P(("dp", "rep")),)
    sizes = (4, mesh.shape["dp"] // 8, mesh.shape["rep"])
    return jax.shard_map(functools.partial(body, sizes), mesh=mesh, in_specs=in_specs, out_specs=out_specs, check_vma=False)
```

```python
import functools
import math

import jax
import jax.numpy as jnp
import numpy as np
from jax import lax
from jax.experimental import pallas as pl
from jax.experimental.pallas import tpu as pltpu
from jax.sharding import PartitionSpec as P

EMB = 256
TR = 8
TC = 32
TSTEPS = 1000
C = 128
PIX = 256
HID = 256
SPAN = 8
RUN = 4
CLIPS = 64
MUL_POS = 1103515245
MUL_SEED = 747796405
ADD_POS = 1013904223
MUL_MIX = 73244475
ROOT3 = 1.7320508
NOISE_A = float(np.float32(2.0 * ROOT3 / 16777216.0))
NOISE_B = float(np.float32(ROOT3 * (1.0 / 16777216.0 - 1.0)))
CHUNK, SKEW = 8, 1
F32 = jnp.float32
BF16 = jnp.bfloat16
ROW_TIME, ROW_IN, ROW_OUT, ROW_DOWN, ROW_UP, ROWS = 0, 512, 768, 1024, 2048, 3072
PARTS = 3
HALF = ROWS // 2
PART = HALF // PARTS


def wrap32(value):
    value &= 0xFFFFFFFF
    return value - (1 << 32) if value >= (1 << 31) else value


def dot(a, b):
    return lax.dot_general(a, b, (((1,), (0,)), ((), ())), preferred_element_type=F32)


def dot_bt(a, b):
    return lax.dot_general(a, b, (((1,), (1,)), ((), ())), preferred_element_type=F32)


def dot_at(a, b):
    return lax.dot_general(a, b, (((0,), (0,)), ((), ())), preferred_element_type=F32)


def shift_right(value, amount):
    return lax.shift_right_logical(value, jnp.int32(amount))


def group_sum(x, lane):
    pair = x + jnp.where(lane % 2 == 0, pltpu.roll(x, 127, 1), pltpu.roll(x, 1, 1))
    return pair + jnp.where(lane % 4 < 2, pltpu.roll(pair, 126, 1), pltpu.roll(pair, 2, 1))


def add_blocks(pack_ref, start, value):
    height = value.shape[0]
    for j in range(value.shape[1] // C):
        pack_ref[pl.ds(start + j * height, height), :] += value[:, j * C:(j + 1) * C]


def span_kernel(
    sizes_ref, seeds_ref, tiles_hbm, sizes_row, dest_row, time_row, freq_ref, wt_ref, gain_ref,
    win_ref, wout_ref, wdown_ref, wup_ref,
    pack_ref, misc_ref,
    buf, sem, itab, perm, emb_s, film_scale, film_shift, sa_s, sb_s, weight_s, inv_s,
    noise, noisy, x_s, hid, slope, resid, patch,
    dact, dslope, glift, gpd_s, gres, gph_s, s1_s, s2_s, loss_s, stat,
    win_h, wout_h, wdown_h, wup_h,
):
    total = sizes_ref[0, 0]
    for entry in range(1, CLIPS):
        total += sizes_ref[0, entry]
    count = total // SPAN

    def fetch(span, slot):
        return pltpu.make_async_copy(
            tiles_hbm.at[pl.ds(span * SPAN, SPAN)], buf.at[slot], sem.at[slot]
        )

    @pl.when(count > 0)
    def _():
        fetch(0, 0).start()

    row = lax.broadcasted_iota(jnp.int32, (PIX, C), 0)
    lane = lax.broadcasted_iota(jnp.int32, (PIX, C), 1)
    quad, rest = row // 64, row % 64
    pixel = (2 * (rest // 16) + quad // 2) * TC + 2 * (rest % 16) + quad % 2
    itab[...] = (pixel * C + lane) * jnp.int32(MUL_POS)
    prow = lax.broadcasted_iota(jnp.int32, (PIX, PIX), 0)
    pcol = lax.broadcasted_iota(jnp.int32, (PIX, PIX), 1)
    pquad, prest = prow // 64, prow % 64
    ppix = (2 * (prest // 16) + pquad // 2) * TC + 2 * (prest % 16) + pquad % 2
    perm[...] = jnp.where(ppix == pcol, 1.0, 0.0).astype(BF16)
    eye = lax.broadcasted_iota(jnp.int32, (CLIPS, CLIPS), 0) == lax.broadcasted_iota(
        jnp.int32, (CLIPS, CLIPS), 1
    )

    def column(values):
        picked = jnp.sum(jnp.where(eye, values, 0.0), axis=1, keepdims=True)
        return jnp.broadcast_to(picked, (CLIPS, C))

    step = time_row[...].astype(F32)
    alpha_bar = jnp.cos(((step + 1.0) / TSTEPS + 0.008) / 1.008 * (math.pi / 2.0)) ** 2
    sa_s[...] = column(jnp.sqrt(alpha_bar))
    sb_s[...] = column(jnp.sqrt(1.0 - alpha_bar))
    inv_len = 1.0 / column(jnp.maximum(sizes_row[...], 1).astype(F32))
    inv_s[...] = inv_len * (1.0 / (PIX * 4))
    weight_s[...] = inv_len * (2.0 / (PIX * C))
    angle = column(step) * freq_ref[...]
    emb_s[:, :C] = jnp.cos(angle).astype(BF16)
    emb_s[:, C:] = jnp.sin(angle).astype(BF16)
    modulation = dot(emb_s[...], wt_ref[...])
    film_scale[...] = modulation[:, :C]
    film_shift[...] = modulation[:, C:]
    win_h[...] = win_ref[...] * jnp.asarray(0.5, BF16)
    wdown_h[...] = wdown_ref[...] * jnp.asarray(0.5, BF16)
    wout_h[...] = wout_ref[...] * jnp.asarray(0.5, BF16)
    wup_h[...] = wup_ref[...] * jnp.asarray(0.5, BF16)
    for ref in (pack_ref, s1_s, s2_s, loss_s):
        ref[...] = jnp.zeros_like(ref)
    lane8 = lax.broadcasted_iota(jnp.int32, (SPAN, C), 1)

    def marks(span):
        one = sizes_ref[0, span * RUN]
        two = one + sizes_ref[0, span * RUN + 1]
        return one, two, two + sizes_ref[0, span * RUN + 2]

    def owner_of(tile, bounds):
        return sum((tile >= bound).astype(jnp.int32) for bound in bounds)

    def make_noisy(span, slot):
        bounds = marks(span)
        owners = [owner_of(jnp.int32(k), bounds) for k in range(SPAN)]
        for k in range(SPAN):
            if k % 2 == 0:
                pair = dot(
                    perm[...], jnp.concatenate([buf[slot, k], buf[slot, k + 1]], axis=1)
                )
            entry = span * RUN + owners[k]
            row = pl.ds(entry, 1)
            start = jnp.int32(0)
            for bound in bounds:
                start = jnp.where(k >= bound, bound, start)
            mix = (
                (k - start) * jnp.int32(wrap32(PIX * C * MUL_POS))
                + seeds_ref[0, entry] * jnp.int32(MUL_SEED) + jnp.int32(ADD_POS)
            )
            stat[4, pl.ds(k, 1), :] = inv_s[row, :]
            stat[5, pl.ds(k, 1), :] = film_scale[row, :]
            stat[6, pl.ds(k, 1), :] = film_shift[row, :]
            mixed = itab[...] + mix
            mixed = mixed ^ shift_right(mixed, 16)
            mixed = mixed * jnp.int32(MUL_MIX)
            mixed = mixed ^ shift_right(mixed, 16)
            mixed = mixed * jnp.int32(MUL_MIX)
            mixed = mixed ^ shift_right(mixed, 16)
            field = shift_right(mixed, 8).astype(F32) * NOISE_A + NOISE_B
            noise[k] = field
            pixels = pair[:, (k % 2) * C:(k % 2 + 1) * C]
            value = sa_s[row, :] * pixels + sb_s[row, :] * field
            noisy[k] = value
            stat[0, pl.ds(k, 1), :] = jnp.sum(value, axis=0, keepdims=True)
            stat[1, pl.ds(k, 1), :] = jnp.sum(value * value, axis=0, keepdims=True)

        tile8 = lax.broadcasted_iota(jnp.int32, (SPAN, C), 0)
        seg = owner_of(tile8, bounds)
        inv_count = stat[4]
        first = jnp.zeros((SPAN, C), F32)
        square = jnp.zeros((SPAN, C), F32)
        for k in range(SPAN):
            member = seg == owners[k]
            first += jnp.where(member, stat[0, pl.ds(k, 1), :], 0.0)
            square += jnp.where(member, stat[1, pl.ds(k, 1), :], 0.0)
        mean = group_sum(first, lane8) * inv_count
        var = group_sum(square, lane8) * inv_count - mean * mean
        spread = lax.rsqrt(var + 1e-05)
        factor = spread * gain_ref[...] * (1.0 + stat[5])
        shift = stat[6]
        stat[0] = mean
        stat[1] = factor
        stat[2] = shift
        stat[3] = spread

    @pl.when(count > 0)
    def _():
        @pl.when(count > 1)
        def _():
            fetch(1, 1).start()

        fetch(0, 0).wait()
        make_noisy(0, 0)

    @pl.loop(0, count)
    def _(span):
        bounds = marks(span)
        entries = [span * RUN + owner_of(jnp.int32(k), bounds) for k in range(SPAN)]
        following = jnp.minimum(span + 1, count - 1)
        slot = lax.rem(span + 1, 2)

        @pl.when(span + 1 < count)
        def _():
            fetch(span + 1, slot).wait()

        @pl.when(span + 2 < count)
        def _():
            fetch(span + 2, 1 - slot).start()

        def chunk_steps(k0):
            tiles = range(k0, k0 + CHUNK)
            rows = pl.ds(k0 * PIX, CHUNK * PIX)
            quads = pl.ds(k0 * 64, CHUNK * 64)
            held = {}

            def normalise():
                for k in tiles:
                    one = pl.ds(k, 1)
                    centre = noisy[k] - stat[0, one, :]
                    x_s[pl.ds(k * PIX, PIX), :] = (
                        centre * stat[1, one, :] + stat[2, one, :]
                    ).astype(BF16)

            def project():
                held["half"] = dot(x_s[rows, :], win_h[...])

            def activate():
                half = held["half"]
                th = jnp.tanh(half)
                q = 1.0 + th
                h = half * q
                slope[rows, :] = q + h * (1.0 - th)
                hid[rows, :] = h.astype(BF16)

            def project_back():
                held["out"] = dot(hid[rows, :], wout_ref[...])

            def residual():
                for k in tiles:
                    at = (k - k0) * PIX
                    out = held["out"][at:at + PIX] + noisy[k]
                    resid[k] = out
                    outb = out.astype(BF16)
                    for j in range(4):
                        patch[pl.ds(k * 64, 64), pl.ds(j * C, C)] = outb[j * 64:(j + 1) * 64]

            def down():
                held["half"] = dot(patch[quads, :], wdown_h[...])

            def down_activate():
                half = held["half"]
                th = jnp.tanh(half)
                q = 1.0 + th
                h = half * q
                dslope[quads, :] = q + h * (1.0 - th)
                dact[quads, :] = h.astype(BF16)

            def up():
                held["lifted"] = dot(dact[quads, :], wup_ref[...])

            def error():
                for k in tiles:
                    at = (k - k0) * 64
                    row = pl.ds(entries[k], 1)
                    weight = weight_s[row, :]
                    total = jnp.zeros((64, C), F32)
                    for j in range(4):
                        part = pl.ds(j * 64, 64)
                        err = (
                            resid[k, part, :]
                            + held["lifted"][at:at + 64, j * C:(j + 1) * C]
                            - noise[k, part, :]
                        )
                        total += err * err
                        gp = err * weight
                        resid[k, part, :] = gp
                        glift[pl.ds(k * 64, 64), pl.ds(j * C, C)] = gp.astype(BF16)
                    loss_s[row, :] += jnp.sum(total, axis=0, keepdims=True)

            def up_back():
                held["gda"] = dot_bt(glift[quads, :], wup_h[...])

            def down_slope():
                gpd_s[quads, :] = (held["gda"] * dslope[quads, :]).astype(BF16)

            def down_back():
                held["back"] = dot_bt(gpd_s[quads, :], wdown_ref[...])

            def grad_residual():
                for k in tiles:
                    at = (k - k0) * 64
                    for j in range(4):
                        part = pl.ds(j * 64, 64)
                        gres[pl.ds(k * PIX + j * 64, 64), :] = (
                            resid[k, part, :] + held["back"][at:at + 64, j * C:(j + 1) * C]
                        ).astype(BF16)

            def out_back():
                held["gh"] = dot_bt(gres[rows, :], wout_h[...])

            def hidden_slope():
                gph_s[rows, :] = (held["gh"] * slope[rows, :]).astype(BF16)

            def in_back():
                held["gn"] = dot_bt(gph_s[rows, :], win_ref[...])

            def tile_sums():
                for k in tiles:
                    at = (k - k0) * PIX
                    one = pl.ds(k, 1)
                    centre = noisy[k] - stat[0, one, :]
                    mine = held["gn"][at:at + PIX]
                    row = pl.ds(entries[k], 1)
                    s1_s[row, :] += jnp.sum(mine, axis=0, keepdims=True)
                    s2_s[row, :] += (
                        jnp.sum(mine * centre, axis=0, keepdims=True) * stat[3, one, :]
                    )

            return [
                normalise, project, activate, project_back, residual, down, down_activate, up,
                error, up_back, down_slope, down_back, grad_residual, out_back, hidden_slope,
                in_back, tile_sums,
            ]

        chunks = [chunk_steps(k0) for k0 in range(0, SPAN, CHUNK)]
        for turn in range(len(chunks[0]) + SKEW * (len(chunks) - 1)):
            for index, steps in enumerate(chunks):
                if 0 <= turn - SKEW * index < len(steps):
                    steps[turn - SKEW * index]()

        make_noisy(following, slot)
        add_blocks(pack_ref, ROW_UP, dot_at(dact[...], glift[...]))
        add_blocks(pack_ref, ROW_DOWN, dot_at(gpd_s[...], patch[...]))
        add_blocks(
            pack_ref, ROW_OUT, dot_at(gres[...], hid[...])
        )
        add_blocks(
            pack_ref, ROW_IN, dot_at(x_s[...], gph_s[...])
        )

    scale1 = 1.0 + film_scale[...]
    s2 = s2_s[...]
    misc_ref[...] = jnp.zeros_like(misc_ref)
    misc_ref[pl.ds(0, 1), :] = jnp.sum(s2 * scale1, axis=0, keepdims=True)
    clip_loss = jnp.sum(loss_s[...], axis=1, keepdims=True) * weight_s[...] * 0.5
    place = column((dest_row[...] * lax.axis_size("rep") + lax.axis_index("rep")).astype(F32))
    hits = place == lax.broadcasted_iota(jnp.int32, (CLIPS, C), 1).astype(F32)
    misc_ref[pl.ds(1, 1), :] = jnp.sum(jnp.where(hits, clip_loss, 0.0), axis=0, keepdims=True)
    emb = emb_s[...].astype(F32)
    for ref, part in ((s2 * gain_ref[...], 0), (s1_s[...], 1)):
        pack_ref[pl.ds(ROW_TIME + part * EMB, EMB), :] = lax.dot_general(
            emb, ref, (((0,), (0,)), ((), ())),
            precision=lax.Precision.HIGHEST, preferred_element_type=F32,
        )


def local_grads(clip_tiles, sizes, dests, times, seeds, w_time, gain, w_in, w_out, w_down, w_up):
    smem = pl.BlockSpec(memory_space=pltpu.SMEM)
    vmem = pl.BlockSpec(memory_space=pltpu.VMEM)
    half = EMB // 2
    freq = np.exp(-math.log(10000.0) * np.arange(half) / half).astype(np.float32)
    return pl.pallas_call(
        span_kernel,
        out_shape=[jax.ShapeDtypeStruct(s, F32) for s in [(ROWS, C), (8, C)]],
        in_specs=[smem] * 2 + [pl.BlockSpec(memory_space=pl.ANY)] + [vmem] * 10,
        out_specs=[vmem] * 2,
        scratch_shapes=[
            pltpu.VMEM((2, SPAN, PIX, C), BF16),
            pltpu.SemaphoreType.DMA((2,)),
            pltpu.VMEM((PIX, C), jnp.int32),
            pltpu.VMEM((PIX, PIX), BF16),
            pltpu.VMEM((CLIPS, EMB), BF16),
            pltpu.VMEM((CLIPS, C), F32),
            pltpu.VMEM((CLIPS, C), F32),
            pltpu.VMEM((CLIPS, C), F32),
            pltpu.VMEM((CLIPS, C), F32),
            pltpu.VMEM((CLIPS, C), F32),
            pltpu.VMEM((CLIPS, C), F32),
            pltpu.VMEM((SPAN, PIX, C), F32),
            pltpu.VMEM((SPAN, PIX, C), F32),
            pltpu.VMEM((SPAN * PIX, C), BF16),
            pltpu.VMEM((SPAN * PIX, HID), BF16),
            pltpu.VMEM((SPAN * PIX, HID), F32),
            pltpu.VMEM((SPAN, PIX, C), F32),
            pltpu.VMEM((512, 512), BF16),
            pltpu.VMEM((512, 256), BF16),
            pltpu.VMEM((512, 256), F32),
            pltpu.VMEM((512, 512), BF16),
            pltpu.VMEM((512, 256), BF16),
            pltpu.VMEM((SPAN * PIX, C), BF16),
            pltpu.VMEM((SPAN * PIX, HID), BF16),
            pltpu.VMEM((CLIPS, C), F32),
            pltpu.VMEM((CLIPS, C), F32),
            pltpu.VMEM((CLIPS, C), F32),
            pltpu.VMEM((7, SPAN, C), F32),
            pltpu.VMEM((C, HID), BF16),
            pltpu.VMEM((HID, C), BF16),
            pltpu.VMEM((512, 256), BF16),
            pltpu.VMEM((256, 512), BF16),
        ],
        compiler_params=pltpu.CompilerParams(vmem_limit_bytes=50 * 1024 * 1024),
    )(sizes, seeds, clip_tiles, sizes, dests, times, freq.reshape(1, half), w_time,
      gain.reshape(1, C), w_in, w_out, w_down, w_up)


def reduce_kernel(
    sizes, x_hbm, misc_ref, res, misc_out,
    acc, other, r1, r2, r3, m_core, m_axes, local_sem, send_sem, recv_sem,
):
    dp, z = lax.axis_index("dp"), lax.axis_index("rep")
    ny = sizes[1]
    core = lax.rem(dp, 2)
    chip = lax.div(dp, 2)
    coord = (lax.div(chip, ny), lax.rem(chip, ny), z)

    def device(x, y, zz, c):
        return ((x * ny + y) * 2 + c, zz)

    def peer(axis, r):
        other_coord = lax.rem(coord[axis] + r, sizes[axis])
        place = list(coord)
        place[axis] = other_coord
        return other_coord, device(*place, core)

    sibling = device(*coord, 1 - core)
    peers = [(axis, r) for axis in range(3) for r in range(1, sizes[axis])]
    barrier = pltpu.get_barrier_semaphore()
    for target in [sibling] + [peer(axis, r)[1] for axis, r in peers]:
        pl.semaphore_signal(barrier, inc=1, device_id=target, device_id_type=pl.DeviceIdType.MESH)

    mine = core * HALF
    theirs = (1 - core) * HALF
    local = []
    for p in range(PARTS):
        copy = pltpu.make_async_copy(
            x_hbm.at[pl.ds(pl.multiple_of(mine + p * PART, 8), PART)],
            acc.at[pl.ds(p * PART, PART)], local_sem.at[p],
        )
        copy.start()
        local.append(copy)
    pl.semaphore_wait(barrier, 1 + len(peers))

    started = []

    def send(src, dst, target):
        index = len(started)
        copy = pltpu.make_async_remote_copy(
            src_ref=src, dst_ref=dst, send_sem=send_sem.at[index], recv_sem=recv_sem.at[index],
            device_id=target, device_id_type=pl.DeviceIdType.MESH,
        )
        copy.start()
        started.append(copy)
        return copy

    m_core_copy = send(misc_ref, m_core, sibling)
    first = [
        send(
            x_hbm.at[pl.ds(pl.multiple_of(theirs + p * PART, 8), PART)],
            other.at[pl.ds(p * PART, PART)], sibling,
        )
        for p in range(PARTS)
    ]

    order = [[(p + s) % 3 for s in range(3)] for p in range(PARTS)]
    lengths = []
    for p in range(PARTS):
        length, row = PART, []
        for s in range(3):
            length //= sizes[order[p][s]]
            row.append(length)
        lengths.append(row)
    landing = (r1, r2)
    base = [jnp.int32(p * PART) for p in range(PARTS)]
    starts = [[None] * 3 for _ in range(PARTS)]

    def scatter(p, s):
        axis, length = order[p][s], lengths[p][s]
        copies = []
        for r in range(1, sizes[axis]):
            q, target = peer(axis, r)
            rows = pl.ds(pl.multiple_of(base[p] + q * length, 8), length)
            copies.append(send(acc.at[rows], landing[s].at[p, r - 1], target))
        base[p] = base[p] + coord[axis] * length
        starts[p][s] = base[p]
        return copies

    flying = [None] * PARTS
    for p in range(PARTS):
        local[p].wait()
        first[p].wait_recv()
        rows = pl.ds(p * PART, PART)
        acc[rows, :] = acc[rows, :] + other[rows, :]
        flying[p] = scatter(p, 0)
    m_core_copy.wait_recv()

    def exchange(slots, axis, value):
        slots[coord[axis]] = value
        return [
            send(slots.at[coord[axis]], slots.at[coord[axis]], peer(axis, r)[1])
            for r in range(1, sizes[axis])
        ]

    def total_of(slots, axis, copies):
        for copy in copies:
            copy.wait_recv()
        total = slots[0]
        for i in range(1, sizes[axis]):
            total = total + slots[i]
        return total

    misc_copies = exchange(m_axes.at[0], 0, misc_ref[...] + m_core[...])
    for s in range(2):
        for p in range(PARTS):
            for copy in flying[p]:
                copy.wait_recv()
            rows = pl.ds(pl.multiple_of(base[p], 8), lengths[p][s])
            total = acc[rows, :]
            for r in range(sizes[order[p][s]] - 1):
                total = total + landing[s][p, r]
            if s == 0:
                acc[rows, :] = total
                flying[p] = scatter(p, 1)
            else:
                flying[p] = exchange(r3.at[p, :, pl.ds(0, lengths[p][1])], order[p][2], total)
        misc_copies = exchange(
            m_axes.at[s + 1], s + 1, total_of(m_axes.at[s], s, misc_copies)
        )
    for p in range(PARTS):
        total = total_of(r3.at[p, :, pl.ds(0, lengths[p][1])], order[p][2], flying[p])
        res[pl.ds(pl.multiple_of(mine + base[p], 8), lengths[p][1]), :] = total
        flying[p] = gather(p, 1, sizes, order, lengths, starts, mine, peer, send, res)
    misc_out[...] = total_of(m_axes.at[2], 2, misc_copies)
    last = []

    def forward(p, q):
        rows = pl.ds(pl.multiple_of(mine + p * PART + q * lengths[p][0], 8), lengths[p][0])
        last.append(send(res.at[rows], res.at[rows], sibling))

    for p in range(PARTS):
        for copy in flying[p]:
            copy.wait_recv()
        flying[p] = gather(p, 0, sizes, order, lengths, starts, mine, peer, send, res)
        forward(p, coord[order[p][0]])
    longest = max(sizes)
    for r in [i for i in range(1, longest) if i != 2] + [2]:
        for p in range(PARTS):
            axis = order[p][0]
            if r < sizes[axis]:
                flying[p][r - 1].wait_recv()
                forward(p, lax.rem(coord[axis] + sizes[axis] - r, sizes[axis]))
    for copy in last:
        copy.wait_recv()
    for copy in started:
        copy.wait_send()


def gather(p, s, sizes, order, lengths, starts, mine, peer, send, res):
    axis = order[p][s]
    rows = pl.ds(pl.multiple_of(mine + starts[p][s], 8), lengths[p][s])
    return [send(res.at[rows], res.at[rows], peer(axis, r)[1]) for r in range(1, sizes[axis])]


def all_reduce(packed, misc, sizes):
    vmem = pl.BlockSpec(memory_space=pltpu.VMEM)
    most = max(sizes) - 1
    per_axis = sum(n - 1 for n in sizes)
    copies = 1 + PARTS + per_axis * (5 * PARTS // 3 + 1) + sum(sizes)
    shapes = []
    for s in range(2):
        longest = 0
        for p in range(PARTS):
            length = PART
            for i in range(s + 1):
                length //= sizes[(p + i) % 3]
            longest = max(longest, length)
        shapes.append(longest)
    return pl.pallas_call(
        functools.partial(reduce_kernel, sizes),
        out_shape=[jax.ShapeDtypeStruct((ROWS, C), F32), jax.ShapeDtypeStruct((8, C), F32)],
        in_specs=[pl.BlockSpec(memory_space=pl.ANY), vmem],
        out_specs=[vmem, vmem],
        scratch_shapes=[
            pltpu.VMEM((HALF, C), F32),
            pltpu.VMEM((HALF, C), F32),
            pltpu.VMEM((PARTS, most, shapes[0], C), F32),
            pltpu.VMEM((PARTS, most, shapes[1], C), F32),
            pltpu.VMEM((PARTS, max(sizes), shapes[1], C), F32),
            pltpu.VMEM((8, C), F32),
            pltpu.VMEM((3, max(sizes), 8, C), F32),
            pltpu.SemaphoreType.DMA((PARTS,)),
            pltpu.SemaphoreType.DMA((copies,)),
            pltpu.SemaphoreType.DMA((copies,)),
        ],
        compiler_params=pltpu.CompilerParams(
            collective_id=0, has_side_effects=True, vmem_limit_bytes=16 * 1024 * 1024
        ),
    )(packed, misc)


def finish_kernel(packed, misc, gt, gain, gin, gout, gdown, gup, own):
    def block(start, height, j):
        return packed[pl.ds(start + j * height, height), :]

    for j in range(2):
        cols = pl.ds(j * C, C)
        gt[:, cols] = block(ROW_TIME, EMB, j)
        gin[:, cols] = block(ROW_IN, C, j)
        gout[cols, :] = block(ROW_OUT, C, j).T
    for j in range(4):
        cols = pl.ds(j * C, C)
        gdown[cols, :] = block(ROW_DOWN, 256, j).T
        gup[:, cols] = block(ROW_UP, 256, j)
    gain[...] = misc[pl.ds(0, 1), :]
    me = lax.axis_index("dp") * lax.axis_size("rep") + lax.axis_index("rep")
    lane = lax.broadcasted_iota(jnp.int32, (1, C), 1)
    own[0] = jnp.sum(jnp.where(lane == me, misc[pl.ds(1, 1), :], 0.0))


def finish(packed, misc):
    vmem = pl.BlockSpec(memory_space=pltpu.VMEM)
    shapes = [(EMB, 2 * C), (1, C), (C, HID), (HID, C), (512, 256), (256, 512), (1,)]
    return pl.pallas_call(
        finish_kernel,
        out_shape=[jax.ShapeDtypeStruct(s, F32) for s in shapes],
        in_specs=[vmem, vmem],
        out_specs=[vmem] * 6 + [pl.BlockSpec(memory_space=pltpu.SMEM)],
        compiler_params=pltpu.CompilerParams(vmem_limit_bytes=32 * 1024 * 1024),
    )(packed, misc)


def body(sizes, clip_tiles, clip_size, clip_dest, timesteps, noise_seeds, w_time, gain, w_in, w_out, w_down, w_up):
    packed, misc = local_grads(
        clip_tiles, clip_size, clip_dest, timesteps, noise_seeds,
        w_time, gain, w_in, w_out, w_down, w_up,
    )
    packed, misc = all_reduce(packed, misc, sizes)
    gt, ggain, gin, gout, gdown, gup, own = finish(packed, misc)
    return (gt, ggain.reshape(C), gin, gout, gdown, gup, own)


def solution(mesh):
    rows = P(("dp", "rep"), None)
    in_specs = (P(("dp", "rep"), None, None), rows, rows, rows, rows) + (P(),) * 6
    out_specs = (P(),) * 6 + (P(("dp", "rep")),)
    sizes = (4, mesh.shape["dp"] // 8, mesh.shape["rep"])
    return jax.shard_map(functools.partial(body, sizes), mesh=mesh, in_specs=in_specs, out_specs=out_specs, check_vma=False)
```

```python
import functools
import math

import jax
import jax.numpy as jnp
import numpy as np
from jax import lax
from jax.experimental import pallas as pl
from jax.experimental.pallas import tpu as pltpu
from jax.sharding import PartitionSpec as P

EMB = 256
TR = 8
TC = 32
TSTEPS = 1000
C = 128
PIX = 256
HID = 256
SPAN = 8
RUN = 4
CLIPS = 64
MUL_POS = 1103515245
MUL_SEED = 747796405
ADD_POS = 1013904223
MUL_MIX = 73244475
ROOT3 = 1.7320508
NOISE_A = float(np.float32(2.0 * ROOT3 / 16777216.0))
NOISE_B = float(np.float32(ROOT3 * (1.0 / 16777216.0 - 1.0)))
CHUNK, SKEW = 8, 1
F32 = jnp.float32
BF16 = jnp.bfloat16
ROW_TIME, ROW_IN, ROW_OUT, ROW_DOWN, ROW_UP, ROWS = 0, 512, 768, 1024, 2048, 3072
PARTS = 3
HALF = ROWS // 2
PART = HALF // PARTS


def wrap32(value):
    value &= 0xFFFFFFFF
    return value - (1 << 32) if value >= (1 << 31) else value


def dot(a, b):
    return lax.dot_general(a, b, (((1,), (0,)), ((), ())), preferred_element_type=F32)


def dot_bt(a, b):
    return lax.dot_general(a, b, (((1,), (1,)), ((), ())), preferred_element_type=F32)


def dot_at(a, b):
    return lax.dot_general(a, b, (((0,), (0,)), ((), ())), preferred_element_type=F32)


def shift_right(value, amount):
    return lax.shift_right_logical(value, jnp.int32(amount))


def group_sum(x, lane):
    pair = x + jnp.where(lane % 2 == 0, pltpu.roll(x, 127, 1), pltpu.roll(x, 1, 1))
    return pair + jnp.where(lane % 4 < 2, pltpu.roll(pair, 126, 1), pltpu.roll(pair, 2, 1))


def add_blocks(pack_ref, start, value):
    height = value.shape[0]
    for j in range(value.shape[1] // C):
        pack_ref[pl.ds(start + j * height, height), :] += value[:, j * C:(j + 1) * C]


def span_kernel(
    tiles_hbm, sizes_hbm, seeds_hbm, dest_hbm, time_hbm, freq_hbm, wt_hbm, gain_hbm,
    win_hbm, wout_hbm, wdown_hbm, wup_hbm,
    pack_ref,
    sizes_ref, seeds_ref, sizes_row, dest_row, time_row, freq_ref, wt_ref, gain_ref,
    win_ref, wout_ref, wdown_ref, wup_ref, input_sem,
    buf, sem, itab, perm, emb_s, film_scale, film_shift, sa_s, sb_s, weight_s, inv_s,
    noise, noisy, x_s, hid, slope, resid, patch,
    dact, dslope, glift, gpd_s, gres, gph_s, s1_s, s2_s, loss_s, stat,
    win_h, wout_h, wdown_h, wup_h,
):
    inputs = [
        pltpu.make_async_copy(source, target, input_sem.at[index])
        for index, (source, target) in enumerate((
            (sizes_hbm, sizes_ref), (seeds_hbm, seeds_ref), (sizes_hbm, sizes_row),
            (time_hbm, time_row), (freq_hbm, freq_ref), (wt_hbm, wt_ref), (gain_hbm, gain_ref),
            (win_hbm, win_ref), (wout_hbm, wout_ref), (wdown_hbm, wdown_ref),
            (wup_hbm, wup_ref), (dest_hbm, dest_row),
        ))
    ]
    for copy in inputs:
        copy.start()
    inputs[0].wait()
    total = sizes_ref[0, 0]
    for entry in range(1, CLIPS):
        total += sizes_ref[0, entry]
    count = total // SPAN

    def fetch(span, slot):
        return pltpu.make_async_copy(
            tiles_hbm.at[pl.ds(span * SPAN, SPAN)], buf.at[slot], sem.at[slot]
        )

    @pl.when(count > 0)
    def _():
        fetch(0, 0).start()

    row = lax.broadcasted_iota(jnp.int32, (PIX, C), 0)
    lane = lax.broadcasted_iota(jnp.int32, (PIX, C), 1)
    quad, rest = row // 64, row % 64
    pixel = (2 * (rest // 16) + quad // 2) * TC + 2 * (rest % 16) + quad % 2
    itab[...] = (pixel * C + lane) * jnp.int32(MUL_POS)
    prow = lax.broadcasted_iota(jnp.int32, (PIX, PIX), 0)
    pcol = lax.broadcasted_iota(jnp.int32, (PIX, PIX), 1)
    pquad, prest = prow // 64, prow % 64
    ppix = (2 * (prest // 16) + pquad // 2) * TC + 2 * (prest % 16) + pquad % 2
    perm[...] = jnp.where(ppix == pcol, 1.0, 0.0).astype(BF16)
    for ref in (pack_ref, s1_s, s2_s, loss_s):
        ref[...] = jnp.zeros_like(ref)
    lane8 = lax.broadcasted_iota(jnp.int32, (SPAN, C), 1)
    for copy in inputs[1:]:
        copy.wait()
    eye = lax.broadcasted_iota(jnp.int32, (CLIPS, CLIPS), 0) == lax.broadcasted_iota(
        jnp.int32, (CLIPS, CLIPS), 1
    )

    def column(values):
        picked = jnp.sum(jnp.where(eye, values, 0.0), axis=1, keepdims=True)
        return jnp.broadcast_to(picked, (CLIPS, C))

    step = time_row[...].astype(F32)
    alpha_bar = jnp.cos(((step + 1.0) / TSTEPS + 0.008) / 1.008 * (math.pi / 2.0)) ** 2
    sa_s[...] = column(jnp.sqrt(alpha_bar))
    sb_s[...] = column(jnp.sqrt(1.0 - alpha_bar))
    inv_len = 1.0 / column(jnp.maximum(sizes_row[...], 1).astype(F32))
    inv_s[...] = inv_len * (1.0 / (PIX * 4))
    weight_s[...] = inv_len * (2.0 / (PIX * C))
    angle = column(step) * freq_ref[...]
    emb_s[:, :C] = jnp.cos(angle).astype(BF16)
    emb_s[:, C:] = jnp.sin(angle).astype(BF16)
    modulation = dot(emb_s[...], wt_ref[...])
    film_scale[...] = modulation[:, :C]
    film_shift[...] = modulation[:, C:]
    win_h[...] = win_ref[...] * jnp.asarray(0.5, BF16)
    wdown_h[...] = wdown_ref[...] * jnp.asarray(0.5, BF16)
    wout_h[...] = wout_ref[...] * jnp.asarray(0.5, BF16)
    wup_h[...] = wup_ref[...] * jnp.asarray(0.5, BF16)

    def marks(span):
        one = sizes_ref[0, span * RUN]
        two = one + sizes_ref[0, span * RUN + 1]
        return one, two, two + sizes_ref[0, span * RUN + 2]

    def owner_of(tile, bounds):
        return sum((tile >= bound).astype(jnp.int32) for bound in bounds)

    def make_noisy(span, slot):
        bounds = marks(span)
        owners = [owner_of(jnp.int32(k), bounds) for k in range(SPAN)]
        for k in range(SPAN):
            if k % 2 == 0:
                pair = dot(
                    perm[...], jnp.concatenate([buf[slot, k], buf[slot, k + 1]], axis=1)
                )
            entry = span * RUN + owners[k]
            row = pl.ds(entry, 1)
            start = jnp.int32(0)
            for bound in bounds:
                start = jnp.where(k >= bound, bound, start)
            mix = (
                (k - start) * jnp.int32(wrap32(PIX * C * MUL_POS))
                + seeds_ref[0, entry] * jnp.int32(MUL_SEED) + jnp.int32(ADD_POS)
            )
            stat[4, pl.ds(k, 1), :] = inv_s[row, :]
            stat[5, pl.ds(k, 1), :] = film_scale[row, :]
            stat[6, pl.ds(k, 1), :] = film_shift[row, :]
            mixed = itab[...] + mix
            mixed = mixed ^ shift_right(mixed, 16)
            mixed = mixed * jnp.int32(MUL_MIX)
            mixed = mixed ^ shift_right(mixed, 16)
            mixed = mixed * jnp.int32(MUL_MIX)
            mixed = mixed ^ shift_right(mixed, 16)
            field = shift_right(mixed, 8).astype(F32) * NOISE_A + NOISE_B
            noise[k] = field
            pixels = pair[:, (k % 2) * C:(k % 2 + 1) * C]
            value = sa_s[row, :] * pixels + sb_s[row, :] * field
            noisy[k] = value
            stat[0, pl.ds(k, 1), :] = jnp.sum(value, axis=0, keepdims=True)
            stat[1, pl.ds(k, 1), :] = jnp.sum(value * value, axis=0, keepdims=True)

        tile8 = lax.broadcasted_iota(jnp.int32, (SPAN, C), 0)
        seg = owner_of(tile8, bounds)
        inv_count = stat[4]
        first = jnp.zeros((SPAN, C), F32)
        square = jnp.zeros((SPAN, C), F32)
        for k in range(SPAN):
            member = seg == owners[k]
            first += jnp.where(member, stat[0, pl.ds(k, 1), :], 0.0)
            square += jnp.where(member, stat[1, pl.ds(k, 1), :], 0.0)
        mean = group_sum(first, lane8) * inv_count
        var = group_sum(square, lane8) * inv_count - mean * mean
        spread = lax.rsqrt(var + 1e-05)
        factor = spread * gain_ref[...] * (1.0 + stat[5])
        shift = stat[6]
        stat[0] = mean
        stat[1] = factor
        stat[2] = shift
        stat[3] = spread

    @pl.when(count > 0)
    def _():
        @pl.when(count > 1)
        def _():
            fetch(1, 1).start()

        fetch(0, 0).wait()
        make_noisy(0, 0)

    @pl.loop(0, count)
    def _(span):
        bounds = marks(span)
        entries = [span * RUN + owner_of(jnp.int32(k), bounds) for k in range(SPAN)]
        following = jnp.minimum(span + 1, count - 1)
        slot = lax.rem(span + 1, 2)

        @pl.when(span + 1 < count)
        def _():
            fetch(span + 1, slot).wait()

        @pl.when(span + 2 < count)
        def _():
            fetch(span + 2, 1 - slot).start()

        def chunk_steps(k0):
            tiles = range(k0, k0 + CHUNK)
            rows = pl.ds(k0 * PIX, CHUNK * PIX)
            quads = pl.ds(k0 * 64, CHUNK * 64)
            held = {}

            def normalise():
                for k in tiles:
                    one = pl.ds(k, 1)
                    centre = noisy[k] - stat[0, one, :]
                    x_s[pl.ds(k * PIX, PIX), :] = (
                        centre * stat[1, one, :] + stat[2, one, :]
                    ).astype(BF16)

            def project():
                held["half"] = dot(x_s[rows, :], win_h[...])

            def activate():
                half = held["half"]
                th = jnp.tanh(half)
                q = 1.0 + th
                h = half * q
                slope[rows, :] = q + h * (1.0 - th)
                hid[rows, :] = h.astype(BF16)

            def project_back():
                held["out"] = dot(hid[rows, :], wout_ref[...])

            def residual():
                for k in tiles:
                    at = (k - k0) * PIX
                    out = held["out"][at:at + PIX] + noisy[k]
                    resid[k] = out
                    outb = out.astype(BF16)
                    for j in range(4):
                        patch[pl.ds(k * 64, 64), pl.ds(j * C, C)] = outb[j * 64:(j + 1) * 64]

            def down():
                held["half"] = dot(patch[quads, :], wdown_h[...])

            def down_activate():
                half = held["half"]
                th = jnp.tanh(half)
                q = 1.0 + th
                h = half * q
                dslope[quads, :] = q + h * (1.0 - th)
                dact[quads, :] = h.astype(BF16)

            def up():
                held["lifted"] = dot(dact[quads, :], wup_ref[...])

            def error():
                for k in tiles:
                    at = (k - k0) * 64
                    row = pl.ds(entries[k], 1)
                    weight = weight_s[row, :]
                    total = jnp.zeros((64, C), F32)
                    for j in range(4):
                        part = pl.ds(j * 64, 64)
                        err = (
                            resid[k, part, :]
                            + held["lifted"][at:at + 64, j * C:(j + 1) * C]
                            - noise[k, part, :]
                        )
                        total += err * err
                        gp = err * weight
                        resid[k, part, :] = gp
                        glift[pl.ds(k * 64, 64), pl.ds(j * C, C)] = gp.astype(BF16)
                    loss_s[row, :] += jnp.sum(total, axis=0, keepdims=True)

            def up_back():
                held["gda"] = dot_bt(glift[quads, :], wup_h[...])

            def down_slope():
                gpd_s[quads, :] = (held["gda"] * dslope[quads, :]).astype(BF16)

            def down_back():
                held["back"] = dot_bt(gpd_s[quads, :], wdown_ref[...])

            def grad_residual():
                for k in tiles:
                    at = (k - k0) * 64
                    for j in range(4):
                        part = pl.ds(j * 64, 64)
                        gres[pl.ds(k * PIX + j * 64, 64), :] = (
                            resid[k, part, :] + held["back"][at:at + 64, j * C:(j + 1) * C]
                        ).astype(BF16)

            def out_back():
                held["gh"] = dot_bt(gres[rows, :], wout_h[...])

            def hidden_slope():
                gph_s[rows, :] = (held["gh"] * slope[rows, :]).astype(BF16)

            def in_back():
                held["gn"] = dot_bt(gph_s[rows, :], win_ref[...])

            def tile_sums():
                for k in tiles:
                    at = (k - k0) * PIX
                    one = pl.ds(k, 1)
                    centre = noisy[k] - stat[0, one, :]
                    mine = held["gn"][at:at + PIX]
                    row = pl.ds(entries[k], 1)
                    s1_s[row, :] += jnp.sum(mine, axis=0, keepdims=True)
                    s2_s[row, :] += (
                        jnp.sum(mine * centre, axis=0, keepdims=True) * stat[3, one, :]
                    )

            return [
                normalise, project, activate, project_back, residual, down, down_activate, up,
                error, up_back, down_slope, down_back, grad_residual, out_back, hidden_slope,
                in_back, tile_sums,
            ]

        chunks = [chunk_steps(k0) for k0 in range(0, SPAN, CHUNK)]
        for turn in range(len(chunks[0]) + SKEW * (len(chunks) - 1)):
            for index, steps in enumerate(chunks):
                if 0 <= turn - SKEW * index < len(steps):
                    steps[turn - SKEW * index]()

        make_noisy(following, slot)
        add_blocks(pack_ref, ROW_UP, dot_at(dact[...], glift[...]))
        add_blocks(pack_ref, ROW_DOWN, dot_at(gpd_s[...], patch[...]))
        add_blocks(
            pack_ref, ROW_OUT, dot_at(gres[...], hid[...])
        )
        add_blocks(
            pack_ref, ROW_IN, dot_at(x_s[...], gph_s[...])
        )

    scale1 = 1.0 + film_scale[...]
    s2 = s2_s[...]
    pack_ref[pl.ds(ROWS, 1), :] = jnp.sum(s2 * scale1, axis=0, keepdims=True)
    clip_loss = jnp.sum(loss_s[...], axis=1, keepdims=True) * weight_s[...] * 0.5
    place = column((dest_row[...] * lax.axis_size("rep") + lax.axis_index("rep")).astype(F32))
    hits = place == lax.broadcasted_iota(jnp.int32, (CLIPS, C), 1).astype(F32)
    pack_ref[pl.ds(ROWS + 1, 1), :] = jnp.sum(jnp.where(hits, clip_loss, 0.0), axis=0, keepdims=True)
    emb = emb_s[...].astype(F32)
    for ref, part in ((s2 * gain_ref[...], 0), (s1_s[...], 1)):
        pack_ref[pl.ds(ROW_TIME + part * EMB, EMB), :] = lax.dot_general(
            emb, ref, (((0,), (0,)), ((), ())),
            precision=lax.Precision.HIGHEST, preferred_element_type=F32,
        )


def local_grads(clip_tiles, sizes, dests, times, seeds, w_time, gain, w_in, w_out, w_down, w_up):
    vmem = pl.BlockSpec(memory_space=pltpu.VMEM)
    half = EMB // 2
    freq = np.exp(-math.log(10000.0) * np.arange(half) / half).astype(np.float32)
    return pl.pallas_call(
        span_kernel,
        out_shape=[jax.ShapeDtypeStruct(s, F32) for s in [(ROWS + 8, C)]],
        in_specs=[pl.BlockSpec(memory_space=pl.ANY)] * 12,
        out_specs=[vmem],
        scratch_shapes=[
            pltpu.SMEM((1, CLIPS), jnp.int32),
            pltpu.SMEM((1, CLIPS), jnp.int32),
            pltpu.VMEM((1, CLIPS), jnp.int32),
            pltpu.VMEM((1, CLIPS), jnp.int32),
            pltpu.VMEM((1, CLIPS), jnp.int32),
            pltpu.VMEM((1, C), F32),
            pltpu.VMEM((EMB, 2 * C), BF16),
            pltpu.VMEM((1, C), F32),
            pltpu.VMEM((C, HID), BF16),
            pltpu.VMEM((HID, C), BF16),
            pltpu.VMEM((512, 256), BF16),
            pltpu.VMEM((256, 512), BF16),
            pltpu.SemaphoreType.DMA((12,)),
            pltpu.VMEM((2, SPAN, PIX, C), BF16),
            pltpu.SemaphoreType.DMA((2,)),
            pltpu.VMEM((PIX, C), jnp.int32),
            pltpu.VMEM((PIX, PIX), BF16),
            pltpu.VMEM((CLIPS, EMB), BF16),
            pltpu.VMEM((CLIPS, C), F32),
            pltpu.VMEM((CLIPS, C), F32),
            pltpu.VMEM((CLIPS, C), F32),
            pltpu.VMEM((CLIPS, C), F32),
            pltpu.VMEM((CLIPS, C), F32),
            pltpu.VMEM((CLIPS, C), F32),
            pltpu.VMEM((SPAN, PIX, C), F32),
            pltpu.VMEM((SPAN, PIX, C), F32),
            pltpu.VMEM((SPAN * PIX, C), BF16),
            pltpu.VMEM((SPAN * PIX, HID), BF16),
            pltpu.VMEM((SPAN * PIX, HID), F32),
            pltpu.VMEM((SPAN, PIX, C), F32),
            pltpu.VMEM((512, 512), BF16),
            pltpu.VMEM((512, 256), BF16),
            pltpu.VMEM((512, 256), F32),
            pltpu.VMEM((512, 512), BF16),
            pltpu.VMEM((512, 256), BF16),
            pltpu.VMEM((SPAN * PIX, C), BF16),
            pltpu.VMEM((SPAN * PIX, HID), BF16),
            pltpu.VMEM((CLIPS, C), F32),
            pltpu.VMEM((CLIPS, C), F32),
            pltpu.VMEM((CLIPS, C), F32),
            pltpu.VMEM((7, SPAN, C), F32),
            pltpu.VMEM((C, HID), BF16),
            pltpu.VMEM((HID, C), BF16),
            pltpu.VMEM((512, 256), BF16),
            pltpu.VMEM((256, 512), BF16),
        ],
        compiler_params=pltpu.CompilerParams(vmem_limit_bytes=56 * 1024 * 1024),
    )(clip_tiles, sizes, seeds, dests, times, freq.reshape(1, half), w_time,
      gain.reshape(1, C), w_in, w_out, w_down, w_up)


def reduce_kernel(
    sizes, x_hbm, res,
    acc, other, r1, r2, r3, m_own, m_core, m_axes, local_sem, send_sem, recv_sem,
):
    dp, z = lax.axis_index("dp"), lax.axis_index("rep")
    ny = sizes[1]
    core = lax.rem(dp, 2)
    chip = lax.div(dp, 2)
    coord = (lax.div(chip, ny), lax.rem(chip, ny), z)

    def device(x, y, zz, c):
        return ((x * ny + y) * 2 + c, zz)

    def peer(axis, r):
        other_coord = lax.rem(coord[axis] + r, sizes[axis])
        place = list(coord)
        place[axis] = other_coord
        return other_coord, device(*place, core)

    sibling = device(*coord, 1 - core)
    peers = [(axis, r) for axis in range(3) for r in range(1, sizes[axis])]
    barrier = pltpu.get_barrier_semaphore()
    for target in [sibling] + [peer(axis, r)[1] for axis, r in peers]:
        pl.semaphore_signal(barrier, inc=1, device_id=target, device_id_type=pl.DeviceIdType.MESH)

    mine = core * HALF
    theirs = (1 - core) * HALF
    local = []
    for p in range(PARTS):
        copy = pltpu.make_async_copy(
            x_hbm.at[pl.ds(pl.multiple_of(mine + p * PART, 8), PART)],
            acc.at[pl.ds(p * PART, PART)], local_sem.at[p],
        )
        copy.start()
        local.append(copy)
    misc_rows = pl.ds(ROWS, 8)
    m_local = pltpu.make_async_copy(x_hbm.at[misc_rows], m_own, local_sem.at[PARTS])
    m_local.start()
    pl.semaphore_wait(barrier, 1 + len(peers))

    started = []

    def send(src, dst, target):
        index = len(started)
        copy = pltpu.make_async_remote_copy(
            src_ref=src, dst_ref=dst, send_sem=send_sem.at[index], recv_sem=recv_sem.at[index],
            device_id=target, device_id_type=pl.DeviceIdType.MESH,
        )
        copy.start()
        started.append(copy)
        return copy

    m_core_copy = send(x_hbm.at[misc_rows], m_core, sibling)
    first = [
        send(
            x_hbm.at[pl.ds(pl.multiple_of(theirs + p * PART, 8), PART)],
            other.at[pl.ds(p * PART, PART)], sibling,
        )
        for p in range(PARTS)
    ]

    order = [[(p + s) % 3 for s in range(3)] for p in range(PARTS)]
    lengths = []
    for p in range(PARTS):
        length, row = PART, []
        for s in range(3):
            length //= sizes[order[p][s]]
            row.append(length)
        lengths.append(row)
    landing = (r1, r2)
    base = [jnp.int32(p * PART) for p in range(PARTS)]
    starts = [[None] * 3 for _ in range(PARTS)]

    def scatter(p, s):
        axis, length = order[p][s], lengths[p][s]
        copies = []
        for r in range(1, sizes[axis]):
            q, target = peer(axis, r)
            rows = pl.ds(pl.multiple_of(base[p] + q * length, 8), length)
            copies.append(send(acc.at[rows], landing[s].at[p, r - 1], target))
        base[p] = base[p] + coord[axis] * length
        starts[p][s] = base[p]
        return copies

    flying = [None] * PARTS
    for p in range(PARTS):
        local[p].wait()
        first[p].wait_recv()
        rows = pl.ds(p * PART, PART)
        acc[rows, :] = acc[rows, :] + other[rows, :]
        flying[p] = scatter(p, 0)
    m_local.wait()
    m_core_copy.wait_recv()

    def exchange(slots, axis, value):
        slots[coord[axis]] = value
        return [
            send(slots.at[coord[axis]], slots.at[coord[axis]], peer(axis, r)[1])
            for r in range(1, sizes[axis])
        ]

    def total_of(slots, axis, copies):
        for copy in copies:
            copy.wait_recv()
        total = slots[0]
        for i in range(1, sizes[axis]):
            total = total + slots[i]
        return total

    misc_copies = exchange(m_axes.at[0], 0, m_own[...] + m_core[...])
    for s in range(2):
        for p in range(PARTS):
            for copy in flying[p]:
                copy.wait_recv()
            rows = pl.ds(pl.multiple_of(base[p], 8), lengths[p][s])
            total = acc[rows, :]
            for r in range(sizes[order[p][s]] - 1):
                total = total + landing[s][p, r]
            if s == 0:
                acc[rows, :] = total
                flying[p] = scatter(p, 1)
            else:
                flying[p] = exchange(r3.at[p, :, pl.ds(0, lengths[p][1])], order[p][2], total)
        misc_copies = exchange(
            m_axes.at[s + 1], s + 1, total_of(m_axes.at[s], s, misc_copies)
        )
    for p in range(PARTS):
        total = total_of(r3.at[p, :, pl.ds(0, lengths[p][1])], order[p][2], flying[p])
        res[pl.ds(pl.multiple_of(mine + base[p], 8), lengths[p][1]), :] = total
        flying[p] = gather(p, 1, sizes, order, lengths, starts, mine, peer, send, res)
    res[misc_rows, :] = total_of(m_axes.at[2], 2, misc_copies)
    last = []

    def forward(p, q):
        rows = pl.ds(pl.multiple_of(mine + p * PART + q * lengths[p][0], 8), lengths[p][0])
        last.append(send(res.at[rows], res.at[rows], sibling))

    for p in range(PARTS):
        for copy in flying[p]:
            copy.wait_recv()
        flying[p] = gather(p, 0, sizes, order, lengths, starts, mine, peer, send, res)
        forward(p, coord[order[p][0]])
    longest = max(sizes)
    for r in [i for i in range(1, longest) if i != 2] + [2]:
        for p in range(PARTS):
            axis = order[p][0]
            if r < sizes[axis]:
                flying[p][r - 1].wait_recv()
                forward(p, lax.rem(coord[axis] + sizes[axis] - r, sizes[axis]))
    for copy in last:
        copy.wait_recv()
    for copy in started:
        copy.wait_send()


def gather(p, s, sizes, order, lengths, starts, mine, peer, send, res):
    axis = order[p][s]
    rows = pl.ds(pl.multiple_of(mine + starts[p][s], 8), lengths[p][s])
    return [send(res.at[rows], res.at[rows], peer(axis, r)[1]) for r in range(1, sizes[axis])]


def all_reduce(packed, sizes):
    vmem = pl.BlockSpec(memory_space=pltpu.VMEM)
    most = max(sizes) - 1
    per_axis = sum(n - 1 for n in sizes)
    copies = 1 + PARTS + per_axis * (5 * PARTS // 3 + 1) + sum(sizes)
    shapes = []
    for s in range(2):
        longest = 0
        for p in range(PARTS):
            length = PART
            for i in range(s + 1):
                length //= sizes[(p + i) % 3]
            longest = max(longest, length)
        shapes.append(longest)
    return pl.pallas_call(
        functools.partial(reduce_kernel, sizes),
        out_shape=jax.ShapeDtypeStruct((ROWS + 8, C), F32),
        in_specs=[pl.BlockSpec(memory_space=pl.ANY)],
        out_specs=vmem,
        scratch_shapes=[
            pltpu.VMEM((HALF, C), F32),
            pltpu.VMEM((HALF, C), F32),
            pltpu.VMEM((PARTS, most, shapes[0], C), F32),
            pltpu.VMEM((PARTS, most, shapes[1], C), F32),
            pltpu.VMEM((PARTS, max(sizes), shapes[1], C), F32),
            pltpu.VMEM((8, C), F32),
            pltpu.VMEM((8, C), F32),
            pltpu.VMEM((3, max(sizes), 8, C), F32),
            pltpu.SemaphoreType.DMA((PARTS + 1,)),
            pltpu.SemaphoreType.DMA((copies,)),
            pltpu.SemaphoreType.DMA((copies,)),
        ],
        compiler_params=pltpu.CompilerParams(
            collective_id=0, has_side_effects=True, vmem_limit_bytes=16 * 1024 * 1024
        ),
    )(packed)


def finish_kernel(packed, gt, gain, gin, gout, gdown, gup, own):
    def block(start, height, j):
        return packed[pl.ds(start + j * height, height), :]

    for j in range(2):
        cols = pl.ds(j * C, C)
        gt[:, cols] = block(ROW_TIME, EMB, j)
        gin[:, cols] = block(ROW_IN, C, j)
        gout[cols, :] = block(ROW_OUT, C, j).T
    for j in range(4):
        cols = pl.ds(j * C, C)
        gdown[cols, :] = block(ROW_DOWN, 256, j).T
        gup[:, cols] = block(ROW_UP, 256, j)
    gain[...] = packed[pl.ds(ROWS, 1), :]
    me = lax.axis_index("dp") * lax.axis_size("rep") + lax.axis_index("rep")
    lane = lax.broadcasted_iota(jnp.int32, (1, C), 1)
    own[0] = jnp.sum(jnp.where(lane == me, packed[pl.ds(ROWS + 1, 1), :], 0.0))


def finish(packed):
    vmem = pl.BlockSpec(memory_space=pltpu.VMEM)
    shapes = [(EMB, 2 * C), (1, C), (C, HID), (HID, C), (512, 256), (256, 512), (1,)]
    return pl.pallas_call(
        finish_kernel,
        out_shape=[jax.ShapeDtypeStruct(s, F32) for s in shapes],
        in_specs=[vmem],
        out_specs=[vmem] * 6 + [pl.BlockSpec(memory_space=pltpu.SMEM)],
        compiler_params=pltpu.CompilerParams(vmem_limit_bytes=32 * 1024 * 1024),
    )(packed)


def body(sizes, clip_tiles, clip_size, clip_dest, timesteps, noise_seeds, w_time, gain, w_in, w_out, w_down, w_up):
    packed, = local_grads(
        clip_tiles, clip_size, clip_dest, timesteps, noise_seeds,
        w_time, gain, w_in, w_out, w_down, w_up,
    )
    packed = all_reduce(packed, sizes)
    gt, ggain, gin, gout, gdown, gup, own = finish(packed)
    return (gt, ggain.reshape(C), gin, gout, gdown, gup, own)


def solution(mesh):
    rows = P(("dp", "rep"), None)
    in_specs = (P(("dp", "rep"), None, None), rows, rows, rows, rows) + (P(),) * 6
    out_specs = (P(),) * 6 + (P(("dp", "rep")),)
    sizes = (4, mesh.shape["dp"] // 8, mesh.shape["rep"])
    return jax.shard_map(functools.partial(body, sizes), mesh=mesh, in_specs=in_specs, out_specs=out_specs, check_vma=False)
```

```python
import functools
import math

import jax
import jax.numpy as jnp
import numpy as np
from jax import lax
from jax.experimental import pallas as pl
from jax.experimental.pallas import tpu as pltpu
from jax.sharding import PartitionSpec as P

EMB = 256
TR = 8
TC = 32
TSTEPS = 1000
C = 128
PIX = 256
HID = 256
SPAN = 8
RUN = 4
CLIPS = 64
MUL_POS = 1103515245
MUL_SEED = 747796405
ADD_POS = 1013904223
MUL_MIX = 73244475
ROOT3 = 1.7320508
NOISE_A = float(np.float32(2.0 * ROOT3 / 16777216.0))
NOISE_B = float(np.float32(ROOT3 * (1.0 / 16777216.0 - 1.0)))
CHUNK, SKEW = 2, 1
F32 = jnp.float32
BF16 = jnp.bfloat16
ROW_TIME, ROW_IN, ROW_OUT, ROW_DOWN, ROW_UP, ROWS = 0, 512, 768, 1024, 2048, 3072
PARTS = 3
HALF = ROWS // 2
PART = HALF // PARTS


def wrap32(value):
    value &= 0xFFFFFFFF
    return value - (1 << 32) if value >= (1 << 31) else value


def dot(a, b):
    return lax.dot_general(a, b, (((1,), (0,)), ((), ())), preferred_element_type=F32)


def dot_bt(a, b):
    return lax.dot_general(a, b, (((1,), (1,)), ((), ())), preferred_element_type=F32)


def dot_at(a, b):
    return lax.dot_general(a, b, (((0,), (0,)), ((), ())), preferred_element_type=F32)


def shift_right(value, amount):
    return lax.shift_right_logical(value, jnp.int32(amount))


def group_sum(x, lane):
    pair = x + jnp.where(lane % 2 == 0, pltpu.roll(x, 127, 1), pltpu.roll(x, 1, 1))
    return pair + jnp.where(lane % 4 < 2, pltpu.roll(pair, 126, 1), pltpu.roll(pair, 2, 1))


def add_blocks(pack_ref, start, value):
    height = value.shape[0]
    for j in range(value.shape[1] // C):
        pack_ref[pl.ds(start + j * height, height), :] += value[:, j * C:(j + 1) * C]


def span_kernel(
    tiles_hbm, sizes_hbm, seeds_hbm, dest_hbm, time_hbm, freq_hbm, wt_hbm, gain_hbm,
    win_hbm, wout_hbm, wdown_hbm, wup_hbm,
    pack_ref,
    sizes_ref, seeds_ref, sizes_row, dest_row, time_row, freq_ref, wt_ref, gain_ref,
    win_ref, wout_ref, wdown_ref, wup_ref, input_sem,
    buf, sem, itab, perm, emb_s, film_scale, film_shift, sa_s, sb_s, weight_s, inv_s,
    noise, noisy, x_s, hid, slope, resid, patch,
    dact, dslope, glift, gpd_s, gres, gph_s, s1_s, s2_s, loss_s, stat,
    win_h, wout_h, wdown_h, wup_h,
):
    inputs = [
        pltpu.make_async_copy(source, target, input_sem.at[index])
        for index, (source, target) in enumerate((
            (sizes_hbm, sizes_ref), (seeds_hbm, seeds_ref), (sizes_hbm, sizes_row),
            (time_hbm, time_row), (freq_hbm, freq_ref), (wt_hbm, wt_ref), (gain_hbm, gain_ref),
            (win_hbm, win_ref), (wout_hbm, wout_ref), (wdown_hbm, wdown_ref),
            (wup_hbm, wup_ref), (dest_hbm, dest_row),
        ))
    ]
    for copy in inputs:
        copy.start()
    inputs[0].wait()
    total = sizes_ref[0, 0]
    for entry in range(1, CLIPS):
        total += sizes_ref[0, entry]
    count = total // SPAN

    def fetch(span, slot):
        return pltpu.make_async_copy(
            tiles_hbm.at[pl.ds(span * SPAN, SPAN)], buf.at[slot], sem.at[slot]
        )

    @pl.when(count > 0)
    def _():
        fetch(0, 0).start()

    row = lax.broadcasted_iota(jnp.int32, (PIX, C), 0)
    lane = lax.broadcasted_iota(jnp.int32, (PIX, C), 1)
    quad, rest = row // 64, row % 64
    pixel = (2 * (rest // 16) + quad // 2) * TC + 2 * (rest % 16) + quad % 2
    itab[...] = (pixel * C + lane) * jnp.int32(MUL_POS)
    prow = lax.broadcasted_iota(jnp.int32, (PIX, PIX), 0)
    pcol = lax.broadcasted_iota(jnp.int32, (PIX, PIX), 1)
    pquad, prest = prow // 64, prow % 64
    ppix = (2 * (prest // 16) + pquad // 2) * TC + 2 * (prest % 16) + pquad % 2
    perm[...] = jnp.where(ppix == pcol, 1.0, 0.0).astype(BF16)
    for ref in (pack_ref, s1_s, s2_s, loss_s):
        ref[...] = jnp.zeros_like(ref)
    lane8 = lax.broadcasted_iota(jnp.int32, (SPAN, C), 1)
    for copy in inputs[1:]:
        copy.wait()
    eye = lax.broadcasted_iota(jnp.int32, (CLIPS, CLIPS), 0) == lax.broadcasted_iota(
        jnp.int32, (CLIPS, CLIPS), 1
    )

    def column(values):
        picked = jnp.sum(jnp.where(eye, values, 0.0), axis=1, keepdims=True)
        return jnp.broadcast_to(picked, (CLIPS, C))

    step = time_row[...].astype(F32)
    alpha_bar = jnp.cos(((step + 1.0) / TSTEPS + 0.008) / 1.008 * (math.pi / 2.0)) ** 2
    sa_s[...] = column(jnp.sqrt(alpha_bar))
    sb_s[...] = column(jnp.sqrt(1.0 - alpha_bar))
    inv_len = 1.0 / column(jnp.maximum(sizes_row[...], 1).astype(F32))
    inv_s[...] = inv_len * (1.0 / (PIX * 4))
    weight_s[...] = inv_len * (2.0 / (PIX * C))
    angle = column(step) * freq_ref[...]
    emb_s[:, :C] = jnp.cos(angle).astype(BF16)
    emb_s[:, C:] = jnp.sin(angle).astype(BF16)
    modulation = dot(emb_s[...], wt_ref[...])
    film_scale[...] = modulation[:, :C]
    film_shift[...] = modulation[:, C:]
    win_h[...] = win_ref[...] * jnp.asarray(0.5, BF16)
    wdown_h[...] = wdown_ref[...] * jnp.asarray(0.5, BF16)
    wout_h[...] = wout_ref[...] * jnp.asarray(0.5, BF16)
    wup_h[...] = wup_ref[...] * jnp.asarray(0.5, BF16)

    def marks(span):
        one = sizes_ref[0, span * RUN]
        two = one + sizes_ref[0, span * RUN + 1]
        return one, two, two + sizes_ref[0, span * RUN + 2]

    def owner_of(tile, bounds):
        return sum((tile >= bound).astype(jnp.int32) for bound in bounds)

    def make_noisy(span, slot):
        bounds = marks(span)
        owners = [owner_of(jnp.int32(k), bounds) for k in range(SPAN)]
        for k in range(SPAN):
            if k % 2 == 0:
                pair = dot(
                    perm[...], jnp.concatenate([buf[slot, k], buf[slot, k + 1]], axis=1)
                )
            entry = span * RUN + owners[k]
            row = pl.ds(entry, 1)
            start = jnp.int32(0)
            for bound in bounds:
                start = jnp.where(k >= bound, bound, start)
            mix = (
                (k - start) * jnp.int32(wrap32(PIX * C * MUL_POS))
                + seeds_ref[0, entry] * jnp.int32(MUL_SEED) + jnp.int32(ADD_POS)
            )
            stat[4, pl.ds(k, 1), :] = inv_s[row, :]
            stat[5, pl.ds(k, 1), :] = film_scale[row, :]
            stat[6, pl.ds(k, 1), :] = film_shift[row, :]
            mixed = itab[...] + mix
            mixed = mixed ^ shift_right(mixed, 16)
            mixed = mixed * jnp.int32(MUL_MIX)
            mixed = mixed ^ shift_right(mixed, 16)
            mixed = mixed * jnp.int32(MUL_MIX)
            mixed = mixed ^ shift_right(mixed, 16)
            field = shift_right(mixed, 8).astype(F32) * NOISE_A + NOISE_B
            noise[k] = field
            pixels = pair[:, (k % 2) * C:(k % 2 + 1) * C]
            value = sa_s[row, :] * pixels + sb_s[row, :] * field
            noisy[k] = value
            stat[0, pl.ds(k, 1), :] = jnp.sum(value, axis=0, keepdims=True)
            stat[1, pl.ds(k, 1), :] = jnp.sum(value * value, axis=0, keepdims=True)

        tile8 = lax.broadcasted_iota(jnp.int32, (SPAN, C), 0)
        seg = owner_of(tile8, bounds)
        inv_count = stat[4]
        first = jnp.zeros((SPAN, C), F32)
        square = jnp.zeros((SPAN, C), F32)
        for k in range(SPAN):
            member = seg == owners[k]
            first += jnp.where(member, stat[0, pl.ds(k, 1), :], 0.0)
            square += jnp.where(member, stat[1, pl.ds(k, 1), :], 0.0)
        mean = group_sum(first, lane8) * inv_count
        var = group_sum(square, lane8) * inv_count - mean * mean
        spread = lax.rsqrt(var + 1e-05)
        factor = spread * gain_ref[...] * (1.0 + stat[5])
        shift = stat[6]
        stat[0] = mean
        stat[1] = factor
        stat[2] = shift
        stat[3] = spread

    @pl.when(count > 0)
    def _():
        @pl.when(count > 1)
        def _():
            fetch(1, 1).start()

        fetch(0, 0).wait()
        make_noisy(0, 0)

    @pl.loop(0, count)
    def _(span):
        bounds = marks(span)
        entries = [span * RUN + owner_of(jnp.int32(k), bounds) for k in range(SPAN)]
        following = jnp.minimum(span + 1, count - 1)
        slot = lax.rem(span + 1, 2)

        @pl.when(span + 1 < count)
        def _():
            fetch(span + 1, slot).wait()

        @pl.when(span + 2 < count)
        def _():
            fetch(span + 2, 1 - slot).start()

        def chunk_steps(k0):
            tiles = range(k0, k0 + CHUNK)
            rows = pl.ds(k0 * PIX, CHUNK * PIX)
            quads = pl.ds(k0 * 64, CHUNK * 64)
            held = {}

            def normalise():
                for k in tiles:
                    one = pl.ds(k, 1)
                    centre = noisy[k] - stat[0, one, :]
                    x_s[pl.ds(k * PIX, PIX), :] = (
                        centre * stat[1, one, :] + stat[2, one, :]
                    ).astype(BF16)

            def project():
                held["half"] = dot(x_s[rows, :], win_h[...])

            def activate():
                half = held["half"]
                th = jnp.tanh(half)
                q = 1.0 + th
                h = half * q
                slope[rows, :] = q + h * (1.0 - th)
                hid[rows, :] = h.astype(BF16)

            def project_back():
                held["out"] = dot(hid[rows, :], wout_ref[...])

            def residual():
                for k in tiles:
                    at = (k - k0) * PIX
                    out = held["out"][at:at + PIX] + noisy[k]
                    resid[k] = out
                    outb = out.astype(BF16)
                    for j in range(4):
                        patch[pl.ds(k * 64, 64), pl.ds(j * C, C)] = outb[j * 64:(j + 1) * 64]

            def down():
                held["half"] = dot(patch[quads, :], wdown_h[...])

            def down_activate():
                half = held["half"]
                th = jnp.tanh(half)
                q = 1.0 + th
                h = half * q
                dslope[quads, :] = q + h * (1.0 - th)
                dact[quads, :] = h.astype(BF16)

            def up():
                held["lifted"] = dot(dact[quads, :], wup_ref[...])

            def error():
                for k in tiles:
                    at = (k - k0) * 64
                    row = pl.ds(entries[k], 1)
                    weight = weight_s[row, :]
                    total = jnp.zeros((64, C), F32)
                    for j in range(4):
                        part = pl.ds(j * 64, 64)
                        err = (
                            resid[k, part, :]
                            + held["lifted"][at:at + 64, j * C:(j + 1) * C]
                            - noise[k, part, :]
                        )
                        total += err * err
                        gp = err * weight
                        resid[k, part, :] = gp
                        glift[pl.ds(k * 64, 64), pl.ds(j * C, C)] = gp.astype(BF16)
                    loss_s[row, :] += jnp.sum(total, axis=0, keepdims=True)

            def up_back():
                held["gda"] = dot_bt(glift[quads, :], wup_h[...])

            def down_slope():
                gpd_s[quads, :] = (held["gda"] * dslope[quads, :]).astype(BF16)

            def down_back():
                held["back"] = dot_bt(gpd_s[quads, :], wdown_ref[...])

            def grad_residual():
                for k in tiles:
                    at = (k - k0) * 64
                    for j in range(4):
                        part = pl.ds(j * 64, 64)
                        gres[pl.ds(k * PIX + j * 64, 64), :] = (
                            resid[k, part, :] + held["back"][at:at + 64, j * C:(j + 1) * C]
                        ).astype(BF16)

            def out_back():
                held["gh"] = dot_bt(gres[rows, :], wout_h[...])

            def hidden_slope():
                gph_s[rows, :] = (held["gh"] * slope[rows, :]).astype(BF16)

            def in_back():
                held["gn"] = dot_bt(gph_s[rows, :], win_ref[...])

            def tile_sums():
                for k in tiles:
                    at = (k - k0) * PIX
                    one = pl.ds(k, 1)
                    centre = noisy[k] - stat[0, one, :]
                    mine = held["gn"][at:at + PIX]
                    row = pl.ds(entries[k], 1)
                    s1_s[row, :] += jnp.sum(mine, axis=0, keepdims=True)
                    s2_s[row, :] += (
                        jnp.sum(mine * centre, axis=0, keepdims=True) * stat[3, one, :]
                    )

            return [
                normalise, project, activate, project_back, residual, down, down_activate, up,
                error, up_back, down_slope, down_back, grad_residual, out_back, hidden_slope,
                in_back, tile_sums,
            ]

        chunks = [chunk_steps(k0) for k0 in range(0, SPAN, CHUNK)]
        for turn in range(len(chunks[0]) + SKEW * (len(chunks) - 1)):
            for index, steps in enumerate(chunks):
                if 0 <= turn - SKEW * index < len(steps):
                    steps[turn - SKEW * index]()

        make_noisy(following, slot)
        add_blocks(pack_ref, ROW_UP, dot_at(dact[...], glift[...]))
        add_blocks(pack_ref, ROW_DOWN, dot_at(gpd_s[...], patch[...]))
        add_blocks(
            pack_ref, ROW_OUT, dot_at(gres[...], hid[...])
        )
        add_blocks(
            pack_ref, ROW_IN, dot_at(x_s[...], gph_s[...])
        )

    scale1 = 1.0 + film_scale[...]
    s2 = s2_s[...]
    pack_ref[pl.ds(ROWS, 1), :] = jnp.sum(s2 * scale1, axis=0, keepdims=True)
    clip_loss = jnp.sum(loss_s[...], axis=1, keepdims=True) * weight_s[...] * 0.5
    place = column((dest_row[...] * lax.axis_size("rep") + lax.axis_index("rep")).astype(F32))
    hits = place == lax.broadcasted_iota(jnp.int32, (CLIPS, C), 1).astype(F32)
    pack_ref[pl.ds(ROWS + 1, 1), :] = jnp.sum(jnp.where(hits, clip_loss, 0.0), axis=0, keepdims=True)
    emb = emb_s[...].astype(F32)
    for ref, part in ((s2 * gain_ref[...], 0), (s1_s[...], 1)):
        pack_ref[pl.ds(ROW_TIME + part * EMB, EMB), :] = lax.dot_general(
            emb, ref, (((0,), (0,)), ((), ())),
            precision=lax.Precision.HIGHEST, preferred_element_type=F32,
        )


def local_grads(clip_tiles, sizes, dests, times, seeds, w_time, gain, w_in, w_out, w_down, w_up):
    vmem = pl.BlockSpec(memory_space=pltpu.VMEM)
    half = EMB // 2
    freq = np.exp(-math.log(10000.0) * np.arange(half) / half).astype(np.float32)
    return pl.pallas_call(
        span_kernel,
        out_shape=[jax.ShapeDtypeStruct(s, F32) for s in [(ROWS + 8, C)]],
        in_specs=[pl.BlockSpec(memory_space=pl.ANY)] * 12,
        out_specs=[vmem],
        scratch_shapes=[
            pltpu.SMEM((1, CLIPS), jnp.int32),
            pltpu.SMEM((1, CLIPS), jnp.int32),
            pltpu.VMEM((1, CLIPS), jnp.int32),
            pltpu.VMEM((1, CLIPS), jnp.int32),
            pltpu.VMEM((1, CLIPS), jnp.int32),
            pltpu.VMEM((1, C), F32),
            pltpu.VMEM((EMB, 2 * C), BF16),
            pltpu.VMEM((1, C), F32),
            pltpu.VMEM((C, HID), BF16),
            pltpu.VMEM((HID, C), BF16),
            pltpu.VMEM((512, 256), BF16),
            pltpu.VMEM((256, 512), BF16),
            pltpu.SemaphoreType.DMA((12,)),
            pltpu.VMEM((2, SPAN, PIX, C), BF16),
            pltpu.SemaphoreType.DMA((2,)),
            pltpu.VMEM((PIX, C), jnp.int32),
            pltpu.VMEM((PIX, PIX), BF16),
            pltpu.VMEM((CLIPS, EMB), BF16),
            pltpu.VMEM((CLIPS, C), F32),
            pltpu.VMEM((CLIPS, C), F32),
            pltpu.VMEM((CLIPS, C), F32),
            pltpu.VMEM((CLIPS, C), F32),
            pltpu.VMEM((CLIPS, C), F32),
            pltpu.VMEM((CLIPS, C), F32),
            pltpu.VMEM((SPAN, PIX, C), F32),
            pltpu.VMEM((SPAN, PIX, C), F32),
            pltpu.VMEM((SPAN * PIX, C), BF16),
            pltpu.VMEM((SPAN * PIX, HID), BF16),
            pltpu.VMEM((SPAN * PIX, HID), F32),
            pltpu.VMEM((SPAN, PIX, C), F32),
            pltpu.VMEM((512, 512), BF16),
            pltpu.VMEM((512, 256), BF16),
            pltpu.VMEM((512, 256), F32),
            pltpu.VMEM((512, 512), BF16),
            pltpu.VMEM((512, 256), BF16),
            pltpu.VMEM((SPAN * PIX, C), BF16),
            pltpu.VMEM((SPAN * PIX, HID), BF16),
            pltpu.VMEM((CLIPS, C), F32),
            pltpu.VMEM((CLIPS, C), F32),
            pltpu.VMEM((CLIPS, C), F32),
            pltpu.VMEM((7, SPAN, C), F32),
            pltpu.VMEM((C, HID), BF16),
            pltpu.VMEM((HID, C), BF16),
            pltpu.VMEM((512, 256), BF16),
            pltpu.VMEM((256, 512), BF16),
        ],
        compiler_params=pltpu.CompilerParams(vmem_limit_bytes=56 * 1024 * 1024),
    )(clip_tiles, sizes, seeds, dests, times, freq.reshape(1, half), w_time,
      gain.reshape(1, C), w_in, w_out, w_down, w_up)


def reduce_kernel(
    sizes, x_hbm, res,
    acc, other, r1, r2, r3, m_own, m_core, m_axes, local_sem, send_sem, recv_sem,
):
    dp, z = lax.axis_index("dp"), lax.axis_index("rep")
    ny = sizes[1]
    core = lax.rem(dp, 2)
    chip = lax.div(dp, 2)
    coord = (lax.div(chip, ny), lax.rem(chip, ny), z)

    def device(x, y, zz, c):
        return ((x * ny + y) * 2 + c, zz)

    def peer(axis, r):
        other_coord = lax.rem(coord[axis] + r, sizes[axis])
        place = list(coord)
        place[axis] = other_coord
        return other_coord, device(*place, core)

    sibling = device(*coord, 1 - core)
    peers = [(axis, r) for axis in range(3) for r in range(1, sizes[axis])]
    barrier = pltpu.get_barrier_semaphore()
    for target in [sibling] + [peer(axis, r)[1] for axis, r in peers]:
        pl.semaphore_signal(barrier, inc=1, device_id=target, device_id_type=pl.DeviceIdType.MESH)

    mine = core * HALF
    theirs = (1 - core) * HALF
    local = []
    for p in range(PARTS):
        copy = pltpu.make_async_copy(
            x_hbm.at[pl.ds(pl.multiple_of(mine + p * PART, 8), PART)],
            acc.at[pl.ds(p * PART, PART)], local_sem.at[p],
        )
        copy.start()
        local.append(copy)
    misc_rows = pl.ds(ROWS, 8)
    m_local = pltpu.make_async_copy(x_hbm.at[misc_rows], m_own, local_sem.at[PARTS])
    m_local.start()
    pl.semaphore_wait(barrier, 1 + len(peers))

    started = []

    def send(src, dst, target):
        index = len(started)
        copy = pltpu.make_async_remote_copy(
            src_ref=src, dst_ref=dst, send_sem=send_sem.at[index], recv_sem=recv_sem.at[index],
            device_id=target, device_id_type=pl.DeviceIdType.MESH,
        )
        copy.start()
        started.append(copy)
        return copy

    m_core_copy = send(x_hbm.at[misc_rows], m_core, sibling)
    first = [
        send(
            x_hbm.at[pl.ds(pl.multiple_of(theirs + p * PART, 8), PART)],
            other.at[pl.ds(p * PART, PART)], sibling,
        )
        for p in range(PARTS)
    ]

    order = [[(p + s) % 3 for s in range(3)] for p in range(PARTS)]
    lengths = []
    for p in range(PARTS):
        length, row = PART, []
        for s in range(3):
            length //= sizes[order[p][s]]
            row.append(length)
        lengths.append(row)
    landing = (r1, r2)
    base = [jnp.int32(p * PART) for p in range(PARTS)]
    starts = [[None] * 3 for _ in range(PARTS)]

    def scatter(p, s):
        axis, length = order[p][s], lengths[p][s]
        copies = []
        for r in range(1, sizes[axis]):
            q, target = peer(axis, r)
            rows = pl.ds(pl.multiple_of(base[p] + q * length, 8), length)
            copies.append(send(acc.at[rows], landing[s].at[p, r - 1], target))
        base[p] = base[p] + coord[axis] * length
        starts[p][s] = base[p]
        return copies

    flying = [None] * PARTS
    for p in range(PARTS):
        local[p].wait()
        first[p].wait_recv()
        rows = pl.ds(p * PART, PART)
        acc[rows, :] = acc[rows, :] + other[rows, :]
        flying[p] = scatter(p, 0)
    m_local.wait()
    m_core_copy.wait_recv()

    def exchange(slots, axis, value):
        slots[coord[axis]] = value
        return [
            send(slots.at[coord[axis]], slots.at[coord[axis]], peer(axis, r)[1])
            for r in range(1, sizes[axis])
        ]

    def total_of(slots, axis, copies):
        for copy in copies:
            copy.wait_recv()
        total = slots[0]
        for i in range(1, sizes[axis]):
            total = total + slots[i]
        return total

    misc_copies = exchange(m_axes.at[0], 0, m_own[...] + m_core[...])
    for s in range(2):
        for p in range(PARTS):
            for copy in flying[p]:
                copy.wait_recv()
            rows = pl.ds(pl.multiple_of(base[p], 8), lengths[p][s])
            total = acc[rows, :]
            for r in range(sizes[order[p][s]] - 1):
                total = total + landing[s][p, r]
            if s == 0:
                acc[rows, :] = total
                flying[p] = scatter(p, 1)
            else:
                flying[p] = exchange(r3.at[p, :, pl.ds(0, lengths[p][1])], order[p][2], total)
        misc_copies = exchange(
            m_axes.at[s + 1], s + 1, total_of(m_axes.at[s], s, misc_copies)
        )
    for p in range(PARTS):
        total = total_of(r3.at[p, :, pl.ds(0, lengths[p][1])], order[p][2], flying[p])
        res[pl.ds(pl.multiple_of(mine + base[p], 8), lengths[p][1]), :] = total
        flying[p] = gather(p, 1, sizes, order, lengths, starts, mine, peer, send, res)
    res[misc_rows, :] = total_of(m_axes.at[2], 2, misc_copies)
    last = []

    def forward(p, q):
        rows = pl.ds(pl.multiple_of(mine + p * PART + q * lengths[p][0], 8), lengths[p][0])
        last.append(send(res.at[rows], res.at[rows], sibling))

    for p in range(PARTS):
        for copy in flying[p]:
            copy.wait_recv()
        flying[p] = gather(p, 0, sizes, order, lengths, starts, mine, peer, send, res)
        forward(p, coord[order[p][0]])
    longest = max(sizes)
    for r in [i for i in range(1, longest) if i != 2] + [2]:
        for p in range(PARTS):
            axis = order[p][0]
            if r < sizes[axis]:
                flying[p][r - 1].wait_recv()
                forward(p, lax.rem(coord[axis] + sizes[axis] - r, sizes[axis]))
    for copy in last:
        copy.wait_recv()
    for copy in started:
        copy.wait_send()


def gather(p, s, sizes, order, lengths, starts, mine, peer, send, res):
    axis = order[p][s]
    rows = pl.ds(pl.multiple_of(mine + starts[p][s], 8), lengths[p][s])
    return [send(res.at[rows], res.at[rows], peer(axis, r)[1]) for r in range(1, sizes[axis])]


def all_reduce(packed, sizes):
    vmem = pl.BlockSpec(memory_space=pltpu.VMEM)
    most = max(sizes) - 1
    per_axis = sum(n - 1 for n in sizes)
    copies = 1 + PARTS + per_axis * (5 * PARTS // 3 + 1) + sum(sizes)
    shapes = []
    for s in range(2):
        longest = 0
        for p in range(PARTS):
            length = PART
            for i in range(s + 1):
                length //= sizes[(p + i) % 3]
            longest = max(longest, length)
        shapes.append(longest)
    return pl.pallas_call(
        functools.partial(reduce_kernel, sizes),
        out_shape=jax.ShapeDtypeStruct((ROWS + 8, C), F32),
        in_specs=[pl.BlockSpec(memory_space=pl.ANY)],
        out_specs=vmem,
        scratch_shapes=[
            pltpu.VMEM((HALF, C), F32),
            pltpu.VMEM((HALF, C), F32),
            pltpu.VMEM((PARTS, most, shapes[0], C), F32),
            pltpu.VMEM((PARTS, most, shapes[1], C), F32),
            pltpu.VMEM((PARTS, max(sizes), shapes[1], C), F32),
            pltpu.VMEM((8, C), F32),
            pltpu.VMEM((8, C), F32),
            pltpu.VMEM((3, max(sizes), 8, C), F32),
            pltpu.SemaphoreType.DMA((PARTS + 1,)),
            pltpu.SemaphoreType.DMA((copies,)),
            pltpu.SemaphoreType.DMA((copies,)),
        ],
        compiler_params=pltpu.CompilerParams(
            collective_id=0, has_side_effects=True, vmem_limit_bytes=16 * 1024 * 1024
        ),
    )(packed)


def finish_kernel(packed, gt, gain, gin, gout, gdown, gup, own):
    def block(start, height, j):
        return packed[pl.ds(start + j * height, height), :]

    for j in range(2):
        cols = pl.ds(j * C, C)
        gt[:, cols] = block(ROW_TIME, EMB, j)
        gin[:, cols] = block(ROW_IN, C, j)
        gout[cols, :] = block(ROW_OUT, C, j).T
    for j in range(4):
        cols = pl.ds(j * C, C)
        gdown[cols, :] = block(ROW_DOWN, 256, j).T
        gup[:, cols] = block(ROW_UP, 256, j)
    gain[...] = packed[pl.ds(ROWS, 1), :]
    me = lax.axis_index("dp") * lax.axis_size("rep") + lax.axis_index("rep")
    lane = lax.broadcasted_iota(jnp.int32, (1, C), 1)
    own[0] = jnp.sum(jnp.where(lane == me, packed[pl.ds(ROWS + 1, 1), :], 0.0))


def finish(packed):
    vmem = pl.BlockSpec(memory_space=pltpu.VMEM)
    shapes = [(EMB, 2 * C), (1, C), (C, HID), (HID, C), (512, 256), (256, 512), (1,)]
    return pl.pallas_call(
        finish_kernel,
        out_shape=[jax.ShapeDtypeStruct(s, F32) for s in shapes],
        in_specs=[vmem],
        out_specs=[vmem] * 6 + [pl.BlockSpec(memory_space=pltpu.SMEM)],
        compiler_params=pltpu.CompilerParams(vmem_limit_bytes=32 * 1024 * 1024),
    )(packed)


def body(sizes, clip_tiles, clip_size, clip_dest, timesteps, noise_seeds, w_time, gain, w_in, w_out, w_down, w_up):
    packed, = local_grads(
        clip_tiles, clip_size, clip_dest, timesteps, noise_seeds,
        w_time, gain, w_in, w_out, w_down, w_up,
    )
    packed = all_reduce(packed, sizes)
    gt, ggain, gin, gout, gdown, gup, own = finish(packed)
    return (gt, ggain.reshape(C), gin, gout, gdown, gup, own)


def solution(mesh):
    rows = P(("dp", "rep"), None)
    in_specs = (P(("dp", "rep"), None, None), rows, rows, rows, rows) + (P(),) * 6
    out_specs = (P(),) * 6 + (P(("dp", "rep")),)
    sizes = (4, mesh.shape["dp"] // 8, mesh.shape["rep"])
    return jax.shard_map(functools.partial(body, sizes), mesh=mesh, in_specs=in_specs, out_specs=out_specs, check_vma=False)
```

```python
import functools
import math

import jax
import jax.numpy as jnp
import numpy as np
from jax import lax
from jax.experimental import pallas as pl
from jax.experimental.pallas import tpu as pltpu
from jax.sharding import PartitionSpec as P

EMB = 256
TR = 8
TC = 32
TSTEPS = 1000
C = 128
PIX = 256
HID = 256
SPAN = 8
RUN = 4
CLIPS = 64
MUL_POS = 1103515245
MUL_SEED = 747796405
ADD_POS = 1013904223
MUL_MIX = 73244475
ROOT3 = 1.7320508
NOISE_A = float(np.float32(2.0 * ROOT3 / 16777216.0))
NOISE_B = float(np.float32(ROOT3 * (1.0 / 16777216.0 - 1.0)))
CHUNK, SKEW = 2, 1
F32 = jnp.float32
BF16 = jnp.bfloat16
ROW_TIME, ROW_IN, ROW_OUT, ROW_DOWN, ROW_UP, ROWS = 0, 512, 768, 1024, 2048, 3072
PARTS = 3
HALF = ROWS // 2
PART = HALF // PARTS


def wrap32(value):
    value &= 0xFFFFFFFF
    return value - (1 << 32) if value >= (1 << 31) else value


def dot(a, b):
    return lax.dot_general(a, b, (((1,), (0,)), ((), ())), preferred_element_type=F32)


def dot_bt(a, b):
    return lax.dot_general(a, b, (((1,), (1,)), ((), ())), preferred_element_type=F32)


def dot_at(a, b):
    return lax.dot_general(a, b, (((0,), (0,)), ((), ())), preferred_element_type=F32)


def shift_right(value, amount):
    return lax.shift_right_logical(value, jnp.int32(amount))


def group_sum(x, lane):
    pair = x + jnp.where(lane % 2 == 0, pltpu.roll(x, 127, 1), pltpu.roll(x, 1, 1))
    return pair + jnp.where(lane % 4 < 2, pltpu.roll(pair, 126, 1), pltpu.roll(pair, 2, 1))


def add_blocks(pack_ref, start, value):
    height = value.shape[0]
    for j in range(value.shape[1] // C):
        pack_ref[pl.ds(start + j * height, height), :] += value[:, j * C:(j + 1) * C]


def span_kernel(
    tiles_hbm, sizes_hbm, seeds_hbm, dest_hbm, time_hbm, freq_hbm, wt_hbm, gain_hbm,
    win_hbm, wout_hbm, wdown_hbm, wup_hbm,
    pack_ref,
    sizes_ref, seeds_ref, sizes_row, dest_row, time_row, freq_ref, wt_ref, gain_ref,
    win_ref, wout_ref, wdown_ref, wup_ref, input_sem,
    buf, sem, itab, perm, emb_s, film_scale, film_shift, sa_s, sb_s, weight_s, inv_s,
    noise, noisy, x_s, hid, slope, resid, patch,
    dact, dslope, glift, gpd_s, gres, gph_s, s1_s, s2_s, loss_s, stat,
    win_h, wout_h, wdown_h, wup_h,
):
    inputs = [
        pltpu.make_async_copy(source, target, input_sem.at[index])
        for index, (source, target) in enumerate((
            (sizes_hbm, sizes_ref), (seeds_hbm, seeds_ref), (sizes_hbm, sizes_row),
            (time_hbm, time_row), (freq_hbm, freq_ref), (wt_hbm, wt_ref), (gain_hbm, gain_ref),
            (win_hbm, win_ref), (wout_hbm, wout_ref), (wdown_hbm, wdown_ref),
            (wup_hbm, wup_ref), (dest_hbm, dest_row),
        ))
    ]
    for copy in inputs:
        copy.start()
    inputs[0].wait()
    total = sizes_ref[0, 0]
    for entry in range(1, CLIPS):
        total += sizes_ref[0, entry]
    count = total // SPAN

    def fetch(span, slot):
        return pltpu.make_async_copy(
            tiles_hbm.at[pl.ds(span * SPAN, SPAN)], buf.at[slot], sem.at[slot]
        )

    @pl.when(count > 0)
    def _():
        fetch(0, 0).start()

    row = lax.broadcasted_iota(jnp.int32, (PIX, C), 0)
    lane = lax.broadcasted_iota(jnp.int32, (PIX, C), 1)
    quad, rest = row // 64, row % 64
    pixel = (2 * (rest // 16) + quad // 2) * TC + 2 * (rest % 16) + quad % 2
    itab[...] = (pixel * C + lane) * jnp.int32(MUL_POS)
    prow = lax.broadcasted_iota(jnp.int32, (PIX, PIX), 0)
    pcol = lax.broadcasted_iota(jnp.int32, (PIX, PIX), 1)
    pquad, prest = prow // 64, prow % 64
    ppix = (2 * (prest // 16) + pquad // 2) * TC + 2 * (prest % 16) + pquad % 2
    perm[...] = jnp.where(ppix == pcol, 1.0, 0.0).astype(BF16)
    for ref in (pack_ref, s1_s, s2_s, loss_s):
        ref[...] = jnp.zeros_like(ref)
    lane8 = lax.broadcasted_iota(jnp.int32, (SPAN, C), 1)
    for copy in inputs[1:]:
        copy.wait()
    eye = lax.broadcasted_iota(jnp.int32, (CLIPS, CLIPS), 0) == lax.broadcasted_iota(
        jnp.int32, (CLIPS, CLIPS), 1
    )

    def column(values):
        picked = jnp.sum(jnp.where(eye, values, 0.0), axis=1, keepdims=True)
        return jnp.broadcast_to(picked, (CLIPS, C))

    step = time_row[...].astype(F32)
    alpha_bar = jnp.cos(((step + 1.0) / TSTEPS + 0.008) / 1.008 * (math.pi / 2.0)) ** 2
    sa_s[...] = column(jnp.sqrt(alpha_bar))
    sb_s[...] = column(jnp.sqrt(1.0 - alpha_bar))
    inv_len = 1.0 / column(jnp.maximum(sizes_row[...], 1).astype(F32))
    inv_s[...] = inv_len * (1.0 / (PIX * 4))
    weight_s[...] = inv_len * (2.0 / (PIX * C))
    angle = column(step) * freq_ref[...]
    emb_s[:, :C] = jnp.cos(angle).astype(BF16)
    emb_s[:, C:] = jnp.sin(angle).astype(BF16)
    modulation = dot(emb_s[...], wt_ref[...])
    film_scale[...] = modulation[:, :C]
    film_shift[...] = modulation[:, C:]
    win_h[...] = win_ref[...] * jnp.asarray(0.5, BF16)
    wdown_h[...] = wdown_ref[...] * jnp.asarray(0.5, BF16)
    wout_h[...] = wout_ref[...] * jnp.asarray(0.5, BF16)
    wup_h[...] = wup_ref[...] * jnp.asarray(0.5, BF16)

    def marks(span):
        one = sizes_ref[0, span * RUN]
        two = one + sizes_ref[0, span * RUN + 1]
        return one, two, two + sizes_ref[0, span * RUN + 2]

    def owner_of(tile, bounds):
        return sum((tile >= bound).astype(jnp.int32) for bound in bounds)

    def make_noisy(span, slot):
        bounds = marks(span)
        owners = [owner_of(jnp.int32(k), bounds) for k in range(SPAN)]
        for k in range(SPAN):
            if k % 2 == 0:
                pair = dot(
                    perm[...], jnp.concatenate([buf[slot, k], buf[slot, k + 1]], axis=1)
                )
            entry = span * RUN + owners[k]
            row = pl.ds(entry, 1)
            start = jnp.int32(0)
            for bound in bounds:
                start = jnp.where(k >= bound, bound, start)
            mix = (
                (k - start) * jnp.int32(wrap32(PIX * C * MUL_POS))
                + seeds_ref[0, entry] * jnp.int32(MUL_SEED) + jnp.int32(ADD_POS)
            )
            stat[4, pl.ds(k, 1), :] = inv_s[row, :]
            stat[5, pl.ds(k, 1), :] = film_scale[row, :]
            stat[6, pl.ds(k, 1), :] = film_shift[row, :]
            mixed = itab[...] + mix
            mixed = mixed ^ shift_right(mixed, 16)
            mixed = mixed * jnp.int32(MUL_MIX)
            mixed = mixed ^ shift_right(mixed, 16)
            mixed = mixed * jnp.int32(MUL_MIX)
            mixed = mixed ^ shift_right(mixed, 16)
            field = shift_right(mixed, 8).astype(F32) * NOISE_A + NOISE_B
            noise[k] = field
            pixels = pair[:, (k % 2) * C:(k % 2 + 1) * C]
            value = sa_s[row, :] * pixels + sb_s[row, :] * field
            noisy[k] = value
            stat[0, pl.ds(k, 1), :] = jnp.sum(value, axis=0, keepdims=True)
            stat[1, pl.ds(k, 1), :] = jnp.sum(value * value, axis=0, keepdims=True)

        tile8 = lax.broadcasted_iota(jnp.int32, (SPAN, C), 0)
        seg = owner_of(tile8, bounds)
        inv_count = stat[4]
        first = jnp.zeros((SPAN, C), F32)
        square = jnp.zeros((SPAN, C), F32)
        for k in range(SPAN):
            member = seg == owners[k]
            first += jnp.where(member, stat[0, pl.ds(k, 1), :], 0.0)
            square += jnp.where(member, stat[1, pl.ds(k, 1), :], 0.0)
        mean = group_sum(first, lane8) * inv_count
        var = group_sum(square, lane8) * inv_count - mean * mean
        spread = lax.rsqrt(var + 1e-05)
        factor = spread * gain_ref[...] * (1.0 + stat[5])
        shift = stat[6]
        stat[0] = mean
        stat[1] = factor
        stat[2] = shift
        stat[3] = spread

    @pl.when(count > 0)
    def _():
        @pl.when(count > 1)
        def _():
            fetch(1, 1).start()

        fetch(0, 0).wait()
        make_noisy(0, 0)

    @pl.loop(0, count)
    def _(span):
        bounds = marks(span)
        entries = [span * RUN + owner_of(jnp.int32(k), bounds) for k in range(SPAN)]
        following = jnp.minimum(span + 1, count - 1)
        slot = lax.rem(span + 1, 2)

        @pl.when(span + 1 < count)
        def _():
            fetch(span + 1, slot).wait()

        @pl.when(span + 2 < count)
        def _():
            fetch(span + 2, 1 - slot).start()

        def chunk_steps(k0):
            tiles = range(k0, k0 + CHUNK)
            rows = pl.ds(k0 * PIX, CHUNK * PIX)
            quads = pl.ds(k0 * 64, CHUNK * 64)
            held = {}

            def normalise():
                for k in tiles:
                    one = pl.ds(k, 1)
                    centre = noisy[k] - stat[0, one, :]
                    x_s[pl.ds(k * PIX, PIX), :] = (
                        centre * stat[1, one, :] + stat[2, one, :]
                    ).astype(BF16)

            def project():
                held["half"] = dot(x_s[rows, :], win_h[...])

            def activate():
                half = held["half"]
                th = jnp.tanh(half)
                q = 1.0 + th
                h = half * q
                slope[rows, :] = q + h * (1.0 - th)
                hid[rows, :] = h.astype(BF16)

            def project_back():
                held["out"] = dot(hid[rows, :], wout_ref[...])

            def residual():
                for k in tiles:
                    at = (k - k0) * PIX
                    out = held["out"][at:at + PIX] + noisy[k]
                    resid[k] = out
                    outb = out.astype(BF16)
                    for j in range(4):
                        patch[pl.ds(k * 64, 64), pl.ds(j * C, C)] = outb[j * 64:(j + 1) * 64]

            def down():
                held["half"] = dot(patch[quads, :], wdown_h[...])

            def down_activate():
                half = held["half"]
                th = jnp.tanh(half)
                q = 1.0 + th
                h = half * q
                dslope[quads, :] = q + h * (1.0 - th)
                dact[quads, :] = h.astype(BF16)

            def up():
                held["lifted"] = dot(dact[quads, :], wup_ref[...])

            def error():
                for k in tiles:
                    at = (k - k0) * 64
                    row = pl.ds(entries[k], 1)
                    weight = weight_s[row, :]
                    total = jnp.zeros((64, C), F32)
                    for j in range(4):
                        part = pl.ds(j * 64, 64)
                        err = (
                            resid[k, part, :]
                            + held["lifted"][at:at + 64, j * C:(j + 1) * C]
                            - noise[k, part, :]
                        )
                        total += err * err
                        gp = err * weight
                        resid[k, part, :] = gp
                        glift[pl.ds(k * 64, 64), pl.ds(j * C, C)] = gp.astype(BF16)
                    loss_s[row, :] += jnp.sum(total, axis=0, keepdims=True)

            def up_back():
                held["gda"] = dot_bt(glift[quads, :], wup_h[...])

            def down_slope():
                gpd_s[quads, :] = (held["gda"] * dslope[quads, :]).astype(BF16)

            def down_back():
                held["back"] = dot_bt(gpd_s[quads, :], wdown_ref[...])

            def grad_residual():
                for k in tiles:
                    at = (k - k0) * 64
                    for j in range(4):
                        part = pl.ds(j * 64, 64)
                        gres[pl.ds(k * PIX + j * 64, 64), :] = (
                            resid[k, part, :] + held["back"][at:at + 64, j * C:(j + 1) * C]
                        ).astype(BF16)

            def out_back():
                held["gh"] = dot_bt(gres[rows, :], wout_h[...])

            def hidden_slope():
                gph_s[rows, :] = (held["gh"] * slope[rows, :]).astype(BF16)

            def in_back():
                held["gn"] = dot_bt(gph_s[rows, :], win_ref[...])

            def tile_sums():
                for k in tiles:
                    at = (k - k0) * PIX
                    one = pl.ds(k, 1)
                    centre = noisy[k] - stat[0, one, :]
                    mine = held["gn"][at:at + PIX]
                    row = pl.ds(entries[k], 1)
                    s1_s[row, :] += jnp.sum(mine, axis=0, keepdims=True)
                    s2_s[row, :] += (
                        jnp.sum(mine * centre, axis=0, keepdims=True) * stat[3, one, :]
                    )

            return [
                normalise, project, activate, project_back, residual, down, down_activate, up,
                error, up_back, down_slope, down_back, grad_residual, out_back, hidden_slope,
                in_back, tile_sums,
            ]

        chunks = [chunk_steps(k0) for k0 in range(0, SPAN, CHUNK)]
        for turn in range(len(chunks[0]) + SKEW * (len(chunks) - 1)):
            for index, steps in enumerate(chunks):
                if 0 <= turn - SKEW * index < len(steps):
                    steps[turn - SKEW * index]()

        make_noisy(following, slot)
        add_blocks(pack_ref, ROW_UP, dot_at(dact[...], glift[...]))
        add_blocks(pack_ref, ROW_DOWN, dot_at(gpd_s[...], patch[...]))
        add_blocks(
            pack_ref, ROW_OUT, dot_at(gres[...], hid[...])
        )
        add_blocks(
            pack_ref, ROW_IN, dot_at(x_s[...], gph_s[...])
        )

    scale1 = 1.0 + film_scale[...]
    s2 = s2_s[...]
    pack_ref[pl.ds(ROWS, 1), :] = jnp.sum(s2 * scale1, axis=0, keepdims=True)
    clip_loss = jnp.sum(loss_s[...], axis=1, keepdims=True) * weight_s[...] * 0.5
    place = column((dest_row[...] * lax.axis_size("rep") + lax.axis_index("rep")).astype(F32))
    hits = place == lax.broadcasted_iota(jnp.int32, (CLIPS, C), 1).astype(F32)
    pack_ref[pl.ds(ROWS + 1, 1), :] = jnp.sum(jnp.where(hits, clip_loss, 0.0), axis=0, keepdims=True)
    emb = emb_s[...].astype(F32)
    for ref, part in ((s2 * gain_ref[...], 0), (s1_s[...], 1)):
        pack_ref[pl.ds(ROW_TIME + part * EMB, EMB), :] = lax.dot_general(
            emb, ref, (((0,), (0,)), ((), ())),
            precision=lax.Precision.HIGHEST, preferred_element_type=F32,
        )


def local_grads(clip_tiles, sizes, dests, times, seeds, w_time, gain, w_in, w_out, w_down, w_up):
    vmem = pl.BlockSpec(memory_space=pltpu.VMEM)
    half = EMB // 2
    freq = np.exp(-math.log(10000.0) * np.arange(half) / half).astype(np.float32)
    return pl.pallas_call(
        span_kernel,
        out_shape=[jax.ShapeDtypeStruct(s, F32) for s in [(ROWS + 8, C)]],
        in_specs=[pl.BlockSpec(memory_space=pl.ANY)] * 12,
        out_specs=[vmem],
        scratch_shapes=[
            pltpu.SMEM((1, CLIPS), jnp.int32),
            pltpu.SMEM((1, CLIPS), jnp.int32),
            pltpu.VMEM((1, CLIPS), jnp.int32),
            pltpu.VMEM((1, CLIPS), jnp.int32),
            pltpu.VMEM((1, CLIPS), jnp.int32),
            pltpu.VMEM((1, C), F32),
            pltpu.VMEM((EMB, 2 * C), BF16),
            pltpu.VMEM((1, C), F32),
            pltpu.VMEM((C, HID), BF16),
            pltpu.VMEM((HID, C), BF16),
            pltpu.VMEM((512, 256), BF16),
            pltpu.VMEM((256, 512), BF16),
            pltpu.SemaphoreType.DMA((12,)),
            pltpu.VMEM((2, SPAN, PIX, C), BF16),
            pltpu.SemaphoreType.DMA((2,)),
            pltpu.VMEM((PIX, C), jnp.int32),
            pltpu.VMEM((PIX, PIX), BF16),
            pltpu.VMEM((CLIPS, EMB), BF16),
            pltpu.VMEM((CLIPS, C), F32),
            pltpu.VMEM((CLIPS, C), F32),
            pltpu.VMEM((CLIPS, C), F32),
            pltpu.VMEM((CLIPS, C), F32),
            pltpu.VMEM((CLIPS, C), F32),
            pltpu.VMEM((CLIPS, C), F32),
            pltpu.VMEM((SPAN, PIX, C), F32),
            pltpu.VMEM((SPAN, PIX, C), F32),
            pltpu.VMEM((SPAN * PIX, C), BF16),
            pltpu.VMEM((SPAN * PIX, HID), BF16),
            pltpu.VMEM((SPAN * PIX, HID), F32),
            pltpu.VMEM((SPAN, PIX, C), F32),
            pltpu.VMEM((512, 512), BF16),
            pltpu.VMEM((512, 256), BF16),
            pltpu.VMEM((512, 256), F32),
            pltpu.VMEM((512, 512), BF16),
            pltpu.VMEM((512, 256), BF16),
            pltpu.VMEM((SPAN * PIX, C), BF16),
            pltpu.VMEM((SPAN * PIX, HID), BF16),
            pltpu.VMEM((CLIPS, C), F32),
            pltpu.VMEM((CLIPS, C), F32),
            pltpu.VMEM((CLIPS, C), F32),
            pltpu.VMEM((7, SPAN, C), F32),
            pltpu.VMEM((C, HID), BF16),
            pltpu.VMEM((HID, C), BF16),
            pltpu.VMEM((512, 256), BF16),
            pltpu.VMEM((256, 512), BF16),
        ],
        compiler_params=pltpu.CompilerParams(vmem_limit_bytes=56 * 1024 * 1024),
    )(clip_tiles, sizes, seeds, dests, times, freq.reshape(1, half), w_time,
      gain.reshape(1, C), w_in, w_out, w_down, w_up)


def reduce_kernel(
    sizes, x_hbm, res,
    acc, other, r1, r2, r3, m_own, m_core, m_axes, local_sem, send_sem, recv_sem,
):
    dp, z = lax.axis_index("dp"), lax.axis_index("rep")
    ny = sizes[1]
    core = lax.rem(dp, 2)
    chip = lax.div(dp, 2)
    coord = (lax.div(chip, ny), lax.rem(chip, ny), z)

    def device(x, y, zz, c):
        return ((x * ny + y) * 2 + c, zz)

    def peer(axis, r):
        other_coord = lax.rem(coord[axis] + r, sizes[axis])
        place = list(coord)
        place[axis] = other_coord
        return other_coord, device(*place, core)

    sibling = device(*coord, 1 - core)
    peers = [(axis, r) for axis in range(3) for r in range(1, sizes[axis])]
    barrier = pltpu.get_barrier_semaphore()
    for target in [sibling] + [peer(axis, r)[1] for axis, r in peers]:
        pl.semaphore_signal(barrier, inc=1, device_id=target, device_id_type=pl.DeviceIdType.MESH)

    mine = core * HALF
    theirs = (1 - core) * HALF
    local = []
    for p in range(PARTS):
        copy = pltpu.make_async_copy(
            x_hbm.at[pl.ds(pl.multiple_of(mine + p * PART, 8), PART)],
            acc.at[pl.ds(p * PART, PART)], local_sem.at[p],
        )
        copy.start()
        local.append(copy)
    misc_rows = pl.ds(ROWS, 8)
    m_local = pltpu.make_async_copy(x_hbm.at[misc_rows], m_own, local_sem.at[PARTS])
    m_local.start()
    pl.semaphore_wait(barrier, 1 + len(peers))

    started = []

    def send(src, dst, target):
        index = len(started)
        copy = pltpu.make_async_remote_copy(
            src_ref=src, dst_ref=dst, send_sem=send_sem.at[index], recv_sem=recv_sem.at[index],
            device_id=target, device_id_type=pl.DeviceIdType.MESH,
        )
        copy.start()
        started.append(copy)
        return copy

    m_core_copy = send(x_hbm.at[misc_rows], m_core, sibling)
    order = [[(p + s) % 3 for s in range(3)] for p in range(PARTS)]
    lengths = []
    for p in range(PARTS):
        length, row = PART, []
        for s in range(3):
            length //= sizes[order[p][s]]
            row.append(length)
        lengths.append(row)
    landing = (r1, r2)
    base = [jnp.int32(p * PART) for p in range(PARTS)]
    starts = [[None] * 3 for _ in range(PARTS)]

    def turns(axis):
        return sorted(range(1, sizes[axis]), key=lambda r: -min(r, sizes[axis] - r))

    def piece(p, r):
        axis, length = order[p][0], lengths[p][0]
        return p * PART + lax.rem(coord[axis] + r, sizes[axis]) * length, length

    arrivals = []
    for turn in range(max(sizes)):
        for p in range(PARTS):
            steps = turns(order[p][0]) + [0]
            if turn < len(steps):
                start, length = piece(p, steps[turn])
                copy = send(
                    x_hbm.at[pl.ds(pl.multiple_of(theirs + start, 8), length)],
                    other.at[pl.ds(pl.multiple_of(start, 8), length)], sibling,
                )
                arrivals.append((p, steps[turn], copy))

    def scatter(p, s):
        axis, length = order[p][s], lengths[p][s]
        copies = []
        for r in turns(axis):
            q, target = peer(axis, r)
            rows = pl.ds(pl.multiple_of(base[p] + q * length, 8), length)
            copies.append(send(acc.at[rows], landing[s].at[p, r - 1], target))
        base[p] = base[p] + coord[axis] * length
        starts[p][s] = base[p]
        return copies

    flying = [[] for _ in range(PARTS)]
    for copy in local:
        copy.wait()
    for p, r, copy in arrivals:
        copy.wait_recv()
        start, length = piece(p, r)
        rows = pl.ds(pl.multiple_of(start, 8), length)
        acc[rows, :] = acc[rows, :] + other[rows, :]
        if r:
            flying[p].append(send(acc.at[rows], r1.at[p, r - 1], peer(order[p][0], r)[1]))
    for p in range(PARTS):
        base[p] = base[p] + coord[order[p][0]] * lengths[p][0]
        starts[p][0] = base[p]
    m_local.wait()
    m_core_copy.wait_recv()

    def exchange(slots, axis, value):
        slots[coord[axis]] = value
        return [
            send(slots.at[coord[axis]], slots.at[coord[axis]], peer(axis, r)[1])
            for r in range(1, sizes[axis])
        ]

    def total_of(slots, axis, copies):
        for copy in copies:
            copy.wait_recv()
        total = slots[0]
        for i in range(1, sizes[axis]):
            total = total + slots[i]
        return total

    misc_copies = exchange(m_axes.at[0], 0, m_own[...] + m_core[...])
    for s in range(2):
        for p in range(PARTS):
            for copy in flying[p]:
                copy.wait_recv()
            rows = pl.ds(pl.multiple_of(base[p], 8), lengths[p][s])
            total = acc[rows, :]
            for r in range(sizes[order[p][s]] - 1):
                total = total + landing[s][p, r]
            if s == 0:
                acc[rows, :] = total
                flying[p] = scatter(p, 1)
            else:
                flying[p] = exchange(r3.at[p, :, pl.ds(0, lengths[p][1])], order[p][2], total)
        misc_copies = exchange(
            m_axes.at[s + 1], s + 1, total_of(m_axes.at[s], s, misc_copies)
        )
    for p in range(PARTS):
        total = total_of(r3.at[p, :, pl.ds(0, lengths[p][1])], order[p][2], flying[p])
        res[pl.ds(pl.multiple_of(mine + base[p], 8), lengths[p][1]), :] = total
        flying[p] = gather(p, 1, sizes, order, lengths, starts, mine, peer, send, res)
    res[misc_rows, :] = total_of(m_axes.at[2], 2, misc_copies)
    last = []

    def forward(p, q):
        rows = pl.ds(pl.multiple_of(mine + p * PART + q * lengths[p][0], 8), lengths[p][0])
        last.append(send(res.at[rows], res.at[rows], sibling))

    for p in range(PARTS):
        for copy in flying[p]:
            copy.wait_recv()
        flying[p] = gather(p, 0, sizes, order, lengths, starts, mine, peer, send, res)
        forward(p, coord[order[p][0]])
    longest = max(sizes)
    for r in [i for i in range(1, longest) if i != 2] + [2]:
        for p in range(PARTS):
            axis = order[p][0]
            if r < sizes[axis]:
                flying[p][r - 1].wait_recv()
                forward(p, lax.rem(coord[axis] + sizes[axis] - r, sizes[axis]))
    for copy in last:
        copy.wait_recv()
    for copy in started:
        copy.wait_send()


def gather(p, s, sizes, order, lengths, starts, mine, peer, send, res):
    axis = order[p][s]
    rows = pl.ds(pl.multiple_of(mine + starts[p][s], 8), lengths[p][s])
    far_first = sorted(range(1, sizes[axis]), key=lambda r: -min(r, sizes[axis] - r))
    copies = {r: send(res.at[rows], res.at[rows], peer(axis, r)[1]) for r in far_first}
    return [copies[r] for r in range(1, sizes[axis])]


def all_reduce(packed, sizes):
    vmem = pl.BlockSpec(memory_space=pltpu.VMEM)
    most = max(sizes) - 1
    per_axis = sum(n - 1 for n in sizes)
    copies = 1 + per_axis * 6 + 2 * sum(sizes)
    shapes = []
    for s in range(2):
        longest = 0
        for p in range(PARTS):
            length = PART
            for i in range(s + 1):
                length //= sizes[(p + i) % 3]
            longest = max(longest, length)
        shapes.append(longest)
    return pl.pallas_call(
        functools.partial(reduce_kernel, sizes),
        out_shape=jax.ShapeDtypeStruct((ROWS + 8, C), F32),
        in_specs=[pl.BlockSpec(memory_space=pl.ANY)],
        out_specs=vmem,
        scratch_shapes=[
            pltpu.VMEM((HALF, C), F32),
            pltpu.VMEM((HALF, C), F32),
            pltpu.VMEM((PARTS, most, shapes[0], C), F32),
            pltpu.VMEM((PARTS, most, shapes[1], C), F32),
            pltpu.VMEM((PARTS, max(sizes), shapes[1], C), F32),
            pltpu.VMEM((8, C), F32),
            pltpu.VMEM((8, C), F32),
            pltpu.VMEM((3, max(sizes), 8, C), F32),
            pltpu.SemaphoreType.DMA((PARTS + 1,)),
            pltpu.SemaphoreType.DMA((copies,)),
            pltpu.SemaphoreType.DMA((copies,)),
        ],
        compiler_params=pltpu.CompilerParams(
            collective_id=0, has_side_effects=True, vmem_limit_bytes=16 * 1024 * 1024
        ),
    )(packed)


def finish_kernel(packed, gt, gain, gin, gout, gdown, gup, own):
    def block(start, height, j):
        return packed[pl.ds(start + j * height, height), :]

    for j in range(2):
        cols = pl.ds(j * C, C)
        gt[:, cols] = block(ROW_TIME, EMB, j)
        gin[:, cols] = block(ROW_IN, C, j)
        gout[cols, :] = block(ROW_OUT, C, j).T
    for j in range(4):
        cols = pl.ds(j * C, C)
        gdown[cols, :] = block(ROW_DOWN, 256, j).T
        gup[:, cols] = block(ROW_UP, 256, j)
    gain[...] = packed[pl.ds(ROWS, 1), :]
    me = lax.axis_index("dp") * lax.axis_size("rep") + lax.axis_index("rep")
    lane = lax.broadcasted_iota(jnp.int32, (1, C), 1)
    own[0] = jnp.sum(jnp.where(lane == me, packed[pl.ds(ROWS + 1, 1), :], 0.0))


def finish(packed):
    vmem = pl.BlockSpec(memory_space=pltpu.VMEM)
    shapes = [(EMB, 2 * C), (1, C), (C, HID), (HID, C), (512, 256), (256, 512), (1,)]
    return pl.pallas_call(
        finish_kernel,
        out_shape=[jax.ShapeDtypeStruct(s, F32) for s in shapes],
        in_specs=[vmem],
        out_specs=[vmem] * 6 + [pl.BlockSpec(memory_space=pltpu.SMEM)],
        compiler_params=pltpu.CompilerParams(vmem_limit_bytes=32 * 1024 * 1024),
    )(packed)


def body(sizes, clip_tiles, clip_size, clip_dest, timesteps, noise_seeds, w_time, gain, w_in, w_out, w_down, w_up):
    packed, = local_grads(
        clip_tiles, clip_size, clip_dest, timesteps, noise_seeds,
        w_time, gain, w_in, w_out, w_down, w_up,
    )
    packed = all_reduce(packed, sizes)
    gt, ggain, gin, gout, gdown, gup, own = finish(packed)
    return (gt, ggain.reshape(C), gin, gout, gdown, gup, own)


def solution(mesh):
    rows = P(("dp", "rep"), None)
    in_specs = (P(("dp", "rep"), None, None), rows, rows, rows, rows) + (P(),) * 6
    out_specs = (P(),) * 6 + (P(("dp", "rep")),)
    sizes = (4, mesh.shape["dp"] // 8, mesh.shape["rep"])
    return jax.shard_map(functools.partial(body, sizes), mesh=mesh, in_specs=in_specs, out_specs=out_specs, check_vma=False)
```
